128 devices in a mesh: lev: 4 (over z), box: 32 (over x, y, core).
Axes of the slice: x: 4, y: 4, z: 4, core: 2. Of those that a mesh axis runs over, the one named last changes fastest.
Arguments:
- box_states: float32 [512, 8, 32, 1024], P(('lev', 'box')), may hold values from -6 to 6
- cell_code: int32 [512, 32, 1024], P(('lev', 'box')), may hold values from 0 to 15
- diffusivity: float32 [8], replicated, may hold values from 0.02 to 0.1
- reaction: float32 [8, 8], replicated, may hold values from -2 to 2
- coarse_child: int32 [128], P('box'), may hold values from -1 to 59, as said below
- coarse_octant: int32 [128], P('box'), may hold values from 0 to 3, as said below
- fine_parent: int32 [512], P(('lev', 'box')), may hold values from -1 to 127, as said below
- fine_octant: int32 [512], P(('lev', 'box')), may hold values from 0 to 3, as said below
- fine_count: int32 [128], P(('lev', 'box')), may hold values from 0 to 4, as said below
Outputs:
- new_states: float32 [512, 8, 32, 1024], P(('lev', 'box'))
The draws below stay inside these ranges and needn't reach their ends.
Inputs may be any that keep to these rules, and one draw needn't show every extreme that they name: `coarse_child`: -1 where the coarse box has no fine box; else ((r - 1) (5) + e + 2) * 4 + s: the fine box is slot s of the device with lev index r >= 1 whose box index is the parent device's box index plus e, |e| <= 2. Each coarse box has at most one fine box. `coarse_octant`: for a refined coarse box, the refined halves; equal to fine_octant of its fine box. `fine_parent`: the parent of each used fine slot, -1 for unused slots and on lev index 0; used slots are those below fine_count, and coarse_child points back to them. `fine_octant`: the halves covered by a used fine slot, 0 for unused slots. `fine_count`: 0 on lev index 0; at most 4, reached on some device in every draw.
All inputs are finite; a program needn't handle non-finite values.
Results may differ from the reference program's by a relative error of at most 0.0003.
Values sent between devices are 32-bit elements; how exact they have to be, the bound alone decides.
No kernel may reach another device: no remote copies, remote signals or barrier semaphores. Data moves between devices by JAX's collectives and lax.ppermute only.
A program may use at most 192 MiB of HBM per device.

```python
import math
import jax
import jax.numpy as jnp
from jax import lax

SPECIES = 8
BOX = 32
SLOTS = 4
REACH = 2
ALL_BOXES = 512
N_LEV = 4
N_BOX = 32


def refinement_plan(key):
    coarse_total = N_BOX * SLOTS
    key_list = jax.random.split(key, 6)
    box_ids = jnp.arange(coarse_total, dtype=jnp.int32)
    home_column = box_ids // SLOTS
    chosen_column = jax.random.randint(key_list[0], (), 0, N_BOX - 1 - REACH)
    forced = home_column == chosen_column
    closing = box_ids == coarse_total - 1
    refined = (jax.random.randint(key_list[2], (coarse_total,), 0, 4) > 0) | forced | closing
    random_row = jax.random.randint(key_list[3], (coarse_total,), 1, N_LEV)
    home_row = jnp.where(forced, N_LEV - 1, jnp.where(closing, 1, random_row))
    shifted = home_column + jax.random.randint(key_list[4], (coarse_total,), -REACH, REACH + 1)
    column = jnp.where(forced, home_column + REACH, jnp.where(closing, home_column, jnp.clip(shifted, 0, N_BOX - 1)))
    octant = jax.random.randint(key_list[5], (coarse_total,), 0, 4)
    target = home_row * N_BOX + column
    priority = jnp.where(forced, 0, jnp.where(closing, coarse_total, 2 * coarse_total)) + box_ids
    earlier = (target[:, None] == target[None, :]) & refined[None, :] & (priority[None, :] < priority[:, None])
    slot_rank = jnp.sum(earlier.astype(jnp.int32), axis=1)
    accepted = refined & (slot_rank < SLOTS)
    return (box_ids, accepted, home_row, column, octant, slot_rank, target)


def parent_table(key):
    box_ids, accepted, home_row, column, octant, slot_rank, target = refinement_plan(key)
    slot_ids = jnp.arange(N_LEV * N_BOX * SLOTS, dtype=jnp.int32)
    device_ids = slot_ids // SLOTS
    places = slot_ids % SLOTS
    matched = (device_ids[:, None] == target[None, :]) & (places[:, None] == slot_rank[None, :]) & accepted[None, :]
    parent = jnp.max(jnp.where(matched, box_ids[None, :], -1), axis=1)
    return (parent, octant)


def draw_coarse_child(key, part):
    box_ids, accepted, home_row, column, octant, slot_rank, target = refinement_plan(key)
    offset = column - box_ids // SLOTS
    encoded = ((home_row - 1) * (2 * REACH + 1) + offset + REACH) * SLOTS + slot_rank
    return jnp.where(accepted, encoded, -1).astype(jnp.int32)


def draw_coarse_octant(key, part):
    box_ids, accepted, home_row, column, octant, slot_rank, target = refinement_plan(key)
    return octant.astype(jnp.int32)


def draw_fine_parent(key, part):
    parent, octant = parent_table(key)
    return parent.astype(jnp.int32)


def draw_fine_octant(key, part):
    parent, octant = parent_table(key)
    return jnp.where(parent >= 0, octant[jnp.maximum(parent, 0)], 0).astype(jnp.int32)


def draw_fine_count(key, part):
    box_ids, accepted, home_row, column, octant, slot_rank, target = refinement_plan(key)
    device_ids = jnp.arange(N_LEV * N_BOX, dtype=jnp.int32)
    matched = (device_ids[:, None] == target[None, :]) & accepted[None, :]
    return jnp.sum(matched.astype(jnp.int32), axis=1).astype(jnp.int32)


def touch_ends(array, key, least, top_value):
    index_at = [jax.random.randint(jax.random.fold_in(key, axis), (), 0, length) for axis, length in enumerate(array.shape)]
    widest = array.shape.index(max(array.shape))
    beside = index_at[:widest] + [(index_at[widest] + 1) % array.shape[widest]] + index_at[widest + 1:]
    return array.at[tuple(index_at)].set(least).at[tuple(beside)].set(top_value)


def shard_levels(stream_key, shape, cuts, least, largest):
    factor_of, own = 1.0, jax.random.fold_in(stream_key, 6)
    for position, parts in cuts:
        heights = jnp.exp(jax.random.uniform(jax.random.fold_in(own, position), (parts,), jnp.float32, least / len(cuts), largest / len(cuts)))
        factor_of = factor_of * jnp.repeat(heights, shape[position] // parts).reshape([-1 if axis == position else 1 for axis in range(len(shape))])
    return factor_of


def normal_values(stream_key, shape, scale, limit, shards=(), kind=jnp.bfloat16):
    gain = shard_levels(stream_key, shape, shards, -0.22, 0.18) if shards else 1.0
    values = jax.random.normal(stream_key, shape, jnp.float32) * scale * gain
    return jnp.minimum(jnp.maximum(values, -limit), limit).astype(kind)


def setup_inputs(seed: int = 0) -> dict:
    keys = jax.random.split(jax.random.key(seed), 10)
    box_states = normal_values(keys[0], (ALL_BOXES, SPECIES, BOX, BOX * BOX), 1.0, 6.0, ((0, 128),), jnp.float32)
    cell_code = touch_ends(jax.random.randint(keys[1], (ALL_BOXES, BOX, BOX * BOX), 0, 16), jax.random.fold_in(keys[1], 1), 0, 15).astype(jnp.int32)
    diffusivity = jnp.clip(jnp.exp(jax.random.uniform(keys[2], (SPECIES,), jnp.float32, math.log(0.02), math.log(0.1))), 0.02, 0.1)
    reaction = normal_values(keys[3], (SPECIES, SPECIES), SPECIES ** -0.5, 2.0, (), jnp.float32)
    coarse_child = draw_coarse_child(jax.random.fold_in(keys[9], 71), 0)
    coarse_octant = draw_coarse_octant(jax.random.fold_in(keys[9], 71), 0)
    fine_parent = draw_fine_parent(jax.random.fold_in(keys[9], 71), 0)
    fine_octant = draw_fine_octant(jax.random.fold_in(keys[9], 71), 0)
    fine_count = draw_fine_count(jax.random.fold_in(keys[9], 71), 0)
    return {"box_states": box_states, "cell_code": cell_code, "diffusivity": diffusivity, "reaction": reaction, "coarse_child": coarse_child, "coarse_octant": coarse_octant, "fine_parent": fine_parent, "fine_octant": fine_octant, "fine_count": fine_count}


ADVECT_SPEED = 0.4
COARSE_STEP = 0.5
KAPPA_FLOOR = 0.5
CODE_LEVELS = 15.0
FINEST_LEVEL = lax.Precision.HIGHEST


def lane_tables(extent, y_half, z_half):
    middle = extent // 2
    lane_ids = jnp.arange(extent * extent, dtype=jnp.int32)
    local_ids = jnp.arange(middle * middle, dtype=jnp.int32)
    across = jnp.arange(middle, dtype=jnp.int32)
    region = (middle * y_half + local_ids // middle) * extent + middle * z_half + local_ids % middle
    y_outer = (middle - y_half) * extent + middle * z_half + across
    z_outer = (middle * y_half + across) * extent + middle - z_half
    y_inner = middle * extent + middle * z_half + across
    z_inner = (middle * y_half + across) * extent + middle - 1

    def selector(target_cells):
        return (lane_ids[None, :] == target_cells[:, None]).astype(jnp.float32)

    return selector(region), selector(y_outer), selector(z_outer), selector(y_inner), selector(z_inner)


def level_tables(extent):
    middle = extent // 2
    lane_ids = jnp.arange(extent * extent, dtype=jnp.int32)
    local_ids = jnp.arange(middle * middle, dtype=jnp.int32)
    parent_lane = (lane_ids // extent // 2) * middle + (lane_ids % extent) // 2
    refine = (local_ids[:, None] == parent_lane[None, :]).astype(jnp.float32)
    return 0.25 * refine.T, refine


def advance(amounts, fraction, ghosts, diffusivity, reaction, spacing, step_size):
    x_low, x_high, y_low, y_high, z_low, z_high = ghosts
    species = amounts.shape[0]
    extent = amounts.shape[1]
    plane_size = amounts.shape[2]
    spread = diffusivity[:, None, None] / spacing
    lower_cell = jnp.concatenate([x_low[:species][:, None], amounts], axis=1)
    upper_cell = jnp.concatenate([amounts, x_high[:species][:, None]], axis=1)
    k_lower = jnp.concatenate([x_low[species][None], fraction], axis=0)
    k_upper = jnp.concatenate([fraction, x_high[species][None]], axis=0)
    flux_x = jnp.minimum(k_lower, k_upper) * (ADVECT_SPEED * lower_cell - spread * (upper_cell - lower_cell))
    change = flux_x[:, :-1] - flux_x[:, 1:]
    lower_cell = jnp.concatenate([y_low[:species], amounts], axis=2)
    upper_cell = jnp.concatenate([amounts, y_high[:species]], axis=2)
    k_lower = jnp.concatenate([y_low[species], fraction], axis=1)
    k_upper = jnp.concatenate([fraction, y_high[species]], axis=1)
    flux_y = jnp.minimum(k_lower, k_upper) * (-spread * (upper_cell - lower_cell))
    change = change + flux_y[:, :, :plane_size] - flux_y[:, :, extent:]
    depth_ids = jnp.arange(plane_size, dtype=jnp.int32) % extent
    top_row = depth_ids == extent - 1
    bottom = depth_ids == 0
    following = jnp.concatenate([amounts[:, :, 1:], jnp.zeros_like(amounts[:, :, :1])], axis=2)
    k_following = jnp.concatenate([fraction[:, 1:], jnp.zeros_like(fraction[:, :1])], axis=1)
    above_cell = jnp.where(top_row, jnp.repeat(z_high[:species], extent, axis=2), following)
    k_above = jnp.where(top_row, jnp.repeat(z_high[species], extent, axis=1), k_following)
    flux_up = jnp.minimum(fraction, k_above) * (-spread * (above_cell - amounts))
    below_cell = jnp.repeat(z_low[:species], extent, axis=2)
    k_below = jnp.repeat(z_low[species], extent, axis=1)
    flux_floor = jnp.minimum(k_below, fraction) * (-spread * (amounts - below_cell))
    previous = jnp.concatenate([jnp.zeros_like(flux_up[:, :, :1]), flux_up[:, :, :-1]], axis=2)
    flux_down = jnp.where(bottom, flux_floor, previous)
    change = change + flux_down - flux_up
    reacted = jnp.einsum("st,txq->sxq", reaction, amounts, precision=FINEST_LEVEL)
    scaling = step_size / (spacing * jnp.maximum(fraction, KAPPA_FLOOR))
    updated = amounts + scaling * change + step_size * reacted
    return updated, flux_x, flux_y, flux_up, flux_floor


def shells_of(slab, octant):
    channels = slab.shape[0]
    extent = 2 * (slab.shape[1] - 2)
    region, y_outer, z_outer, y_inner, z_inner = lane_tables(extent, octant % 2, octant // 2)
    low_face = jnp.dot(slab[:, 0], region.T, precision=FINEST_LEVEL)
    upper_face = jnp.dot(slab[:, -1], region.T, precision=FINEST_LEVEL)
    y_side = jnp.einsum("sxq,tq->sxt", slab[:, 1:-1], y_outer, precision=FINEST_LEVEL).reshape(channels, -1)
    z_side = jnp.einsum("sxq,tq->sxt", slab[:, 1:-1], z_outer, precision=FINEST_LEVEL).reshape(channels, -1)
    return jnp.stack([low_face, upper_face, y_side, z_side])


def coarse_box(amounts, fraction, low_plane, high_plane, octant, diffusivity, reaction):
    species = amounts.shape[0]
    extent = amounts.shape[1]
    quarter = extent // 4
    wall_faces = jnp.zeros((species + 1, extent, extent), jnp.float32)
    updated, flux_x, flux_y, flux_up, flux_floor = advance(
        amounts, fraction, (low_plane, high_plane, wall_faces, wall_faces, wall_faces, wall_faces),
        diffusivity, reaction, 1.0, COARSE_STEP)
    region, y_outer, z_outer, y_inner, z_inner = lane_tables(extent, octant % 2, octant // 2)
    y_sign = 1.0 - 2.0 * (octant % 2).astype(jnp.float32)
    z_sign = 1.0 - 2.0 * (octant // 2).astype(jnp.float32)
    low_face = -jnp.dot(flux_x[:, quarter], region.T, precision=FINEST_LEVEL)
    upper_face = jnp.dot(flux_x[:, 3 * quarter], region.T, precision=FINEST_LEVEL)
    y_side = y_sign * jnp.einsum("sxq,tq->sxt", flux_y[:, quarter:3 * quarter, :extent * extent], y_inner,
                                 precision=FINEST_LEVEL).reshape(species, -1)
    z_side = z_sign * jnp.einsum("sxq,tq->sxt", flux_up[:, quarter:3 * quarter], z_inner,
                                 precision=FINEST_LEVEL).reshape(species, -1)
    return updated, jnp.stack([low_face, upper_face, y_side, z_side])


def fine_ghosts(shells, refine, octant, extent):
    channels = shells.shape[1]
    x_low = jnp.dot(shells[0], refine, precision=FINEST_LEVEL)
    x_high = jnp.dot(shells[1], refine, precision=FINEST_LEVEL)
    y_side = jnp.dot(shells[2], refine, precision=FINEST_LEVEL).reshape(channels, extent, extent)
    z_side = jnp.dot(shells[3], refine, precision=FINEST_LEVEL).reshape(channels, extent, extent)
    blank_face = jnp.zeros_like(y_side)
    y_half = octant % 2
    z_half = octant // 2
    return (x_low, x_high, jnp.where(y_half == 1, y_side, blank_face), jnp.where(y_half == 0, y_side, blank_face),
            jnp.where(z_half == 1, z_side, blank_face), jnp.where(z_half == 0, z_side, blank_face))


def fine_register(flux_values, restrict_to_coarse, octant):
    flux_x, flux_y, flux_up, flux_floor = flux_values
    species = flux_x.shape[0]
    extent = flux_x.shape[1] - 1
    plane_size = flux_x.shape[2]
    y_side = jnp.where(octant % 2 == 0, flux_y[:, :, plane_size:], -flux_y[:, :, :extent]).reshape(species, plane_size)
    z_side = jnp.where(octant // 2 == 0, flux_up[:, :, extent - 1::extent],
                       -flux_floor[:, :, ::extent]).reshape(species, plane_size)
    interface_flux = jnp.stack([-flux_x[:, 0], flux_x[:, extent], y_side, z_side])
    return jnp.einsum("tmd,di->tmi", interface_flux, restrict_to_coarse, precision=FINEST_LEVEL)


def fine_box(amounts, fraction, old_shells, new_shells, octant, diffusivity, reaction):
    species = amounts.shape[0]
    extent = amounts.shape[1]
    middle = extent // 2
    restrict_to_coarse, refine = level_tables(extent)
    between = 0.5 * (old_shells + new_shells)
    first_step = advance(amounts, fraction, fine_ghosts(old_shells, refine, octant, extent),
                         diffusivity, reaction, 0.5, 0.5 * COARSE_STEP)
    second_step = advance(first_step[0], fraction, fine_ghosts(between, refine, octant, extent),
                          diffusivity, reaction, 0.5, 0.5 * COARSE_STEP)
    register = 0.5 * (fine_register(first_step[1:], restrict_to_coarse, octant) + fine_register(second_step[1:], restrict_to_coarse, octant))
    pooled = jnp.einsum("sxq,qr->sxr", second_step[0], restrict_to_coarse, precision=FINEST_LEVEL).reshape(
        species, middle, 2, middle * middle)
    averaged = 0.5 * (pooled[:, :, 0] + pooled[:, :, 1])
    payload = jnp.concatenate([averaged, jnp.transpose(register, (1, 0, 2))], axis=1)
    return second_step[0], payload


def coarse_finish(updated, fraction, payload, register, octant, child_code):
    species = updated.shape[0]
    extent = updated.shape[1]
    quarter = extent // 4
    middle = extent // 2
    region, y_outer, z_outer, y_inner, z_inner = lane_tables(extent, octant % 2, octant // 2)
    outer_fraction = shells_of(fraction[None, quarter - 1:3 * quarter + 1], octant)
    fine_faces = jnp.transpose(payload[:, middle:], (1, 0, 2))
    factor = COARSE_STEP / jnp.maximum(outer_fraction, KAPPA_FLOOR)
    corrections = jnp.where(child_code >= 0, factor * (fine_faces - register), 0.0)
    region_rows = (updated[:, quarter:3 * quarter]
                   + jnp.einsum("sxt,tq->sxq", corrections[2].reshape(species, middle, middle), y_outer,
                                precision=FINEST_LEVEL)
                   + jnp.einsum("sxt,tq->sxq", corrections[3].reshape(species, middle, middle), z_outer,
                                precision=FINEST_LEVEL))
    covered = jnp.sum(region, axis=0) > 0.5
    filled = jnp.einsum("sxr,rq->sxq", payload[:, :middle], region, precision=FINEST_LEVEL)
    region_rows = jnp.where(covered & (child_code >= 0), filled, region_rows)
    result = updated.at[:, quarter - 1].add(jnp.dot(corrections[0], region, precision=FINEST_LEVEL))
    result = result.at[:, 3 * quarter].add(jnp.dot(corrections[1], region, precision=FINEST_LEVEL))
    return result.at[:, quarter:3 * quarter].set(region_rows)


def reference(box_states, cell_code, diffusivity, reaction, coarse_child, coarse_octant, fine_parent, fine_octant,
              fine_count):
    coarse_count = N_BOX * SLOTS
    extent = box_states.shape[2]
    quarter = extent // 4
    offset_count = 2 * REACH + 1
    fractions = cell_code.astype(jnp.float32) / CODE_LEVELS
    coarse = box_states[:coarse_count]
    coarse_fraction = fractions[:coarse_count]
    with_fraction = jnp.concatenate([coarse, coarse_fraction[:, None]], axis=1)
    blank_plane = jnp.zeros_like(with_fraction[:1, :, 0])
    low_planes = jnp.concatenate([blank_plane, with_fraction[:-1, :, extent - 1]], axis=0)
    high_planes = jnp.concatenate([with_fraction[1:, :, 0], blank_plane], axis=0)

    def coarse_entry(entries):
        amounts, fraction, low_plane, high_plane, octant = entries
        return coarse_box(amounts, fraction, low_plane, high_plane, octant, diffusivity, reaction)

    updated, registers = lax.map(coarse_entry, (coarse, coarse_fraction, low_planes, high_planes, coarse_octant))
    later_full = jnp.concatenate([updated, coarse_fraction[:, None]], axis=1)
    old_slabs = with_fraction[:, :, quarter - 1:3 * quarter + 1]
    new_slabs = later_full[:, :, quarter - 1:3 * quarter + 1]

    def fine_entry(box_index):
        parent = jnp.maximum(fine_parent[box_index], 0)
        octant = fine_octant[box_index]
        in_use = box_index % SLOTS < fine_count[box_index // SLOTS]
        amounts = box_states[box_index]
        result, payload = fine_box(amounts, fractions[box_index], shells_of(old_slabs[parent], octant),
                                   shells_of(new_slabs[parent], octant), octant, diffusivity, reaction)
        return jnp.where(in_use, result, amounts), jnp.where(in_use, payload, 0.0)

    fine_states, payloads = lax.map(fine_entry, jnp.arange(coarse_count, box_states.shape[0], dtype=jnp.int32))

    def finish_entry(entries):
        box_index, amounts, fraction, register, octant, child_code = entries
        safe_code = jnp.maximum(child_code, 0)
        level_row = safe_code // (offset_count * SLOTS) + 1
        offset = (safe_code // SLOTS) % offset_count - REACH
        column = box_index // SLOTS + offset
        source = (level_row * N_BOX + column) * SLOTS + safe_code % SLOTS - coarse_count
        source = jnp.clip(source, 0, payloads.shape[0] - 1)
        return coarse_finish(amounts, fraction, payloads[source], register, octant, child_code)

    coarse_states = lax.map(finish_entry, (jnp.arange(coarse_count, dtype=jnp.int32), updated, coarse_fraction,
                                           registers, coarse_octant, coarse_child))
    return jnp.concatenate([coarse_states, fine_states], axis=0)
```

```python
import functools

import jax
import jax.numpy as jnp
import numpy as np
from jax import lax
from jax.experimental import pallas as pl
from jax.experimental.pallas import tpu as pltpu
from jax.sharding import PartitionSpec as P

ADVECT = 0.4
COARSE_STEP = 0.5
FLOOR = 0.5
LEVELS = 15.0
SLOTS = 4
REACH = 2
OFFSETS = 2 * REACH + 1
F32 = jnp.float32
BF16 = jnp.bfloat16


def selection_tables():
    lane = np.arange(1024)
    y, z = lane // 32, lane % 32
    place = np.arange(256)
    a, b = place // 16, place % 16
    i = np.arange(16)
    sel_x = np.zeros((4, 1024, 256), np.float32)
    sel_yz = np.zeros((4, 1024, 128), np.float32)
    for octant in range(4):
        y_half, z_half = octant % 2, octant // 2
        sel_x[octant, (16 * y_half + a) * 32 + 16 * z_half + b, place] = 1
        for g in range(4):
            sel_yz[octant, (16 - y_half) * 32 + 16 * z_half + i, 32 * g + i] = 1
            sel_yz[octant, (16 * y_half + i) * 32 + 16 - z_half, 32 * g + 16 + i] = 1
    up_x = np.zeros((256, 1024), np.float32)
    up_x[(y // 2) * 16 + z // 2, lane] = 1
    up_y = np.zeros((128, 128), np.float32)
    up_z = np.zeros((128, 1024), np.float32)
    short = np.arange(128)
    for g in range(4):
        up_y[32 * g + (short % 32) // 2, short] = 1
        for edge in (0, 31):
            rows = np.arange(32)
            up_z[32 * g + 16 + rows // 2, rows * 32 + edge] = 1
    twice = np.zeros((256, 128), np.float32)
    rows = np.arange(256)
    twice[rows, rows // 32 * 16 + rows % 32 // 2] = 1
    return sel_x, sel_yz, up_x, up_y, up_z, twice


SEL_X, SEL_YZ, UP_X, UP_Y, UP_Z, TWICE = selection_tables()


def table(values):
    return jnp.asarray(values.astype(jnp.bfloat16))


def halves(a):
    high = a.astype(BF16)
    return high, (a - high.astype(F32)).astype(BF16)


def dot(a, b):
    return jnp.dot(a, b, preferred_element_type=F32)


def pick(a, w):
    high, low = halves(a)
    return dot(high, w) + dot(low, w)


def left_pick(w, a):
    high, low = halves(a)
    return dot(w, high) + dot(w, low)


def iota(shape, dim):
    return lax.broadcasted_iota(jnp.int32, shape, dim)


def pack_rows(rows):
    group = iota((32, 128), 1) // 32
    out = rows[0:32]
    for g in range(1, 4):
        out = jnp.where(group == g, rows[32 * g : 32 * g + 32], out)
    return out


def unpack_rows(packed):
    group = iota((32, 128), 1) // 32
    return jnp.concatenate([jnp.where(group == g, packed, 0.0) for g in range(4)], axis=0)


def species_column(values_ref, factor, width):
    row = iota((8, width), 0)
    out = jnp.zeros((8, width), F32)
    for s in range(8):
        out = jnp.where(row == s, values_ref[s] * factor, out)
    return out


def reaction_halves(reaction_ref, step):
    rates = reaction_ref[...]
    row = iota((256, 256), 0)
    column = iota((256, 256), 1)
    spread_row = (iota((256, 8), 0) // 32 == iota((256, 8), 1)).astype(F32)
    spread_column = (iota((8, 256), 1) // 32 == iota((8, 256), 0)).astype(F32)
    exact = lax.Precision.HIGHEST
    wide = jnp.dot(spread_row, rates, precision=exact, preferred_element_type=F32)
    wide = jnp.dot(wide, spread_column, precision=exact, preferred_element_type=F32)
    return halves(jnp.where(row % 32 == column % 32, step * wide, 0.0))


def load_cells(cells, amounts):
    for t in range(8):
        cells[:, t + 1, 8:40, :] = amounts[:, :, 128 * t : 128 * t + 128]


def prepare(f, f_low, f_high, fy_low, fy_high, fz, coef, scale):
    lane = iota((32, 1024), 1)
    row = iota((32, 1024), 0)
    depth = lane % 32
    scaling = scale / jnp.maximum(f, FLOOR)
    x_low = scaling * jnp.minimum(f, jnp.where(row == 0, f_low, pltpu.roll(f, 1, 0)))
    x_high = scaling * jnp.minimum(f, jnp.where(row == 31, f_high, pltpu.roll(f, 31, 0)))
    y_low = scaling * jnp.minimum(f, jnp.where(lane < 32, fy_low, pltpu.roll(f, 32, 1)))
    y_high = scaling * jnp.minimum(f, jnp.where(lane >= 992, fy_high, pltpu.roll(f, 992, 1)))
    z_low = scaling * jnp.where(depth == 0, 0.0, jnp.minimum(f, pltpu.roll(f, 1, 1)))
    z_high = scaling * jnp.where(depth == 31, 0.0, jnp.minimum(f, pltpu.roll(f, 1023, 1)))
    everything = x_low + x_high + y_low + y_high + z_low + z_high
    kinds = [x_low, x_high, y_low, y_high, z_low, z_high, everything, 1.0 - ADVECT * x_high, ADVECT * x_low]
    if fz is not None:
        kinds += [jnp.minimum(f, fz), scaling]
    for k, kind in enumerate(kinds):
        for t in range(8):
            coef[k, t] = kind[:, 128 * t : 128 * t + 128]


def react(cells, reacted, rates_high, rates_low):
    for n in range(4):
        block = jnp.concatenate(
            [cells[:, 2 * n + 1 + h, 8:40, :].reshape(256, 128) for h in range(2)], axis=1
        )
        high, low = halves(block)
        out = dot(rates_high, high) + dot(rates_low, high) + dot(rates_high, low)
        for h in range(2):
            reacted[:, 2 * n + h] = out[:, 128 * h : 128 * h + 128].reshape(8, 32, 128)


def advance(cells, coef, reacted, spread, store, ghost=None, held=None, first=True):
    lane = iota((8, 128), 1)

    def tile(t, carry):
        for xt in range(4):
            kinds = [coef[k, t, 8 * xt : 8 * xt + 8, :] for k in range(9 if ghost is None else 11)]
            x_low, x_high, y_low, y_high, z_low, z_high, everything, own, upwind = kinds[:9]
            at = 8 + 8 * xt
            for s in range(8):
                c = cells[s, t + 1, at : at + 8, :]
                below = cells[s, t + 1, at - 1 : at + 7, :]
                above = cells[s, t + 1, at + 1 : at + 9, :]
                left = pltpu.roll(jnp.where(lane >= 96, cells[s, t, at : at + 8, :], c), 32, 1)
                right = pltpu.roll(jnp.where(lane < 32, cells[s, t + 2, at : at + 8, :], c), 96, 1)
                change = x_low * below + x_high * above + y_low * left + y_high * right
                change = change + z_low * pltpu.roll(c, 1, 1) + z_high * pltpu.roll(c, 127, 1)
                change = change - everything * c
                if ghost is not None:
                    through = kinds[9] * (ghost[s, t, 8 * xt : 8 * xt + 8, :] - c)
                    if first:
                        held[s, t, 8 * xt : 8 * xt + 8, :] = through
                    else:
                        held[s, t, 8 * xt : 8 * xt + 8, :] += through
                    change = change + kinds[10] * through
                result = own * c + upwind * below + spread[s] * change
                store(s, t, xt, result + reacted[s, t, 8 * xt : 8 * xt + 8, :])
        return carry

    lax.fori_loop(0, 8, tile, 0)


def coarse_kernel(
    place, octants, codes, spread_ref, reaction_ref, box, code, before, code_before, after, code_after, sel_x, sel_yz,
    updated, message, halo, register, cells, coef, reacted, rates,
):
    i = pl.program_id(0)

    @pl.when(place[0] == 0)
    def _():
        @pl.when(i == 0)
        def _():
            high, low = reaction_halves(reaction_ref, COARSE_STEP)
            rates[0] = high
            rates[1] = low
            cells[:, 0] = jnp.zeros((8, 48, 128), F32)
            cells[:, 9] = jnp.zeros((8, 48, 128), F32)

        f = code[0].astype(F32) / LEVELS
        f_before = jnp.where(i > 0, code_before[0, 7:8, :].astype(F32) / LEVELS, 0.0)
        f_after = jnp.where(i < SLOTS - 1, code_after[0, 0:1, :].astype(F32) / LEVELS, 0.0)
        load_cells(cells, box[0])
        for t in range(8):
            cells[:, t + 1, 7, :] = before[0, :, 7, 128 * t : 128 * t + 128]
            cells[:, t + 1, 40, :] = after[0, :, 0, 128 * t : 128 * t + 128]
        prepare(f, f_before, f_after, 0.0, 0.0, None, coef, COARSE_STEP)
        react(cells, reacted, rates[0], rates[1])
        spread = [spread_ref[s] for s in range(8)]

        def store(s, t, xt, value):
            updated[0, s, 8 * xt : 8 * xt + 8, pl.ds(pl.multiple_of(128 * t, 128), 128)] = value

        advance(cells, coef, reacted, spread, store)

        octant = octants[i]
        y_half = octant % 2
        z_half = octant // 2
        wide = species_column(spread_ref, 1.0, 1024)
        row = iota((8, 1024), 0)
        c7, c8 = box[0, :, 7, :], box[0, :, 8, :]
        c23, c24 = box[0, :, 23, :], box[0, :, 24, :]
        faces = jnp.where(row == 0, f[7:8], jnp.where(row == 1, f[24:25], 0.0))
        low_flux = -jnp.minimum(f[7:8], f[8:9]) * (ADVECT * c7 - wide * (c8 - c7))
        high_flux = jnp.minimum(f[23:24], f[24:25]) * (ADVECT * c23 - wide * (c24 - c23))
        blank = jnp.zeros((8, 1024), F32)
        rows = [c7, c24, faces, updated[0, :, 7, :], updated[0, :, 24, :], low_flux, high_flux, blank]
        x_parts = pick(jnp.concatenate(rows, axis=0), sel_x[0])

        lane = iota((1, 1024), 1)
        y_row = lane // 32 == 16 - y_half
        y_roll = jnp.where(y_half == 0, 32, 992)
        z_roll = jnp.where(z_half == 0, 1, 1023)
        middle = f[8:24]
        inner_f = jnp.where(y_row, pltpu.roll(middle, y_roll, 1), pltpu.roll(middle, z_roll, 1))
        weight = -jnp.minimum(middle, inner_f)
        fluxes = []
        for s in range(8):
            c = box[0, s, 8:24, :]
            inner = jnp.where(y_row, pltpu.roll(c, y_roll, 1), pltpu.roll(c, z_roll, 1))
            fluxes.append(spread[s] * weight * (c - inner))
        old_rows = box[0, :, 8:24, :].reshape(128, 1024)
        new_rows = updated[0, :, 8:24, :].reshape(128, 1024)
        side_parts = pick(jnp.concatenate([old_rows, new_rows] + fluxes + [middle], axis=0), sel_yz[0])

        message[0, 0:24, :] = x_parts[0:24, 0:128]
        message[0, 24:48, :] = x_parts[0:24, 128:256]
        message[0, 48:80, :] = pack_rows(side_parts[0:128])
        message[0, 80:96, :] = side_parts[384:400]
        message[0, 96:112, :] = x_parts[24:40, 0:128]
        message[0, 112:128, :] = x_parts[24:40, 128:256]
        message[0, 128:160, :] = pack_rows(side_parts[128:256])
        register[0, 0:16, :] = x_parts[40:56, 0:128]
        register[0, 16:32, :] = x_parts[40:56, 128:256]
        register[0, 32:64, :] = pack_rows(side_parts[256:384])

        def put_plane(p, x):
            plane = box[0, :, x, :]
            for t in range(8):
                base = 32 + (p * 8 + t) * 16
                halo[base : base + 8, :] = plane[:, 128 * t : 128 * t + 128]
                halo[base + 8 : base + 16, :] = jnp.broadcast_to(f[x : x + 1, 128 * t : 128 * t + 128], (8, 128))

        @pl.when(i == 0)
        def _():
            halo[...] = jnp.zeros((640, 128), F32)
            where = iota((8, 128), 1)
            listed = jnp.zeros((8, 128), F32)
            for j in range(SLOTS):
                listed = jnp.where(where == j, codes[j].astype(F32), listed)
            halo[16:24, :] = listed
            put_plane(0, 0)

        @pl.when(i == SLOTS - 1)
        def _():
            put_plane(1, 31)


def fine_kernel(
    place, parents, octants, counts, spread_ref, reaction_ref, box, code, own, own_low, own_high, other, other_low,
    other_high, up_x, up_y, up_z, twice, mean_x, mean_y, mean_z, couple, _updated, states, payload,
    cells, later, coef, reacted, rates, ghost, held, chosen, x_faces, out, sems,
):
    i = pl.program_id(0)
    column = place[1]

    @pl.when(place[0] > 0)
    def _():
        slot = i % 2

        @pl.when(i == 0)
        def _():
            high, low = reaction_halves(reaction_ref, 0.5 * COARSE_STEP)
            rates[0] = high
            rates[1] = low

        @pl.when(i >= 2)
        def _():
            pltpu.make_async_copy(out.at[slot], states.at[i - 2], sems.at[slot]).wait()

        used = i < counts[0]

        @pl.when(jnp.logical_not(used))
        def _():
            out[slot] = box[0]

        @pl.when(used)
        def _():
            home = parents[i] // SLOTS
            away = (home >> 1) - (column >> 1)
            same = ((home - column) & 1) == 0
            for source, is_same, step in (
                (own_low, True, -1), (own, True, 0), (own_high, True, 1),
                (other_low, False, -1), (other, False, 0), (other_high, False, 1),
            ):

                @pl.when((same == is_same) & (away == step))
                def _():
                    chosen[...] = source[0]

            octant = octants[i]
            y_half = octant % 2
            z_half = octant // 2
            spread = [spread_ref[s] * 2.0 for s in range(8)]
            wide = species_column(spread_ref, 2.0, 128)
            f = code[0].astype(F32) / LEVELS

            x_old = jnp.concatenate([chosen[0:24], chosen[24:48]], axis=1)
            x_new = jnp.concatenate([chosen[96:112], chosen[112:128]], axis=1)
            x_mid = 0.5 * (x_old[0:16] + x_new)
            wide_x = pick(jnp.concatenate([x_old, x_mid, jnp.zeros((8, 256), F32)], axis=0), up_x[...])
            side_old = chosen[48:80]
            side_mid = 0.5 * (side_old + chosen[128:160])

            def side_ghosts(side):
                high, low = halves(unpack_rows(side))
                high = dot(twice[...], high).astype(BF16)
                low = dot(twice[...], low).astype(BF16)
                y_ghost = (dot(high, up_y[...]) + dot(low, up_y[...])).reshape(8, 32, 128)
                z_ghost = dot(high, up_z[...]) + dot(low, up_z[...])
                for t in range(8):
                    ghost[:, t] = z_ghost[:, 128 * t : 128 * t + 128].reshape(8, 32, 128)
                return y_ghost

            side_f = jnp.where(iota((16, 128), 1) < 32, chosen[80:96], 0.0)
            high, low = halves(side_f)
            high = dot(twice[0:32, 0:16], high).astype(BF16)
            low = dot(twice[0:32, 0:16], low).astype(BF16)
            fy = dot(high, up_y[...]) + dot(low, up_y[...])
            fz = dot(high, up_z[...]) + dot(low, up_z[...])
            edge = jnp.where(z_half == 1, 0, 31)
            fz = jnp.where(iota((32, 1024), 1) % 32 == edge, fz, 0.0)
            fy_low = jnp.where(y_half == 1, fy, 0.0)
            fy_high = jnp.where(y_half == 0, fy, 0.0)
            short = iota((32, 128), 1)
            y_first = jnp.where(short < 32, jnp.minimum(f[:, 0:128], fy_low), 0.0)
            y_last = jnp.where(short >= 96, jnp.minimum(f[:, 896:1024], fy_high), 0.0)
            f_low = wide_x[16:17]
            f_high = wide_x[17:18]
            prepare(
                f, f_low, f_high, jnp.concatenate([fy_low] * 8, axis=1), jnp.concatenate([fy_high] * 8, axis=1), fz,
                coef, COARSE_STEP,
            )
            m_low = jnp.minimum(f[0:1], f_low)
            m_high = jnp.minimum(f[31:32], f_high)
            load_cells(cells, box[0])

            def put_ghosts(to, low, high, y_ghost):
                for t in range(8):
                    to[:, t + 1, 7, :] = low[:, 128 * t : 128 * t + 128]
                    to[:, t + 1, 40, :] = high[:, 128 * t : 128 * t + 128]
                to[:, 0, 8:40, :] = y_ghost
                to[:, 9, 8:40, :] = y_ghost

            def face_fluxes(at, low, high, y_ghost, first):
                for t in range(8):
                    part = slice(128 * t, 128 * t + 128)
                    c0 = at[:, t + 1, 8, :]
                    c31 = at[:, t + 1, 39, :]
                    low_flux = -m_low[:, part] * (ADVECT * low[:, part] - wide * (c0 - low[:, part]))
                    high_flux = m_high[:, part] * (ADVECT * c31 - wide * (high[:, part] - c31))
                    if first:
                        x_faces[0:8, part] = low_flux
                        x_faces[8:16, part] = high_flux
                    else:
                        x_faces[0:8, part] += low_flux
                        x_faces[8:16, part] += high_flux
                return y_first * (y_ghost - at[:, 1, 8:40, :]) + y_last * (y_ghost - at[:, 8, 8:40, :])

            def store_later(s, t, xt, value):
                later[s, t + 1, 8 + 8 * xt : 16 + 8 * xt, :] = value

            def store_out(s, t, xt, value):
                out[slot, s, 8 * xt : 8 * xt + 8, pl.ds(pl.multiple_of(128 * t, 128), 128)] = value

            y_ghost = side_ghosts(side_old)
            put_ghosts(cells, wide_x[0:8], wide_x[8:16], y_ghost)
            y_flux = face_fluxes(cells, wide_x[0:8], wide_x[8:16], y_ghost, True)
            react(cells, reacted, rates[0], rates[1])
            advance(cells, coef, reacted, spread, store_later, ghost, held, True)
            y_ghost = side_ghosts(side_mid)
            put_ghosts(later, wide_x[24:32], wide_x[32:40], y_ghost)
            y_flux = y_flux + face_fluxes(later, wide_x[24:32], wide_x[32:40], y_ghost, False)
            react(later, reacted, rates[0], rates[1])
            advance(later, coef, reacted, spread, store_out, ghost, held, False)

            pooled = pick(out[slot].reshape(256, 1024), mean_x[...])
            payload[0, 0:128, :] = 0.5 * left_pick(couple[...], pooled)
            payload[0, 128:144, :] = 0.5 * pick(x_faces[...], mean_x[...])
            sides = pick(y_flux.reshape(256, 128), mean_y[...])
            for n in range(4):
                part = jnp.concatenate([held[:, 2 * n + h].reshape(256, 128) for h in range(2)], axis=1)
                sides = sides + pick(part, mean_z[256 * n : 256 * n + 256, :])
            sides = left_pick(couple[...], sides).reshape(8, 16, 128)
            sides = jnp.concatenate([(-0.5 * spread[s]) * sides[s] for s in range(8)], axis=0)
            sides = pack_rows(sides)
            payload[0, 144:160, 0:128] = sides[0:16]
            payload[0, 144:160, 128:256] = sides[16:32]

        pltpu.make_async_copy(out.at[slot], states.at[i], sems.at[slot]).start()

        @pl.when(i == SLOTS - 1)
        def _():
            pltpu.make_async_copy(out.at[1 - slot], states.at[i - 1], sems.at[1 - slot]).wait()
            pltpu.make_async_copy(out.at[slot], states.at[i], sems.at[slot]).wait()


def decode(code):
    safe = jnp.maximum(code, 0)
    return safe // (OFFSETS * SLOTS) + 1, safe // SLOTS % OFFSETS - REACH, safe % SLOTS


def route_kernel(
    place, codes, own1, own2, own3, other1, other2, other3, to_low, stay, to_high, sems
):
    column = place[1]

    @pl.when(place[0] == 0)
    def _():
        def each(act):
            for n, (step, target) in enumerate(((-1, to_low), (0, stay), (1, to_high))):
                for j in range(SLOTS):
                    code = codes[n, j]
                    row, offset, slot = decode(code)
                    child = column + 2 * step + offset
                    there = (code >= 0) & ((child >> 1) == (column >> 1))
                    for parity, sources in ((0, (own1, own2, own3)), (1, (other1, other2, other3))):
                        for r, source in enumerate(sources):

                            @pl.when(there & (((child - column) & 1) == parity) & (row == r + 1))
                            def _():
                                act(pltpu.make_async_copy(source.at[slot], target.at[j], sems.at[n * SLOTS + j]))

        each(lambda copy: copy.start())
        each(lambda copy: copy.wait())


def finish_kernel(
    place, octants, codes, spread_ref, updated, message, register, code_words, halo, other_low, other, other_high,
    from_low, stay, from_high, sel_x, sel_yz, states, chosen,
):
    i = pl.program_id(0)
    column = place[1]
    states[...] = updated[...]

    @pl.when(place[0] == 0)
    def _():
        wide = species_column(spread_ref, 1.0, 128)
        odd = (column & 1) == 1

        def end_plane(x, p, neighbour_p, neighbour):
            f = code_words[0, x : x + 1, :].astype(F32) / LEVELS
            scaling = COARSE_STEP / jnp.maximum(f, FLOOR)
            for t in range(8):
                part = slice(128 * t, 128 * t + 128)
                base = 32 + (p * 8 + t) * 16
                there = 32 + (neighbour_p * 8 + t) * 16
                c = halo[base : base + 8, :]
                g = neighbour(there, there + 8)
                m = jnp.minimum(f[:, part], neighbour(there + 8, there + 9))
                if p == 0:
                    gain = m * (ADVECT * g - wide * (c - g))
                else:
                    gain = -m * (ADVECT * c - wide * (g - c))
                states[0, :, x, part] += scaling[:, part] * gain

        @pl.when(i == 0)
        def _():
            end_plane(0, 0, 1, lambda a, b: jnp.where(odd, other[a:b, :], other_low[a:b, :]))

        @pl.when(i == SLOTS - 1)
        def _():
            end_plane(31, 1, 0, lambda a, b: jnp.where(odd, other_high[a:b, :], other[a:b, :]))

        child = codes[i]

        @pl.when(child >= 0)
        def _():
            _, offset, _ = decode(child)
            away = ((column + offset) >> 1) - (column >> 1)
            for step, source in ((-1, from_low), (0, stay), (1, from_high)):

                @pl.when(away == step)
                def _():
                    chosen[...] = source[0]

            octant = octants[i]
            y_half = octant % 2
            z_half = octant // 2
            lane = iota((1, 1024), 1)
            inside = (lane // 512 == y_half) & (lane % 32 // 16 == z_half)
            own_f = jnp.concatenate([message[0, 0:24, :], message[0, 24:48, :]], axis=1)
            half = iota((16, 256), 0) < 8
            x_f = jnp.where(half, own_f[16:17], own_f[17:18])
            reg_x = jnp.concatenate([register[0, 0:16, :], register[0, 16:32, :]], axis=1)
            fix_x = COARSE_STEP / jnp.maximum(x_f, FLOOR) * (chosen[128:144, :] - reg_x)
            side_f = jnp.concatenate([message[0, 80:96, :]] * 2, axis=0)
            sides = jnp.concatenate([chosen[144:160, 0:128], chosen[144:160, 128:256]], axis=0)
            fix_sides = COARSE_STEP / jnp.maximum(side_f, FLOOR) * (sides - register[0, 32:64, :])
            planes = pick(fix_x, sel_x[0])
            states[0, :, 7, :] += planes[0:8]
            states[0, :, 24, :] += planes[8:16]
            filled = pick(chosen[0:128, :], sel_x[0])
            added = pick(unpack_rows(fix_sides), sel_yz[0])
            for s in range(8):
                part = slice(16 * s, 16 * s + 16)
                here = states[0, s, 8:24, :]
                states[0, s, 8:24, :] = jnp.where(inside, filled[part], here + added[part])


def shifted(block, axis, distance):
    devices = range(lax.axis_size(axis))
    return lax.ppermute(block, axis, [(i - distance, i) for i in devices if i - distance in devices])


def per_device(
    box_states, cell_code, diffusivity, reaction, coarse_child, coarse_octant, fine_parent, fine_octant, fine_count
):
    row = lax.axis_index("lev")
    place = jnp.stack([row, lax.axis_index("box")]).astype(jnp.int32)
    count = lax.axis_size("box")
    swap = [(i, i ^ 1) for i in range(count)]
    vmem = pltpu.CompilerParams(vmem_limit_bytes=48 * 1024 * 1024)

    def whole(a):
        zeros = (0,) * a.ndim
        return pl.BlockSpec(a.shape, lambda i, *_: zeros)

    def each(shape):
        tail = (0,) * len(shape)
        return pl.BlockSpec((1,) + shape, lambda i, *_: (i,) + tail)

    smem = pl.BlockSpec(memory_space=pltpu.SMEM)
    hbm = pl.BlockSpec(memory_space=pl.ANY)
    previous = lambda i: jnp.maximum(i - 1, 0)
    following = lambda i: jnp.minimum(i + 1, SLOTS - 1)
    shape = jax.ShapeDtypeStruct
    sel_x, sel_yz = table(SEL_X), table(SEL_YZ)
    by_octant = lambda i, place, octants, *_: (octants[i], 0, 0)

    updated, message, halo, register = pl.pallas_call(
        coarse_kernel,
        grid_spec=pltpu.PrefetchScalarGridSpec(
            num_scalar_prefetch=3,
            grid=(SLOTS,),
            in_specs=[
                smem,
                whole(reaction),
                each((8, 32, 1024)),
                each((32, 1024)),
                pl.BlockSpec((1, 8, 8, 1024), lambda i, *_: (previous(i), 0, 3, 0)),
                pl.BlockSpec((1, 8, 1024), lambda i, *_: (previous(i), 3, 0)),
                pl.BlockSpec((1, 8, 8, 1024), lambda i, *_: (following(i), 0, 0, 0)),
                pl.BlockSpec((1, 8, 1024), lambda i, *_: (following(i), 0, 0)),
                pl.BlockSpec((1, 1024, 256), by_octant),
                pl.BlockSpec((1, 1024, 128), by_octant),
            ],
            out_specs=[
                each((8, 32, 1024)),
                each((160, 128)),
                pl.BlockSpec((640, 128), lambda i, *_: (0, 0)),
                each((64, 128)),
            ],
            scratch_shapes=[
                pltpu.VMEM((8, 10, 48, 128), F32),
                pltpu.VMEM((9, 8, 32, 128), F32),
                pltpu.VMEM((8, 8, 32, 128), F32),
                pltpu.VMEM((2, 256, 256), BF16),
            ],
        ),
        out_shape=[
            shape((SLOTS, 8, 32, 1024), F32),
            shape((SLOTS, 160, 128), F32),
            shape((640, 128), F32),
            shape((SLOTS, 64, 128), F32),
        ],
        compiler_params=vmem,
        name="coarse_step",
    )(
        place, coarse_octant, coarse_child, diffusivity, reaction, box_states, cell_code, box_states, cell_code,
        box_states, cell_code, sel_x, sel_yz,
    )

    spread_out = [lax.ppermute(message, "lev", [(0, r)]) for r in (1, 3, 2)]
    own = jnp.where(row == 0, halo.reshape(SLOTS, 160, 128), spread_out[0] + spread_out[1] + spread_out[2])
    own_low = shifted(own, "box", 2)
    own_high = shifted(own, "box", -2)
    other = lax.ppermute(own, "box", swap)
    other_low = lax.ppermute(own_low, "box", swap)
    other_high = lax.ppermute(own_high, "box", swap)
    near_codes = jnp.stack([a[0, 23, :SLOTS] for a in (own_low, own, own_high)]).astype(jnp.int32)

    def near(i, place, parents, *_):
        return (jnp.maximum(parents[i], 0) % SLOTS, 0, 0)

    up_x, up_y, up_z, twice = table(UP_X), table(UP_Y), table(UP_Z), table(TWICE)
    mean_x, mean_y, mean_z = table(0.25 * UP_X.T), table(0.25 * UP_Y.T), table(0.25 * UP_Z.T)
    couple = table(TWICE.T)
    constants = [up_x, up_y, up_z, twice, mean_x, mean_y, mean_z, couple]
    states, payload = pl.pallas_call(
        fine_kernel,
        grid_spec=pltpu.PrefetchScalarGridSpec(
            num_scalar_prefetch=4,
            grid=(SLOTS,),
            in_specs=[smem, whole(reaction), each((8, 32, 1024)), each((32, 1024))]
            + [pl.BlockSpec((1, 160, 128), near)] * 6
            + [whole(a) for a in constants]
            + [hbm],
            out_specs=[hbm, each((160, 256))],
            scratch_shapes=[
                pltpu.VMEM((8, 10, 48, 128), F32),
                pltpu.VMEM((8, 10, 48, 128), F32),
                pltpu.VMEM((11, 8, 32, 128), F32),
                pltpu.VMEM((8, 8, 32, 128), F32),
                pltpu.VMEM((2, 256, 256), BF16),
                pltpu.VMEM((8, 8, 32, 128), F32),
                pltpu.VMEM((8, 8, 32, 128), F32),
                pltpu.VMEM((160, 128), F32),
                pltpu.VMEM((16, 1024), F32),
                pltpu.VMEM((2, 8, 32, 1024), F32),
                pltpu.SemaphoreType.DMA((2,)),
            ],
        ),
        out_shape=[shape((SLOTS, 8, 32, 1024), F32), shape((SLOTS, 160, 256), F32)],
        input_output_aliases={4 + 4 + 6 + len(constants): 0},
        compiler_params=vmem,
        name="fine_steps",
    )(
        place, fine_parent, fine_octant, fine_count, diffusivity, reaction, box_states, cell_code, own, own_low,
        own_high, other, other_low, other_high, *constants, updated,
    )

    def level(pairs):
        return [(a, b) for a, b in pairs]

    home = [lax.ppermute(payload, "lev", [(r, 0)]) for r in (1, 2, 3)]
    across = [lax.ppermute(a, ("lev", "box"), [(i, i ^ 1) for i in range(count)]) for a in home]
    bundle = shape((SLOTS, 160, 256), F32)
    to_low, stay, to_high = pl.pallas_call(
        route_kernel,
        in_specs=[smem, smem] + [hbm] * 6,
        out_specs=[hbm] * 3,
        scratch_shapes=[pltpu.SemaphoreType.DMA((3 * SLOTS,))],
        out_shape=[bundle] * 3,
        name="route",
    )(place, near_codes, *home, *across)
    down = [(i, i - 2) for i in range(2, count)]
    up = [(i, i + 2) for i in range(count - 2)]
    from_high = lax.ppermute(to_low, ("lev", "box"), down)
    from_low = lax.ppermute(to_high, ("lev", "box"), up)

    back_x, back_yz = table(SEL_X.transpose(0, 2, 1)), table(SEL_YZ.transpose(0, 2, 1))
    flat = [a.reshape(640, 128) for a in (other_low, other, other_high)]
    return pl.pallas_call(
        finish_kernel,
        grid_spec=pltpu.PrefetchScalarGridSpec(
            num_scalar_prefetch=3,
            grid=(SLOTS,),
            in_specs=[smem, each((8, 32, 1024)), each((160, 128)), each((64, 128)), each((32, 1024))]
            + [whole(halo)] * 4
            + [each((160, 256))] * 3
            + [pl.BlockSpec((1, 256, 1024), by_octant), pl.BlockSpec((1, 128, 1024), by_octant)],
            out_specs=each((8, 32, 1024)),
            scratch_shapes=[pltpu.VMEM((160, 256), F32)],
        ),
        out_shape=shape((SLOTS, 8, 32, 1024), F32),
        input_output_aliases={4: 0},
        compiler_params=vmem,
        name="finish",
    )(
        place, coarse_octant, coarse_child, diffusivity, states, message, register, cell_code, halo, *flat,
        from_low, stay, from_high, back_x, back_yz,
    )


def solution(mesh):
    return jax.shard_map(
        per_device,
        mesh=mesh,
        in_specs=(
            P(("lev", "box"), None, None, None),
            P(("lev", "box"), None, None),
            P(),
            P(),
            P("box"),
            P("box"),
            P(("lev", "box")),
            P(("lev", "box")),
            P(("lev", "box")),
        ),
        out_specs=P(("lev", "box"), None, None, None),
        check_vma=False,
    )
```

```python
import functools

import jax
import jax.numpy as jnp
import numpy as np
from jax import lax
from jax.experimental import pallas as pl
from jax.experimental.pallas import tpu as pltpu
from jax.sharding import PartitionSpec as P

ADVECT = 0.4
COARSE_STEP = 0.5
FLOOR = 0.5
LEVELS = 15.0
SLOTS = 4
REACH = 2
OFFSETS = 2 * REACH + 1
F32 = jnp.float32
BF16 = jnp.bfloat16


def selection_tables():
    lane = np.arange(1024)
    y, z = lane // 32, lane % 32
    place = np.arange(256)
    a, b = place // 16, place % 16
    i = np.arange(16)
    sel_x = np.zeros((4, 1024, 256), np.float32)
    sel_yz = np.zeros((4, 1024, 128), np.float32)
    for octant in range(4):
        y_half, z_half = octant % 2, octant // 2
        sel_x[octant, (16 * y_half + a) * 32 + 16 * z_half + b, place] = 1
        for g in range(4):
            sel_yz[octant, (16 - y_half) * 32 + 16 * z_half + i, 32 * g + i] = 1
            sel_yz[octant, (16 * y_half + i) * 32 + 16 - z_half, 32 * g + 16 + i] = 1
    up_x = np.zeros((256, 1024), np.float32)
    up_x[(y // 2) * 16 + z // 2, lane] = 1
    up_y = np.zeros((128, 128), np.float32)
    up_z = np.zeros((128, 1024), np.float32)
    short = np.arange(128)
    for g in range(4):
        up_y[32 * g + (short % 32) // 2, short] = 1
        for edge in (0, 31):
            rows = np.arange(32)
            up_z[32 * g + 16 + rows // 2, rows * 32 + edge] = 1
    twice = np.zeros((256, 128), np.float32)
    rows = np.arange(256)
    twice[rows, rows // 32 * 16 + rows % 32 // 2] = 1
    window_z = np.zeros((2, 1024, 128), np.float32)
    for z_half in range(2):
        for step in range(3):
            rows = np.arange(32)
            window_z[z_half, rows * 32 + 15 - z_half + step, step * 32 + rows] = 1
    center = np.zeros((4, 256, 128), np.float32)
    for octant in range(4):
        for g in range(4):
            center[octant, 32 + 16 * (octant // 2) + i, 32 * g + i] = 1
            center[octant, 160 + 16 * (octant % 2) + i, 32 * g + 16 + i] = 1
    return sel_x, sel_yz, up_x, up_y, up_z, twice, window_z, center


SEL_X, SEL_YZ, UP_X, UP_Y, UP_Z, TWICE, WINDOW_Z, CENTER = selection_tables()


def table(values):
    return jnp.asarray(values.astype(jnp.bfloat16))


def halves(a):
    high = a.astype(BF16)
    return high, (a - high.astype(F32)).astype(BF16)


def dot(a, b):
    return jnp.dot(a, b, preferred_element_type=F32)


def pick(a, w):
    high, low = halves(a)
    return dot(high, w) + dot(low, w)


def left_pick(w, a):
    high, low = halves(a)
    return dot(w, high) + dot(w, low)


def iota(shape, dim):
    return lax.broadcasted_iota(jnp.int32, shape, dim)


def pack_rows(rows):
    group = iota((32, 128), 1) // 32
    out = rows[0:32]
    for g in range(1, 4):
        out = jnp.where(group == g, rows[32 * g : 32 * g + 32], out)
    return out


def unpack_rows(packed):
    group = iota((32, 128), 1) // 32
    return jnp.concatenate([jnp.where(group == g, packed, 0.0) for g in range(4)], axis=0)


def species_column(values_ref, factor, width):
    row = iota((8, width), 0)
    out = jnp.zeros((8, width), F32)
    for s in range(8):
        out = jnp.where(row == s, values_ref[s] * factor, out)
    return out


def reaction_halves(reaction_ref, step):
    rates = reaction_ref[...]
    row = iota((256, 256), 0)
    column = iota((256, 256), 1)
    spread_row = (iota((256, 8), 0) // 32 == iota((256, 8), 1)).astype(F32)
    spread_column = (iota((8, 256), 1) // 32 == iota((8, 256), 0)).astype(F32)
    exact = lax.Precision.HIGHEST
    wide = jnp.dot(spread_row, rates, precision=exact, preferred_element_type=F32)
    wide = jnp.dot(wide, spread_column, precision=exact, preferred_element_type=F32)
    return halves(jnp.where(row % 32 == column % 32, step * wide, 0.0))


def load_cells(cells, amounts):
    for t in range(8):
        cells[:, t + 1, 8:40, :] = amounts[:, :, 128 * t : 128 * t + 128]


def prepare(f, f_low, f_high, fy_low, fy_high, fz, coef, scale):
    lane = iota((32, 1024), 1)
    row = iota((32, 1024), 0)
    depth = lane % 32
    scaling = scale / jnp.maximum(f, FLOOR)
    x_low = scaling * jnp.minimum(f, jnp.where(row == 0, f_low, pltpu.roll(f, 1, 0)))
    x_high = scaling * jnp.minimum(f, jnp.where(row == 31, f_high, pltpu.roll(f, 31, 0)))
    y_low = scaling * jnp.minimum(f, jnp.where(lane < 32, fy_low, pltpu.roll(f, 32, 1)))
    y_high = scaling * jnp.minimum(f, jnp.where(lane >= 992, fy_high, pltpu.roll(f, 992, 1)))
    z_low = scaling * jnp.where(depth == 0, 0.0, jnp.minimum(f, pltpu.roll(f, 1, 1)))
    z_high = scaling * jnp.where(depth == 31, 0.0, jnp.minimum(f, pltpu.roll(f, 1023, 1)))
    everything = x_low + x_high + y_low + y_high + z_low + z_high
    kinds = [x_low, x_high, y_low, y_high, z_low, z_high, everything, 1.0 - ADVECT * x_high, ADVECT * x_low]
    if fz is not None:
        kinds += [jnp.minimum(f, fz), scaling]
    for k, kind in enumerate(kinds):
        for t in range(8):
            coef[k, t] = kind[:, 128 * t : 128 * t + 128]


def react(cells, reacted, rates_high, rates_low):
    for n in range(4):
        block = jnp.concatenate(
            [cells[:, 2 * n + 1 + h, 8:40, :].reshape(256, 128) for h in range(2)], axis=1
        )
        high, low = halves(block)
        out = dot(rates_high, high) + dot(rates_low, high) + dot(rates_high, low)
        for h in range(2):
            reacted[:, 2 * n + h] = out[:, 128 * h : 128 * h + 128].reshape(8, 32, 128)


def advance(cells, coef, reacted, spread, store, ghost=None, held=None, first=True):
    lane = iota((8, 128), 1)

    def tile(t, carry):
        for xt in range(4):
            kinds = [coef[k, t, 8 * xt : 8 * xt + 8, :] for k in range(9 if ghost is None else 11)]
            x_low, x_high, y_low, y_high, z_low, z_high, everything, own, upwind = kinds[:9]
            at = 8 + 8 * xt
            for s in range(8):
                c = cells[s, t + 1, at : at + 8, :]
                below = cells[s, t + 1, at - 1 : at + 7, :]
                above = cells[s, t + 1, at + 1 : at + 9, :]
                left = pltpu.roll(jnp.where(lane >= 96, cells[s, t, at : at + 8, :], c), 32, 1)
                right = pltpu.roll(jnp.where(lane < 32, cells[s, t + 2, at : at + 8, :], c), 96, 1)
                change = x_low * below + x_high * above + y_low * left + y_high * right
                change = change + z_low * pltpu.roll(c, 1, 1) + z_high * pltpu.roll(c, 127, 1)
                change = change - everything * c
                if ghost is not None:
                    through = kinds[9] * (ghost[s, t, 8 * xt : 8 * xt + 8, :] - c)
                    if first:
                        held[s, t, 8 * xt : 8 * xt + 8, :] = through
                    else:
                        held[s, t, 8 * xt : 8 * xt + 8, :] += through
                    change = change + kinds[10] * through
                result = own * c + upwind * below + spread[s] * change
                store(s, t, xt, result + reacted[s, t, 8 * xt : 8 * xt + 8, :])
        return carry

    lax.fori_loop(0, 8, tile, 0, unroll=2)


def message_kernel(
    octants, codes, spread_ref, reaction_ref, box, code, sel_x, window_z, center, message, halo, rates
):
    i = pl.program_id(0)
    row = lax.axis_index("lev")

    @pl.when(row == 0)
    def _():
        @pl.when(i == 0)
        def _():
            high, low = reaction_halves(reaction_ref, COARSE_STEP)
            rates[0] = high
            rates[1] = low

        octant = octants[i]
        y_half = octant % 2
        f = code[0].astype(F32) / LEVELS
        lane = iota((32, 128), 1)
        place = lane % 32
        turn = 32 * (1 + y_half)
        spread = [spread_ref[s] for s in range(8)]

        def window_y(a, b):
            return jnp.where(iota(a.shape, 1) < turn, pltpu.roll(a, turn, 1), pltpu.roll(b, turn, 1))

        around_y = window_y(
            box[0, :, :, 384:512].reshape(256, 128), box[0, :, :, 512:640].reshape(256, 128)
        )
        around_z = pick(box[0].reshape(256, 1024), window_z[0])
        f_windows = (window_y(f[:, 384:512], f[:, 512:640]), pick(f, window_z[0]))
        both = jnp.concatenate([around_y, around_z], axis=1)
        high, low = halves(both)
        reacted = dot(rates[0], high) + dot(rates[1], high) + dot(rates[0], low)
        old_rows, new_rows = [[], []], [[], []]
        for w, (around, fw) in enumerate(zip((around_y, around_z), f_windows)):
            inner = fw[8:24]
            scaling = COARSE_STEP / jnp.maximum(inner, FLOOR)
            x_low = scaling * jnp.minimum(inner, pltpu.roll(fw, 1, 0)[8:24])
            x_high = scaling * jnp.minimum(inner, pltpu.roll(fw, 31, 0)[8:24])
            low_side = scaling * jnp.minimum(inner, pltpu.roll(inner, 32, 1))
            high_side = scaling * jnp.minimum(inner, pltpu.roll(inner, 96, 1))
            before = scaling * jnp.where(place[8:24] == 0, 0.0, jnp.minimum(inner, pltpu.roll(inner, 1, 1)))
            after = scaling * jnp.where(place[8:24] == 31, 0.0, jnp.minimum(inner, pltpu.roll(inner, 127, 1)))
            everything = x_low + x_high + low_side + high_side + before + after
            own = 1.0 - ADVECT * x_high
            upwind = ADVECT * x_low
            for s in range(8):
                rows = around[32 * s : 32 * s + 32]
                c = rows[8:24]
                below = pltpu.roll(rows, 1, 0)[8:24]
                above = pltpu.roll(rows, 31, 0)[8:24]
                change = x_low * below + x_high * above
                change = change + low_side * pltpu.roll(c, 32, 1) + high_side * pltpu.roll(c, 96, 1)
                change = change + before * pltpu.roll(c, 1, 1) + after * pltpu.roll(c, 127, 1) - everything * c
                term = reacted[32 * s + 8 : 32 * s + 24, 128 * w : 128 * w + 128]
                old_rows[w].append(c)
                new_rows[w].append(own * c + upwind * below + spread[s] * change + term)
        fractions = jnp.concatenate([fw[8:24] for fw in f_windows], axis=1)
        sides = [
            jnp.concatenate([jnp.concatenate(part[0], axis=0), jnp.concatenate(part[1], axis=0)], axis=1)
            for part in (old_rows, new_rows)
        ]
        side_parts = pick(jnp.concatenate(sides + [fractions], axis=0), center[0])

        wide = species_column(spread_ref, 1.0, 1024)
        long = iota((1, 1024), 1)
        planes = [box[0, :, x, :] for x in (7, 24)]
        mixed = jnp.dot(
            reaction_ref[...], jnp.concatenate(planes, axis=1), precision=lax.Precision.HIGHEST,
            preferred_element_type=F32,
        )
        new_planes = []
        for n, x in enumerate((7, 24)):
            fx = f[x : x + 1]
            scaling = COARSE_STEP / jnp.maximum(fx, FLOOR)
            x_low = scaling * jnp.minimum(fx, f[x - 1 : x])
            x_high = scaling * jnp.minimum(fx, f[x + 1 : x + 2])
            shifts = ((32, long < 32), (992, long >= 992), (1, long % 32 == 0), (1023, long % 32 == 31))
            c = planes[n]
            below = box[0, :, x - 1, :]
            change = x_low * below + x_high * box[0, :, x + 1, :]
            everything = x_low + x_high
            for amount, wall in shifts:
                factor = scaling * jnp.where(wall, 0.0, jnp.minimum(fx, pltpu.roll(fx, amount, 1)))
                change = change + factor * pltpu.roll(c, amount, 1)
                everything = everything + factor
            change = change - everything * c
            moved = (1.0 - ADVECT * x_high) * c + ADVECT * x_low * below + wide * change
            new_planes.append(moved + COARSE_STEP * mixed[:, 1024 * n : 1024 * n + 1024])
        sublane = iota((8, 1024), 0)
        faces = jnp.where(sublane == 0, f[7:8], jnp.where(sublane == 1, f[24:25], 0.0))
        blank = jnp.zeros((8, 1024), F32)
        x_parts = pick(jnp.concatenate(planes + [faces] + new_planes + [blank], axis=0), sel_x[0])

        message[0, 0:24, :] = x_parts[0:24, 0:128]
        message[0, 24:48, :] = x_parts[0:24, 128:256]
        message[0, 48:80, :] = pack_rows(side_parts[0:128])
        message[0, 80:96, :] = side_parts[256:272]
        message[0, 96:112, :] = x_parts[24:40, 0:128]
        message[0, 112:128, :] = x_parts[24:40, 128:256]
        message[0, 128:160, :] = pack_rows(side_parts[128:256])

        def put_plane(p, x):
            plane = box[0, :, x, :]
            for t in range(8):
                base = 32 + (p * 8 + t) * 16
                halo[base : base + 8, :] = plane[:, 128 * t : 128 * t + 128]
                halo[base + 8 : base + 16, :] = jnp.broadcast_to(f[x : x + 1, 128 * t : 128 * t + 128], (8, 128))

        @pl.when(i == 0)
        def _():
            halo[...] = jnp.zeros((640, 128), F32)
            where = iota((8, 128), 1)
            listed = jnp.zeros((8, 128), F32)
            for j in range(SLOTS):
                listed = jnp.where(where == j, codes[j].astype(F32), listed)
            halo[16:24, :] = listed
            put_plane(0, 0)

        @pl.when(i == SLOTS - 1)
        def _():
            put_plane(1, 31)


def first_kernel(
    octants, counts, spread_ref, reaction_ref, box, code, before, code_before, after, code_after, sel_x, sel_yz,
    updated, register, cells, coef, reacted, rates,
):
    i = pl.program_id(0)
    coarse = lax.axis_index("lev") == 0

    @pl.when(coarse | (i < counts[0]))
    def _():
        @pl.when(i == 0)
        def _():
            high, low = reaction_halves(reaction_ref, jnp.where(coarse, COARSE_STEP, 0.5 * COARSE_STEP))
            rates[0] = high
            rates[1] = low
            cells[:, 0] = jnp.zeros((8, 48, 128), F32)
            cells[:, 9] = jnp.zeros((8, 48, 128), F32)

        f = code[0].astype(F32) / LEVELS
        f_before = jnp.where(coarse & (i > 0), code_before[0, 7:8, :].astype(F32) / LEVELS, 0.0)
        f_after = jnp.where(coarse & (i < SLOTS - 1), code_after[0, 0:1, :].astype(F32) / LEVELS, 0.0)
        load_cells(cells, box[0])
        for t in range(8):
            cells[:, t + 1, 7, :] = before[0, :, 7, 128 * t : 128 * t + 128]
            cells[:, t + 1, 40, :] = after[0, :, 0, 128 * t : 128 * t + 128]
        prepare(f, f_before, f_after, 0.0, 0.0, None, coef, COARSE_STEP)
        react(cells, reacted, rates[0], rates[1])
        fineness = jnp.where(coarse, 1.0, 2.0)
        spread = [spread_ref[s] * fineness for s in range(8)]

        def store(s, t, xt, value):
            updated[0, s, 8 * xt : 8 * xt + 8, pl.ds(pl.multiple_of(128 * t, 128), 128)] = value

        advance(cells, coef, reacted, spread, store)

        @pl.when(coarse)
        def _():
            octant = octants[i]
            y_half = octant % 2
            z_half = octant // 2
            wide = species_column(spread_ref, 1.0, 1024)
            c7, c8 = box[0, :, 7, :], box[0, :, 8, :]
            c23, c24 = box[0, :, 23, :], box[0, :, 24, :]
            low_flux = -jnp.minimum(f[7:8], f[8:9]) * (ADVECT * c7 - wide * (c8 - c7))
            high_flux = jnp.minimum(f[23:24], f[24:25]) * (ADVECT * c23 - wide * (c24 - c23))
            x_parts = pick(jnp.concatenate([low_flux, high_flux], axis=0), sel_x[0])

            lane = iota((1, 1024), 1)
            y_row = lane // 32 == 16 - y_half
            y_roll = jnp.where(y_half == 0, 32, 992)
            z_roll = jnp.where(z_half == 0, 1, 1023)
            middle = f[8:24]
            inner_f = jnp.where(y_row, pltpu.roll(middle, y_roll, 1), pltpu.roll(middle, z_roll, 1))
            weight = -jnp.minimum(middle, inner_f)
            fluxes = []
            for s in range(8):
                c = box[0, s, 8:24, :]
                inner = jnp.where(y_row, pltpu.roll(c, y_roll, 1), pltpu.roll(c, z_roll, 1))
                fluxes.append(spread_ref[s] * weight * (c - inner))
            side_parts = pick(jnp.concatenate(fluxes, axis=0), sel_yz[0])
            register[0, 0:16, :] = x_parts[:, 0:128]
            register[0, 16:32, :] = x_parts[:, 128:256]
            register[0, 32:64, :] = pack_rows(side_parts)


def fine_kernel(
    parents, octants, counts, spread_ref, reaction_ref, box, code, own, own_low, own_high, other, other_low,
    other_high, up_x, up_y, up_z, twice, mean_x, mean_y, mean_z, couple, started, states, payload,
    cells, coef, reacted, rates, ghost, held, chosen, x_faces, first, out, sems,
):
    i = pl.program_id(0)
    column = lax.axis_index("box")

    @pl.when(lax.axis_index("lev") > 0)
    def _():
        slot = i % 2

        @pl.when(i == 0)
        def _():
            high, low = reaction_halves(reaction_ref, 0.5 * COARSE_STEP)
            rates[0] = high
            rates[1] = low

        @pl.when(i >= 2)
        def _():
            pltpu.make_async_copy(out.at[slot], states.at[i - 2], sems.at[slot]).wait()

        used = i < counts[0]

        @pl.when((i == 0) & used)
        def _():
            pltpu.make_async_copy(started.at[i], first.at[slot], sems.at[2 + slot]).start()

        @pl.when(i + 1 < counts[0])
        def _():
            pltpu.make_async_copy(started.at[i + 1], first.at[1 - slot], sems.at[3 - slot]).start()

        @pl.when(jnp.logical_not(used))
        def _():
            out[slot] = box[0]

        @pl.when(used)
        def _():
            home = parents[i] // SLOTS
            away = (home >> 1) - (column >> 1)
            same = ((home - column) & 1) == 0
            for source, is_same, step in (
                (own_low, True, -1), (own, True, 0), (own_high, True, 1),
                (other_low, False, -1), (other, False, 0), (other_high, False, 1),
            ):

                @pl.when((same == is_same) & (away == step))
                def _():
                    chosen[...] = source[0]

            octant = octants[i]
            y_half = octant % 2
            z_half = octant // 2
            spread = [spread_ref[s] * 2.0 for s in range(8)]
            wide = species_column(spread_ref, 2.0, 128)
            f = code[0].astype(F32) / LEVELS

            x_old = jnp.concatenate([chosen[0:24], chosen[24:48]], axis=1)
            x_new = jnp.concatenate([chosen[96:112], chosen[112:128]], axis=1)
            x_mid = 0.5 * (x_old[0:16] + x_new)
            wide_x = pick(jnp.concatenate([x_old, x_mid, jnp.zeros((8, 256), F32)], axis=0), up_x[...])
            side_old = chosen[48:80]
            side_mid = 0.5 * (side_old + chosen[128:160])

            def side_ghosts(side):
                high, low = halves(unpack_rows(side))
                high = dot(twice[...], high).astype(BF16)
                low = dot(twice[...], low).astype(BF16)
                y_ghost = (dot(high, up_y[...]) + dot(low, up_y[...])).reshape(8, 32, 128)
                z_ghost = dot(high, up_z[...]) + dot(low, up_z[...])
                for t in range(8):
                    ghost[:, t] = z_ghost[:, 128 * t : 128 * t + 128].reshape(8, 32, 128)
                return y_ghost

            side_f = jnp.where(iota((16, 128), 1) < 32, chosen[80:96], 0.0)
            high, low = halves(side_f)
            high = dot(twice[0:32, 0:16], high).astype(BF16)
            low = dot(twice[0:32, 0:16], low).astype(BF16)
            fy = dot(high, up_y[...]) + dot(low, up_y[...])
            fz = dot(high, up_z[...]) + dot(low, up_z[...])
            edge = jnp.where(z_half == 1, 0, 31)
            fz = jnp.where(iota((32, 1024), 1) % 32 == edge, fz, 0.0)
            fy_low = jnp.where(y_half == 1, fy, 0.0)
            fy_high = jnp.where(y_half == 0, fy, 0.0)
            short = iota((32, 128), 1)
            y_first = jnp.where(short < 32, jnp.minimum(f[:, 0:128], fy_low), 0.0)
            y_last = jnp.where(short >= 96, jnp.minimum(f[:, 896:1024], fy_high), 0.0)
            f_low = wide_x[16:17]
            f_high = wide_x[17:18]
            prepare(
                f, f_low, f_high, jnp.concatenate([fy_low] * 8, axis=1), jnp.concatenate([fy_high] * 8, axis=1), fz,
                coef, COARSE_STEP,
            )
            m_low = jnp.minimum(f[0:1], f_low)
            m_high = jnp.minimum(f[31:32], f_high)

            inverse = COARSE_STEP / jnp.maximum(f, FLOOR)

            def face_fluxes(low, high, c0, c31, t):
                part = slice(128 * t, 128 * t + 128)
                low_flux = -m_low[:, part] * (ADVECT * low[:, part] - wide * (c0 - low[:, part]))
                high_flux = m_high[:, part] * (ADVECT * c31 - wide * (high[:, part] - c31))
                return low_flux, high_flux

            def store_out(s, t, xt, value):
                out[slot, s, 8 * xt : 8 * xt + 8, pl.ds(pl.multiple_of(128 * t, 128), 128)] = value

            y_ghost = side_ghosts(side_old)
            pltpu.make_async_copy(started.at[i], first.at[slot], sems.at[2 + slot]).wait()

            def open_z(t, carry):
                part = pl.ds(pl.multiple_of(128 * t, 128), 128)
                for xt in range(4):
                    rows = slice(8 * xt, 8 * xt + 8)
                    through_f = coef[9, t, rows, :]
                    scaling = coef[10, t, rows, :]
                    for s in range(8):
                        through = through_f * (ghost[s, t, rows, :] - box[0, s, rows, part])
                        held[s, t, rows, :] = through
                        cells[s, t + 1, 8 + 8 * xt : 16 + 8 * xt, :] = (
                            first[slot, s, rows, part] + spread[s] * (scaling * through)
                        )
                return carry

            lax.fori_loop(0, 8, open_z, 0)
            for t in range(8):
                part = slice(128 * t, 128 * t + 128)
                low_flux, high_flux = face_fluxes(wide_x[0:8], wide_x[8:16], box[0, :, 0, part], box[0, :, 31, part], t)
                x_faces[0:8, part] = low_flux
                x_faces[8:16, part] = high_flux
                cells[:, t + 1, 8, :] += -inverse[0:1, part] * low_flux
                cells[:, t + 1, 39, :] += -inverse[31:32, part] * high_flux
                cells[:, t + 1, 7, :] = wide_x[24:32, part]
                cells[:, t + 1, 40, :] = wide_x[32:40, part]
            y_low_flux = y_first * (y_ghost - box[0, :, :, 0:128])
            y_high_flux = y_last * (y_ghost - box[0, :, :, 896:1024])
            y_flux = y_low_flux + y_high_flux
            for s in range(8):
                cells[s, 1, 8:40, :] += spread[s] * (inverse[:, 0:128] * y_low_flux[s])
                cells[s, 8, 8:40, :] += spread[s] * (inverse[:, 896:1024] * y_high_flux[s])

            y_ghost = side_ghosts(side_mid)
            cells[:, 0, 8:40, :] = y_ghost
            cells[:, 9, 8:40, :] = y_ghost
            for t in range(8):
                part = slice(128 * t, 128 * t + 128)
                low_flux, high_flux = face_fluxes(wide_x[24:32], wide_x[32:40], cells[:, t + 1, 8, :], cells[:, t + 1, 39, :], t)
                x_faces[0:8, part] += low_flux
                x_faces[8:16, part] += high_flux
            y_flux = y_flux + y_first * (y_ghost - cells[:, 1, 8:40, :]) + y_last * (y_ghost - cells[:, 8, 8:40, :])
            react(cells, reacted, rates[0], rates[1])
            advance(cells, coef, reacted, spread, store_out, ghost, held, False)

            pooled = pick(out[slot].reshape(256, 1024), mean_x[...])
            payload[0, 0:128, :] = 0.5 * left_pick(couple[...], pooled)
            payload[0, 128:144, :] = 0.5 * pick(x_faces[...], mean_x[...])
            sides = pick(y_flux.reshape(256, 128), mean_y[...])
            for n in range(4):
                part = jnp.concatenate([held[:, 2 * n + h].reshape(256, 128) for h in range(2)], axis=1)
                sides = sides + pick(part, mean_z[256 * n : 256 * n + 256, :])
            sides = left_pick(couple[...], sides).reshape(8, 16, 128)
            sides = jnp.concatenate([(-0.5 * spread[s]) * sides[s] for s in range(8)], axis=0)
            sides = pack_rows(sides)
            payload[0, 144:160, 0:128] = sides[0:16]
            payload[0, 144:160, 128:256] = sides[16:32]

        pltpu.make_async_copy(out.at[slot], states.at[i], sems.at[slot]).start()

        @pl.when(i == SLOTS - 1)
        def _():
            pltpu.make_async_copy(out.at[1 - slot], states.at[i - 1], sems.at[1 - slot]).wait()
            pltpu.make_async_copy(out.at[slot], states.at[i], sems.at[slot]).wait()


def decode(code):
    safe = jnp.maximum(code, 0)
    return safe // (OFFSETS * SLOTS) + 1, safe // SLOTS % OFFSETS - REACH, safe % SLOTS


def route_kernel(
    low, own, high, own1, own2, own3, other1, other2, other3, to_low, stay, to_high, codes, sems
):
    column = lax.axis_index("box")

    @pl.when(lax.axis_index("lev") == 0)
    def _():
        lists = [
            pltpu.make_async_copy(source.at[0, 16:24], codes.at[n], sems.at[n]) for n, source in enumerate((low, own, high))
        ]
        for copy in lists:
            copy.start()
        for copy in lists:
            copy.wait()

        def each(act):
            for n, (step, target) in enumerate(((-1, to_low), (0, stay), (1, to_high))):
                for j in range(SLOTS):
                    code = codes[n, 7, j].astype(jnp.int32)
                    row, offset, slot = decode(code)
                    child = column + 2 * step + offset
                    there = (code >= 0) & ((child >> 1) == (column >> 1))
                    for parity, sources in ((0, (own1, own2, own3)), (1, (other1, other2, other3))):
                        for r, source in enumerate(sources):

                            @pl.when(there & (((child - column) & 1) == parity) & (row == r + 1))
                            def _():
                                act(pltpu.make_async_copy(source.at[slot], target.at[j], sems.at[n * SLOTS + j]))

        each(lambda copy: copy.start())
        each(lambda copy: copy.wait())


def finish_kernel(
    octants, codes, spread_ref, updated, message, register, code_words, halo, other_low, other, other_high,
    from_low, stay, from_high, sel_x, sel_yz, states, chosen,
):
    i = pl.program_id(0)
    column = lax.axis_index("box")
    states[...] = updated[...]

    @pl.when(lax.axis_index("lev") == 0)
    def _():
        wide = species_column(spread_ref, 1.0, 128)
        odd = (column & 1) == 1

        def end_plane(x, p, neighbour_p, neighbour):
            f = code_words[0, x : x + 1, :].astype(F32) / LEVELS
            scaling = COARSE_STEP / jnp.maximum(f, FLOOR)
            for t in range(8):
                part = slice(128 * t, 128 * t + 128)
                base = 32 + (p * 8 + t) * 16
                there = 32 + (neighbour_p * 8 + t) * 16
                c = halo[base : base + 8, :]
                g = neighbour(there, there + 8)
                m = jnp.minimum(f[:, part], neighbour(there + 8, there + 9))
                if p == 0:
                    gain = m * (ADVECT * g - wide * (c - g))
                else:
                    gain = -m * (ADVECT * c - wide * (g - c))
                states[0, :, x, part] += scaling[:, part] * gain

        @pl.when(i == 0)
        def _():
            end_plane(0, 0, 1, lambda a, b: jnp.where(odd, other[a:b, :], other_low[a:b, :]))

        @pl.when(i == SLOTS - 1)
        def _():
            end_plane(31, 1, 0, lambda a, b: jnp.where(odd, other_high[a:b, :], other[a:b, :]))

        child = codes[i]

        @pl.when(child >= 0)
        def _():
            _, offset, _ = decode(child)
            away = ((column + offset) >> 1) - (column >> 1)
            for step, source in ((-1, from_low), (0, stay), (1, from_high)):

                @pl.when(away == step)
                def _():
                    chosen[...] = source[0]

            octant = octants[i]
            y_half = octant % 2
            z_half = octant // 2
            lane = iota((1, 1024), 1)
            inside = (lane // 512 == y_half) & (lane % 32 // 16 == z_half)
            own_f = jnp.concatenate([message[0, 0:24, :], message[0, 24:48, :]], axis=1)
            half = iota((16, 256), 0) < 8
            x_f = jnp.where(half, own_f[16:17], own_f[17:18])
            reg_x = jnp.concatenate([register[0, 0:16, :], register[0, 16:32, :]], axis=1)
            fix_x = COARSE_STEP / jnp.maximum(x_f, FLOOR) * (chosen[128:144, :] - reg_x)
            side_f = jnp.concatenate([message[0, 80:96, :]] * 2, axis=0)
            sides = jnp.concatenate([chosen[144:160, 0:128], chosen[144:160, 128:256]], axis=0)
            fix_sides = COARSE_STEP / jnp.maximum(side_f, FLOOR) * (sides - register[0, 32:64, :])
            planes = pick(fix_x, sel_x[0])
            states[0, :, 7, :] += planes[0:8]
            states[0, :, 24, :] += planes[8:16]
            filled = pick(chosen[0:128, :], sel_x[0])
            added = pick(unpack_rows(fix_sides), sel_yz[0])
            for s in range(8):
                part = slice(16 * s, 16 * s + 16)
                here = states[0, s, 8:24, :]
                states[0, s, 8:24, :] = jnp.where(inside, filled[part], here + added[part])


def shifted(block, axis, distance):
    devices = range(lax.axis_size(axis))
    return lax.ppermute(block, axis, [(i - distance, i) for i in devices if i - distance in devices])


def per_device(
    box_states, cell_code, diffusivity, reaction, coarse_child, coarse_octant, fine_parent, fine_octant, fine_count
):
    row = lax.axis_index("lev")
    count = lax.axis_size("box")
    swap = [(i, i ^ 1) for i in range(count)]
    vmem = pltpu.CompilerParams(vmem_limit_bytes=62 * 1024 * 1024)

    def whole(a):
        zeros = (0,) * a.ndim
        return pl.BlockSpec(a.shape, lambda i, *_: zeros)

    def each(shape):
        tail = (0,) * len(shape)
        return pl.BlockSpec((1,) + shape, lambda i, *_: (i,) + tail)

    smem = pl.BlockSpec(memory_space=pltpu.SMEM)
    hbm = pl.BlockSpec(memory_space=pl.ANY)
    previous = lambda i: jnp.maximum(i - 1, 0)
    following = lambda i: jnp.minimum(i + 1, SLOTS - 1)
    shape = jax.ShapeDtypeStruct
    sel_x, sel_yz = table(SEL_X), table(SEL_YZ)
    by_octant = lambda i, octants, *_: (octants[i], 0, 0)

    message, halo = pl.pallas_call(
        message_kernel,
        grid_spec=pltpu.PrefetchScalarGridSpec(
            num_scalar_prefetch=2,
            grid=(SLOTS,),
            in_specs=[
                smem,
                whole(reaction),
                each((8, 32, 1024)),
                each((32, 1024)),
                pl.BlockSpec((1, 1024, 256), by_octant),
                pl.BlockSpec((1, 1024, 128), lambda i, octants, *_: (octants[i] // 2, 0, 0)),
                pl.BlockSpec((1, 256, 128), by_octant),
            ],
            out_specs=[each((160, 128)), pl.BlockSpec((640, 128), lambda i, *_: (0, 0))],
            scratch_shapes=[pltpu.VMEM((2, 256, 256), BF16)],
        ),
        out_shape=[shape((SLOTS, 160, 128), F32), shape((640, 128), F32)],
        compiler_params=vmem,
        name="shells",
    )(
        coarse_octant, coarse_child, diffusivity, reaction, box_states, cell_code, sel_x, table(WINDOW_Z), table(CENTER)
    )

    updated, register = pl.pallas_call(
        first_kernel,
        grid_spec=pltpu.PrefetchScalarGridSpec(
            num_scalar_prefetch=2,
            grid=(SLOTS,),
            in_specs=[
                smem,
                whole(reaction),
                each((8, 32, 1024)),
                each((32, 1024)),
                pl.BlockSpec((1, 8, 8, 1024), lambda i, *_: (previous(i), 0, 3, 0)),
                pl.BlockSpec((1, 8, 1024), lambda i, *_: (previous(i), 3, 0)),
                pl.BlockSpec((1, 8, 8, 1024), lambda i, *_: (following(i), 0, 0, 0)),
                pl.BlockSpec((1, 8, 1024), lambda i, *_: (following(i), 0, 0)),
                pl.BlockSpec((1, 1024, 256), by_octant),
                pl.BlockSpec((1, 1024, 128), by_octant),
            ],
            out_specs=[each((8, 32, 1024)), each((64, 128))],
            scratch_shapes=[
                pltpu.VMEM((8, 10, 48, 128), F32),
                pltpu.VMEM((9, 8, 32, 128), F32),
                pltpu.VMEM((8, 8, 32, 128), F32),
                pltpu.VMEM((2, 256, 256), BF16),
            ],
        ),
        out_shape=[shape((SLOTS, 8, 32, 1024), F32), shape((SLOTS, 64, 128), F32)],
        compiler_params=vmem,
        cost_estimate=pl.CostEstimate(flops=10**9, bytes_accessed=40 * 10**6, transcendentals=0),
        name="first_step",
    )(
        coarse_octant, fine_count, diffusivity, reaction, box_states, cell_code, box_states, cell_code,
        box_states, cell_code, sel_x, sel_yz,
    )

    spread_out = [lax.ppermute(message, "lev", [(0, r)]) for r in (1, 3, 2)]
    *spread_out, updated = lax.optimization_barrier((*spread_out, updated))
    own = jnp.where(row == 0, halo.reshape(SLOTS, 160, 128), spread_out[0] + spread_out[1] + spread_out[2])
    own_low = shifted(own, "box", 2)
    own_high = shifted(own, "box", -2)
    other = lax.ppermute(own, "box", swap)
    other_low = lax.ppermute(own_low, "box", swap)
    other_high = lax.ppermute(own_high, "box", swap)

    def near(i, parents, *_):
        return (jnp.maximum(parents[i], 0) % SLOTS, 0, 0)

    up_x, up_y, up_z, twice = table(UP_X), table(UP_Y), table(UP_Z), table(TWICE)
    mean_x, mean_y, mean_z = table(0.25 * UP_X.T), table(0.25 * UP_Y.T), table(0.25 * UP_Z.T)
    couple = table(TWICE.T)
    constants = [up_x, up_y, up_z, twice, mean_x, mean_y, mean_z, couple]
    states, payload = pl.pallas_call(
        fine_kernel,
        grid_spec=pltpu.PrefetchScalarGridSpec(
            num_scalar_prefetch=3,
            grid=(SLOTS,),
            in_specs=[smem, whole(reaction), each((8, 32, 1024)), each((32, 1024))]
            + [pl.BlockSpec((1, 160, 128), near)] * 6
            + [whole(a) for a in constants]
            + [hbm],
            out_specs=[hbm, each((160, 256))],
            scratch_shapes=[
                pltpu.VMEM((8, 10, 48, 128), F32),
                pltpu.VMEM((11, 8, 32, 128), F32),
                pltpu.VMEM((8, 8, 32, 128), F32),
                pltpu.VMEM((2, 256, 256), BF16),
                pltpu.VMEM((8, 8, 32, 128), F32),
                pltpu.VMEM((8, 8, 32, 128), F32),
                pltpu.VMEM((160, 128), F32),
                pltpu.VMEM((16, 1024), F32),
                pltpu.VMEM((2, 8, 32, 1024), F32),
                pltpu.VMEM((2, 8, 32, 1024), F32),
                pltpu.SemaphoreType.DMA((4,)),
            ],
        ),
        out_shape=[shape((SLOTS, 8, 32, 1024), F32), shape((SLOTS, 160, 256), F32)],
        input_output_aliases={3 + 4 + 6 + len(constants): 0},
        compiler_params=vmem,
        name="fine_steps",
    )(
        fine_parent, fine_octant, fine_count, diffusivity, reaction, box_states, cell_code, own, own_low,
        own_high, other, other_low, other_high, *constants, updated,
    )

    def level(pairs):
        return [(a, b) for a, b in pairs]

    home = [lax.ppermute(payload, "lev", [(r, 0)]) for r in (1, 2, 3)]
    across = [lax.ppermute(a, ("lev", "box"), [(i, i ^ 1) for i in range(count)]) for a in home]
    bundle = shape((SLOTS, 160, 256), F32)
    to_low, stay, to_high = pl.pallas_call(
        route_kernel,
        in_specs=[hbm] * 9,
        out_specs=[pl.BlockSpec(memory_space=pltpu.VMEM)] * 3,
        scratch_shapes=[pltpu.SMEM((3, 8, 128), F32), pltpu.SemaphoreType.DMA((3 * SLOTS,))],
        out_shape=[bundle] * 3,
        compiler_params=vmem,
        name="route",
    )(own_low, own, own_high, *home, *across)
    down = [(i, i - 2) for i in range(2, count)]
    up = [(i, i + 2) for i in range(count - 2)]
    from_high = lax.ppermute(to_low, ("lev", "box"), down)
    from_low = lax.ppermute(to_high, ("lev", "box"), up)

    back_x, back_yz = table(SEL_X.transpose(0, 2, 1)), table(SEL_YZ.transpose(0, 2, 1))
    flat = [a.reshape(640, 128) for a in (other_low, other, other_high)]
    return pl.pallas_call(
        finish_kernel,
        grid_spec=pltpu.PrefetchScalarGridSpec(
            num_scalar_prefetch=2,
            grid=(SLOTS,),
            in_specs=[smem, each((8, 32, 1024)), each((160, 128)), each((64, 128)), each((32, 1024))]
            + [whole(halo)] * 4
            + [each((160, 256))] * 3
            + [pl.BlockSpec((1, 256, 1024), by_octant), pl.BlockSpec((1, 128, 1024), by_octant)],
            out_specs=each((8, 32, 1024)),
            scratch_shapes=[pltpu.VMEM((160, 256), F32)],
        ),
        out_shape=shape((SLOTS, 8, 32, 1024), F32),
        input_output_aliases={3: 0},
        compiler_params=vmem,
        name="finish",
    )(
        coarse_octant, coarse_child, diffusivity, states, message, register, cell_code, halo, *flat,
        from_low, stay, from_high, back_x, back_yz,
    )


def solution(mesh):
    return jax.shard_map(
        per_device,
        mesh=mesh,
        in_specs=(
            P(("lev", "box"), None, None, None),
            P(("lev", "box"), None, None),
            P(),
            P(),
            P("box"),
            P("box"),
            P(("lev", "box")),
            P(("lev", "box")),
            P(("lev", "box")),
        ),
        out_specs=P(("lev", "box"), None, None, None),
        check_vma=False,
    )
```

```python
import functools

import jax
import jax.numpy as jnp
import numpy as np
from jax import lax
from jax.experimental import pallas as pl
from jax.experimental.pallas import tpu as pltpu
from jax.sharding import PartitionSpec as P

ADVECT = 0.4
COARSE_STEP = 0.5
FLOOR = 0.5
LEVELS = 15.0
SLOTS = 4
REACH = 2
OFFSETS = 2 * REACH + 1
F32 = jnp.float32
BF16 = jnp.bfloat16


def selection_tables():
    lane = np.arange(1024)
    y, z = lane // 32, lane % 32
    place = np.arange(256)
    a, b = place // 16, place % 16
    i = np.arange(16)
    sel_x = np.zeros((4, 1024, 256), np.float32)
    sel_yz = np.zeros((4, 1024, 128), np.float32)
    for octant in range(4):
        y_half, z_half = octant % 2, octant // 2
        sel_x[octant, (16 * y_half + a) * 32 + 16 * z_half + b, place] = 1
        for g in range(4):
            sel_yz[octant, (16 - y_half) * 32 + 16 * z_half + i, 32 * g + i] = 1
            sel_yz[octant, (16 * y_half + i) * 32 + 16 - z_half, 32 * g + 16 + i] = 1
    up_x = np.zeros((256, 1024), np.float32)
    up_x[(y // 2) * 16 + z // 2, lane] = 1
    up_y = np.zeros((128, 128), np.float32)
    up_z = np.zeros((128, 1024), np.float32)
    short = np.arange(128)
    for g in range(4):
        up_y[32 * g + (short % 32) // 2, short] = 1
        for edge in (0, 31):
            rows = np.arange(32)
            up_z[32 * g + 16 + rows // 2, rows * 32 + edge] = 1
    twice = np.zeros((256, 128), np.float32)
    rows = np.arange(256)
    twice[rows, rows // 32 * 16 + rows % 32 // 2] = 1
    window_z = np.zeros((2, 1024, 128), np.float32)
    for z_half in range(2):
        for step in range(3):
            rows = np.arange(32)
            window_z[z_half, rows * 32 + 15 - z_half + step, step * 32 + rows] = 1
    center = np.zeros((4, 256, 128), np.float32)
    for octant in range(4):
        for g in range(4):
            center[octant, 32 + 16 * (octant // 2) + i, 32 * g + i] = 1
            center[octant, 160 + 16 * (octant % 2) + i, 32 * g + 16 + i] = 1
    return sel_x, sel_yz, up_x, up_y, up_z, twice, window_z, center


SEL_X, SEL_YZ, UP_X, UP_Y, UP_Z, TWICE, WINDOW_Z, CENTER = selection_tables()


def table(values):
    return jnp.asarray(values.astype(jnp.bfloat16))


def halves(a):
    high = a.astype(BF16)
    return high, (a - high.astype(F32)).astype(BF16)


def dot(a, b):
    return jnp.dot(a, b, preferred_element_type=F32)


def pick(a, w):
    high, low = halves(a)
    return dot(high, w) + dot(low, w)


def left_pick(w, a):
    high, low = halves(a)
    return dot(w, high) + dot(w, low)


def iota(shape, dim):
    return lax.broadcasted_iota(jnp.int32, shape, dim)


def pack_rows(rows):
    group = iota((32, 128), 1) // 32
    out = rows[0:32]
    for g in range(1, 4):
        out = jnp.where(group == g, rows[32 * g : 32 * g + 32], out)
    return out


def unpack_rows(packed):
    group = iota((32, 128), 1) // 32
    return jnp.concatenate([jnp.where(group == g, packed, 0.0) for g in range(4)], axis=0)


def species_column(values_ref, factor, width):
    row = iota((8, width), 0)
    out = jnp.zeros((8, width), F32)
    for s in range(8):
        out = jnp.where(row == s, values_ref[s] * factor, out)
    return out


def reaction_halves(reaction_ref, step):
    rates = reaction_ref[...]
    row = iota((256, 256), 0)
    column = iota((256, 256), 1)
    spread_row = (iota((256, 8), 0) // 32 == iota((256, 8), 1)).astype(F32)
    spread_column = (iota((8, 256), 1) // 32 == iota((8, 256), 0)).astype(F32)
    exact = lax.Precision.HIGHEST
    wide = jnp.dot(spread_row, rates, precision=exact, preferred_element_type=F32)
    wide = jnp.dot(wide, spread_column, precision=exact, preferred_element_type=F32)
    return halves(jnp.where(row % 32 == column % 32, step * wide, 0.0))


def load_cells(cells, amounts):
    for t in range(8):
        cells[:, t + 1, 8:40, :] = amounts[:, :, 128 * t : 128 * t + 128]


def prepare(f, f_low, f_high, fy_low, fy_high, fz, coef, scale):
    lane = iota((32, 1024), 1)
    row = iota((32, 1024), 0)
    depth = lane % 32
    scaling = scale / jnp.maximum(f, FLOOR)
    x_low = scaling * jnp.minimum(f, jnp.where(row == 0, f_low, pltpu.roll(f, 1, 0)))
    x_high = scaling * jnp.minimum(f, jnp.where(row == 31, f_high, pltpu.roll(f, 31, 0)))
    y_low = scaling * jnp.minimum(f, jnp.where(lane < 32, fy_low, pltpu.roll(f, 32, 1)))
    y_high = scaling * jnp.minimum(f, jnp.where(lane >= 992, fy_high, pltpu.roll(f, 992, 1)))
    z_low = scaling * jnp.where(depth == 0, 0.0, jnp.minimum(f, pltpu.roll(f, 1, 1)))
    z_high = scaling * jnp.where(depth == 31, 0.0, jnp.minimum(f, pltpu.roll(f, 1023, 1)))
    everything = x_low + x_high + y_low + y_high + z_low + z_high
    kinds = [x_low, x_high, y_low, y_high, z_low, z_high, everything, 1.0 - ADVECT * x_high, ADVECT * x_low]
    if fz is not None:
        kinds += [jnp.minimum(f, fz), scaling]
    for k, kind in enumerate(kinds):
        for t in range(8):
            coef[k, t] = kind[:, 128 * t : 128 * t + 128]


def react(cells, reacted, rates_high, rates_low):
    for n in range(4):
        block = jnp.concatenate(
            [cells[:, 2 * n + 1 + h, 8:40, :].reshape(256, 128) for h in range(2)], axis=1
        )
        high, low = halves(block)
        out = dot(rates_high, high) + dot(rates_low, high) + dot(rates_high, low)
        for h in range(2):
            reacted[:, 2 * n + h] = out[:, 128 * h : 128 * h + 128].reshape(8, 32, 128)


def advance(cells, coef, reacted, spread, store, ghost=None, held=None, first=True):
    lane = iota((8, 128), 1)

    def tile(t, carry):
        for xt in range(4):
            kinds = [coef[k, t, 8 * xt : 8 * xt + 8, :] for k in range(9 if ghost is None else 11)]
            x_low, x_high, y_low, y_high, z_low, z_high, everything, own, upwind = kinds[:9]
            at = 8 + 8 * xt
            for s in range(8):
                c = cells[s, t + 1, at : at + 8, :]
                below = cells[s, t + 1, at - 1 : at + 7, :]
                above = cells[s, t + 1, at + 1 : at + 9, :]
                left = pltpu.roll(jnp.where(lane >= 96, cells[s, t, at : at + 8, :], c), 32, 1)
                right = pltpu.roll(jnp.where(lane < 32, cells[s, t + 2, at : at + 8, :], c), 96, 1)
                change = x_low * below + x_high * above + y_low * left + y_high * right
                change = change + z_low * pltpu.roll(c, 1, 1) + z_high * pltpu.roll(c, 127, 1)
                change = change - everything * c
                if ghost is not None:
                    through = kinds[9] * (ghost[s, t, 8 * xt : 8 * xt + 8, :] - c)
                    if first:
                        held[s, t, 8 * xt : 8 * xt + 8, :] = through
                    else:
                        held[s, t, 8 * xt : 8 * xt + 8, :] += through
                    change = change + kinds[10] * through
                result = own * c + upwind * below + spread[s] * change
                store(s, t, xt, result + reacted[s, t, 8 * xt : 8 * xt + 8, :])
        return carry

    lax.fori_loop(0, 8, tile, 0, unroll=2)


def message_kernel(
    octants, codes, spread_ref, reaction_ref, box, code, sel_x, window_z, center, message, halo, rates
):
    i = pl.program_id(0)
    row = lax.axis_index("lev")

    @pl.when(row == 0)
    def _():
        @pl.when(i == 0)
        def _():
            high, low = reaction_halves(reaction_ref, COARSE_STEP)
            rates[0] = high
            rates[1] = low

        octant = octants[i]
        y_half = octant % 2
        f = code[0].astype(F32) / LEVELS
        lane = iota((32, 128), 1)
        place = lane % 32
        turn = 32 * (1 + y_half)
        spread = [spread_ref[s] for s in range(8)]

        def window_y(a, b):
            return jnp.where(iota(a.shape, 1) < turn, pltpu.roll(a, turn, 1), pltpu.roll(b, turn, 1))

        around_y = window_y(
            box[0, :, :, 384:512].reshape(256, 128), box[0, :, :, 512:640].reshape(256, 128)
        )
        around_z = pick(box[0].reshape(256, 1024), window_z[0])
        f_windows = (window_y(f[:, 384:512], f[:, 512:640]), pick(f, window_z[0]))
        both = jnp.concatenate([around_y, around_z], axis=1)
        high, low = halves(both)
        reacted = dot(rates[0], high) + dot(rates[1], high) + dot(rates[0], low)
        old_rows, new_rows = [[], []], [[], []]
        for w, (around, fw) in enumerate(zip((around_y, around_z), f_windows)):
            inner = fw[8:24]
            scaling = COARSE_STEP / jnp.maximum(inner, FLOOR)
            x_low = scaling * jnp.minimum(inner, pltpu.roll(fw, 1, 0)[8:24])
            x_high = scaling * jnp.minimum(inner, pltpu.roll(fw, 31, 0)[8:24])
            low_side = scaling * jnp.minimum(inner, pltpu.roll(inner, 32, 1))
            high_side = scaling * jnp.minimum(inner, pltpu.roll(inner, 96, 1))
            before = scaling * jnp.where(place[8:24] == 0, 0.0, jnp.minimum(inner, pltpu.roll(inner, 1, 1)))
            after = scaling * jnp.where(place[8:24] == 31, 0.0, jnp.minimum(inner, pltpu.roll(inner, 127, 1)))
            everything = x_low + x_high + low_side + high_side + before + after
            own = 1.0 - ADVECT * x_high
            upwind = ADVECT * x_low
            for s in range(8):
                rows = around[32 * s : 32 * s + 32]
                c = rows[8:24]
                below = pltpu.roll(rows, 1, 0)[8:24]
                above = pltpu.roll(rows, 31, 0)[8:24]
                change = x_low * below + x_high * above
                change = change + low_side * pltpu.roll(c, 32, 1) + high_side * pltpu.roll(c, 96, 1)
                change = change + before * pltpu.roll(c, 1, 1) + after * pltpu.roll(c, 127, 1) - everything * c
                term = reacted[32 * s + 8 : 32 * s + 24, 128 * w : 128 * w + 128]
                old_rows[w].append(c)
                new_rows[w].append(own * c + upwind * below + spread[s] * change + term)
        fractions = jnp.concatenate([fw[8:24] for fw in f_windows], axis=1)
        sides = [
            jnp.concatenate([jnp.concatenate(part[0], axis=0), jnp.concatenate(part[1], axis=0)], axis=1)
            for part in (old_rows, new_rows)
        ]
        side_parts = pick(jnp.concatenate(sides + [fractions], axis=0), center[0])

        wide = species_column(spread_ref, 1.0, 1024)
        long = iota((1, 1024), 1)
        planes = [box[0, :, x, :] for x in (7, 24)]
        mixed = jnp.dot(
            reaction_ref[...], jnp.concatenate(planes, axis=1), precision=lax.Precision.HIGHEST,
            preferred_element_type=F32,
        )
        new_planes = []
        for n, x in enumerate((7, 24)):
            fx = f[x : x + 1]
            scaling = COARSE_STEP / jnp.maximum(fx, FLOOR)
            x_low = scaling * jnp.minimum(fx, f[x - 1 : x])
            x_high = scaling * jnp.minimum(fx, f[x + 1 : x + 2])
            shifts = ((32, long < 32), (992, long >= 992), (1, long % 32 == 0), (1023, long % 32 == 31))
            c = planes[n]
            below = box[0, :, x - 1, :]
            change = x_low * below + x_high * box[0, :, x + 1, :]
            everything = x_low + x_high
            for amount, wall in shifts:
                factor = scaling * jnp.where(wall, 0.0, jnp.minimum(fx, pltpu.roll(fx, amount, 1)))
                change = change + factor * pltpu.roll(c, amount, 1)
                everything = everything + factor
            change = change - everything * c
            moved = (1.0 - ADVECT * x_high) * c + ADVECT * x_low * below + wide * change
            new_planes.append(moved + COARSE_STEP * mixed[:, 1024 * n : 1024 * n + 1024])
        sublane = iota((8, 1024), 0)
        faces = jnp.where(sublane == 0, f[7:8], jnp.where(sublane == 1, f[24:25], 0.0))
        blank = jnp.zeros((8, 1024), F32)
        x_parts = pick(jnp.concatenate(planes + [faces] + new_planes + [blank], axis=0), sel_x[0])

        where = iota((8, 128), 1)
        listed = jnp.zeros((8, 128), F32)
        for j in range(SLOTS):
            listed = jnp.where(where == j, codes[j].astype(F32), listed)
        message[0, 0:16, :] = x_parts[0:16, 0:128]
        message[0, 16:24, :] = jnp.where(iota((8, 128), 0) == 7, listed, x_parts[16:24, 0:128])
        message[0, 24:48, :] = x_parts[0:24, 128:256]
        message[0, 48:80, :] = pack_rows(side_parts[0:128])
        message[0, 80:96, :] = side_parts[256:272]
        message[0, 96:112, :] = x_parts[24:40, 0:128]
        message[0, 112:128, :] = x_parts[24:40, 128:256]
        message[0, 128:160, :] = pack_rows(side_parts[128:256])

        def put_plane(p, x):
            plane = box[0, :, x, :]
            for t in range(8):
                base = 32 + (p * 8 + t) * 16
                halo[base : base + 8, :] = plane[:, 128 * t : 128 * t + 128]
                halo[base + 8 : base + 16, :] = jnp.broadcast_to(f[x : x + 1, 128 * t : 128 * t + 128], (8, 128))

        @pl.when(i == 0)
        def _():
            halo[...] = jnp.zeros((640, 128), F32)
            halo[16:24, :] = listed
            put_plane(0, 0)

        @pl.when(i == SLOTS - 1)
        def _():
            put_plane(1, 31)


def first_kernel(
    octants, counts, spread_ref, reaction_ref, box, code, before, code_before, after, code_after, sel_x, sel_yz,
    updated, register, cells, coef, reacted, rates,
):
    i = pl.program_id(0)
    coarse = lax.axis_index("lev") == 0

    @pl.when(coarse | (i < counts[0]))
    def _():
        @pl.when(i == 0)
        def _():
            high, low = reaction_halves(reaction_ref, jnp.where(coarse, COARSE_STEP, 0.5 * COARSE_STEP))
            rates[0] = high
            rates[1] = low
            cells[:, 0] = jnp.zeros((8, 48, 128), F32)
            cells[:, 9] = jnp.zeros((8, 48, 128), F32)

        f = code[0].astype(F32) / LEVELS
        f_before = jnp.where(coarse & (i > 0), code_before[0, 7:8, :].astype(F32) / LEVELS, 0.0)
        f_after = jnp.where(coarse & (i < SLOTS - 1), code_after[0, 0:1, :].astype(F32) / LEVELS, 0.0)
        load_cells(cells, box[0])
        for t in range(8):
            cells[:, t + 1, 7, :] = before[0, :, 7, 128 * t : 128 * t + 128]
            cells[:, t + 1, 40, :] = after[0, :, 0, 128 * t : 128 * t + 128]
        prepare(f, f_before, f_after, 0.0, 0.0, None, coef, COARSE_STEP)
        react(cells, reacted, rates[0], rates[1])
        fineness = jnp.where(coarse, 1.0, 2.0)
        spread = [spread_ref[s] * fineness for s in range(8)]

        def store(s, t, xt, value):
            updated[0, s, 8 * xt : 8 * xt + 8, pl.ds(pl.multiple_of(128 * t, 128), 128)] = value

        advance(cells, coef, reacted, spread, store)

        @pl.when(coarse)
        def _():
            octant = octants[i]
            y_half = octant % 2
            z_half = octant // 2
            wide = species_column(spread_ref, 1.0, 1024)
            c7, c8 = box[0, :, 7, :], box[0, :, 8, :]
            c23, c24 = box[0, :, 23, :], box[0, :, 24, :]
            low_flux = -jnp.minimum(f[7:8], f[8:9]) * (ADVECT * c7 - wide * (c8 - c7))
            high_flux = jnp.minimum(f[23:24], f[24:25]) * (ADVECT * c23 - wide * (c24 - c23))
            x_parts = pick(jnp.concatenate([low_flux, high_flux], axis=0), sel_x[0])

            lane = iota((1, 1024), 1)
            y_row = lane // 32 == 16 - y_half
            y_roll = jnp.where(y_half == 0, 32, 992)
            z_roll = jnp.where(z_half == 0, 1, 1023)
            middle = f[8:24]
            inner_f = jnp.where(y_row, pltpu.roll(middle, y_roll, 1), pltpu.roll(middle, z_roll, 1))
            weight = -jnp.minimum(middle, inner_f)
            fluxes = []
            for s in range(8):
                c = box[0, s, 8:24, :]
                inner = jnp.where(y_row, pltpu.roll(c, y_roll, 1), pltpu.roll(c, z_roll, 1))
                fluxes.append(spread_ref[s] * weight * (c - inner))
            side_parts = pick(jnp.concatenate(fluxes, axis=0), sel_yz[0])
            register[0, 0:16, :] = x_parts[:, 0:128]
            register[0, 16:32, :] = x_parts[:, 128:256]
            register[0, 32:64, :] = pack_rows(side_parts)


def fine_kernel(
    parents, octants, counts, spread_ref, reaction_ref, box, code, own, own_low, own_high, other, other_low,
    other_high, up_x, up_y, up_z, twice, mean_x, mean_y, mean_z, couple, started, states, payload,
    cells, coef, reacted, rates, ghost, held, chosen, x_faces, first, out, sems,
):
    i = pl.program_id(0)
    column = lax.axis_index("box")

    @pl.when(lax.axis_index("lev") > 0)
    def _():
        slot = i % 2

        @pl.when(i == 0)
        def _():
            high, low = reaction_halves(reaction_ref, 0.5 * COARSE_STEP)
            rates[0] = high
            rates[1] = low

        @pl.when(i >= 2)
        def _():
            pltpu.make_async_copy(out.at[slot], states.at[i - 2], sems.at[slot]).wait()

        used = i < counts[0]

        @pl.when((i == 0) & used)
        def _():
            pltpu.make_async_copy(started.at[i], first.at[slot], sems.at[2 + slot]).start()

        @pl.when(i + 1 < counts[0])
        def _():
            pltpu.make_async_copy(started.at[i + 1], first.at[1 - slot], sems.at[3 - slot]).start()

        @pl.when(jnp.logical_not(used))
        def _():
            out[slot] = box[0]

        @pl.when(used)
        def _():
            home = parents[i] // SLOTS
            away = (home >> 1) - (column >> 1)
            same = ((home - column) & 1) == 0
            for source, is_same, step in (
                (own_low, True, -1), (own, True, 0), (own_high, True, 1),
                (other_low, False, -1), (other, False, 0), (other_high, False, 1),
            ):

                @pl.when((same == is_same) & (away == step))
                def _():
                    chosen[...] = source[0]

            octant = octants[i]
            y_half = octant % 2
            z_half = octant // 2
            spread = [spread_ref[s] * 2.0 for s in range(8)]
            wide = species_column(spread_ref, 2.0, 128)
            f = code[0].astype(F32) / LEVELS

            x_old = jnp.concatenate([chosen[0:24], chosen[24:48]], axis=1)
            x_new = jnp.concatenate([chosen[96:112], chosen[112:128]], axis=1)
            x_mid = 0.5 * (x_old[0:16] + x_new)
            wide_x = pick(jnp.concatenate([x_old, x_mid, jnp.zeros((8, 256), F32)], axis=0), up_x[...])
            side_old = chosen[48:80]
            side_mid = 0.5 * (side_old + chosen[128:160])

            def side_ghosts(side):
                high, low = halves(unpack_rows(side))
                high = dot(twice[...], high).astype(BF16)
                low = dot(twice[...], low).astype(BF16)
                y_ghost = (dot(high, up_y[...]) + dot(low, up_y[...])).reshape(8, 32, 128)
                z_ghost = dot(high, up_z[...]) + dot(low, up_z[...])
                for t in range(8):
                    ghost[:, t] = z_ghost[:, 128 * t : 128 * t + 128].reshape(8, 32, 128)
                return y_ghost

            side_f = jnp.where(iota((16, 128), 1) < 32, chosen[80:96], 0.0)
            high, low = halves(side_f)
            high = dot(twice[0:32, 0:16], high).astype(BF16)
            low = dot(twice[0:32, 0:16], low).astype(BF16)
            fy = dot(high, up_y[...]) + dot(low, up_y[...])
            fz = dot(high, up_z[...]) + dot(low, up_z[...])
            edge = jnp.where(z_half == 1, 0, 31)
            fz = jnp.where(iota((32, 1024), 1) % 32 == edge, fz, 0.0)
            fy_low = jnp.where(y_half == 1, fy, 0.0)
            fy_high = jnp.where(y_half == 0, fy, 0.0)
            short = iota((32, 128), 1)
            y_first = jnp.where(short < 32, jnp.minimum(f[:, 0:128], fy_low), 0.0)
            y_last = jnp.where(short >= 96, jnp.minimum(f[:, 896:1024], fy_high), 0.0)
            f_low = wide_x[16:17]
            f_high = wide_x[17:18]
            prepare(
                f, f_low, f_high, jnp.concatenate([fy_low] * 8, axis=1), jnp.concatenate([fy_high] * 8, axis=1), fz,
                coef, COARSE_STEP,
            )
            m_low = jnp.minimum(f[0:1], f_low)
            m_high = jnp.minimum(f[31:32], f_high)

            inverse = COARSE_STEP / jnp.maximum(f, FLOOR)

            def face_fluxes(low, high, c0, c31, t):
                part = slice(128 * t, 128 * t + 128)
                low_flux = -m_low[:, part] * (ADVECT * low[:, part] - wide * (c0 - low[:, part]))
                high_flux = m_high[:, part] * (ADVECT * c31 - wide * (high[:, part] - c31))
                return low_flux, high_flux

            def store_out(s, t, xt, value):
                out[slot, s, 8 * xt : 8 * xt + 8, pl.ds(pl.multiple_of(128 * t, 128), 128)] = value

            y_ghost = side_ghosts(side_old)
            pltpu.make_async_copy(started.at[i], first.at[slot], sems.at[2 + slot]).wait()

            def open_z(t, carry):
                part = pl.ds(pl.multiple_of(128 * t, 128), 128)
                for xt in range(4):
                    rows = slice(8 * xt, 8 * xt + 8)
                    through_f = coef[9, t, rows, :]
                    scaling = coef[10, t, rows, :]
                    for s in range(8):
                        through = through_f * (ghost[s, t, rows, :] - box[0, s, rows, part])
                        held[s, t, rows, :] = through
                        cells[s, t + 1, 8 + 8 * xt : 16 + 8 * xt, :] = (
                            first[slot, s, rows, part] + spread[s] * (scaling * through)
                        )
                return carry

            lax.fori_loop(0, 8, open_z, 0)
            for t in range(8):
                part = slice(128 * t, 128 * t + 128)
                low_flux, high_flux = face_fluxes(wide_x[0:8], wide_x[8:16], box[0, :, 0, part], box[0, :, 31, part], t)
                x_faces[0:8, part] = low_flux
                x_faces[8:16, part] = high_flux
                cells[:, t + 1, 8, :] += -inverse[0:1, part] * low_flux
                cells[:, t + 1, 39, :] += -inverse[31:32, part] * high_flux
                cells[:, t + 1, 7, :] = wide_x[24:32, part]
                cells[:, t + 1, 40, :] = wide_x[32:40, part]
            y_low_flux = y_first * (y_ghost - box[0, :, :, 0:128])
            y_high_flux = y_last * (y_ghost - box[0, :, :, 896:1024])
            y_flux = y_low_flux + y_high_flux
            for s in range(8):
                cells[s, 1, 8:40, :] += spread[s] * (inverse[:, 0:128] * y_low_flux[s])
                cells[s, 8, 8:40, :] += spread[s] * (inverse[:, 896:1024] * y_high_flux[s])

            y_ghost = side_ghosts(side_mid)
            cells[:, 0, 8:40, :] = y_ghost
            cells[:, 9, 8:40, :] = y_ghost
            for t in range(8):
                part = slice(128 * t, 128 * t + 128)
                low_flux, high_flux = face_fluxes(wide_x[24:32], wide_x[32:40], cells[:, t + 1, 8, :], cells[:, t + 1, 39, :], t)
                x_faces[0:8, part] += low_flux
                x_faces[8:16, part] += high_flux
            y_flux = y_flux + y_first * (y_ghost - cells[:, 1, 8:40, :]) + y_last * (y_ghost - cells[:, 8, 8:40, :])
            react(cells, reacted, rates[0], rates[1])
            advance(cells, coef, reacted, spread, store_out, ghost, held, False)

            pooled = pick(out[slot].reshape(256, 1024), mean_x[...])
            averaged = 0.5 * left_pick(couple[...], pooled)
            for q in range(3):
                payload[q, 0] = averaged[40 * q : 40 * q + 40]
            payload[3, 0, 0:8] = averaged[120:128]
            payload[3, 0, 8:24] = 0.5 * pick(x_faces[...], mean_x[...])
            sides = pick(y_flux.reshape(256, 128), mean_y[...])
            for n in range(4):
                part = jnp.concatenate([held[:, 2 * n + h].reshape(256, 128) for h in range(2)], axis=1)
                sides = sides + pick(part, mean_z[256 * n : 256 * n + 256, :])
            sides = left_pick(couple[...], sides).reshape(8, 16, 128)
            sides = jnp.concatenate([(-0.5 * spread[s]) * sides[s] for s in range(8)], axis=0)
            sides = pack_rows(sides)
            payload[3, 0, 24:40, 0:128] = sides[0:16]
            payload[3, 0, 24:40, 128:256] = sides[16:32]

        pltpu.make_async_copy(out.at[slot], states.at[i], sems.at[slot]).start()

        @pl.when(i == SLOTS - 1)
        def _():
            pltpu.make_async_copy(out.at[1 - slot], states.at[i - 1], sems.at[1 - slot]).wait()
            pltpu.make_async_copy(out.at[slot], states.at[i], sems.at[slot]).wait()


def decode(code):
    safe = jnp.maximum(code, 0)
    return safe // (OFFSETS * SLOTS) + 1, safe // SLOTS % OFFSETS - REACH, safe % SLOTS


def route_kernel(low, own, high, mine, others, to_low, stay, to_high, codes, sems):
    column = lax.axis_index("box")
    lists = [
        pltpu.make_async_copy(source.at[0, 16:24], codes.at[n], sems.at[n]) for n, source in enumerate((low, own, high))
    ]
    for copy in lists:
        copy.start()
    for copy in lists:
        copy.wait()

    def each(act):
        for n, (step, target) in enumerate(((-1, to_low), (0, stay), (1, to_high))):
            for j in range(SLOTS):
                code = codes[n, 7, j].astype(jnp.int32)
                row, offset, slot = decode(code)
                child = column + 2 * step + offset
                there = (code >= 0) & ((child >> 1) == (column >> 1))
                for parity, source in enumerate((mine, others)):

                    @pl.when(there & (((child - column) & 1) == parity))
                    def _():
                        act(pltpu.make_async_copy(source.at[row, slot], target.at[j], sems.at[n * SLOTS + j]))

    each(lambda copy: copy.start())
    each(lambda copy: copy.wait())


def choose_kernel(codes, from_low, stay, from_high, chosen):
    column = lax.axis_index("box")
    for j in range(SLOTS):
        _, offset, _ = decode(codes[j])
        away = ((column + offset) >> 1) - (column >> 1)
        chosen[j] = jnp.where(away < 0, from_low[j], jnp.where(away == 0, stay[j], from_high[j]))


def finish_kernel(
    octants, codes, spread_ref, updated, message, register, code_words, halo, other_low, other, other_high,
    part0, part1, part2, part3, sel_x, sel_yz, states, chosen,
):
    i = pl.program_id(0)
    column = lax.axis_index("box")
    states[...] = updated[...]

    @pl.when(lax.axis_index("lev") == 0)
    def _():
        wide = species_column(spread_ref, 1.0, 128)
        odd = (column & 1) == 1

        def end_plane(x, p, neighbour_p, neighbour):
            f = code_words[0, x : x + 1, :].astype(F32) / LEVELS
            scaling = COARSE_STEP / jnp.maximum(f, FLOOR)
            for t in range(8):
                part = slice(128 * t, 128 * t + 128)
                base = 32 + (p * 8 + t) * 16
                there = 32 + (neighbour_p * 8 + t) * 16
                c = halo[base : base + 8, :]
                g = neighbour(there, there + 8)
                m = jnp.minimum(f[:, part], neighbour(there + 8, there + 9))
                if p == 0:
                    gain = m * (ADVECT * g - wide * (c - g))
                else:
                    gain = -m * (ADVECT * c - wide * (g - c))
                states[0, :, x, part] += scaling[:, part] * gain

        @pl.when(i == 0)
        def _():
            end_plane(0, 0, 1, lambda a, b: jnp.where(odd, other[a:b, :], other_low[a:b, :]))

        @pl.when(i == SLOTS - 1)
        def _():
            end_plane(31, 1, 0, lambda a, b: jnp.where(odd, other_high[a:b, :], other[a:b, :]))

        child = codes[i]

        @pl.when(child >= 0)
        def _():
            for q, part in enumerate((part0, part1, part2, part3)):
                chosen[40 * q : 40 * q + 40, :] = part[0]
            octant = octants[i]
            y_half = octant % 2
            z_half = octant // 2
            lane = iota((1, 1024), 1)
            inside = (lane // 512 == y_half) & (lane % 32 // 16 == z_half)
            own_f = jnp.concatenate([message[0, 0:24, :], message[0, 24:48, :]], axis=1)
            half = iota((16, 256), 0) < 8
            x_f = jnp.where(half, own_f[16:17], own_f[17:18])
            reg_x = jnp.concatenate([register[0, 0:16, :], register[0, 16:32, :]], axis=1)
            fix_x = COARSE_STEP / jnp.maximum(x_f, FLOOR) * (chosen[128:144, :] - reg_x)
            side_f = jnp.concatenate([message[0, 80:96, :]] * 2, axis=0)
            sides = jnp.concatenate([chosen[144:160, 0:128], chosen[144:160, 128:256]], axis=0)
            fix_sides = COARSE_STEP / jnp.maximum(side_f, FLOOR) * (sides - register[0, 32:64, :])
            planes = pick(fix_x, sel_x[0])
            states[0, :, 7, :] += planes[0:8]
            states[0, :, 24, :] += planes[8:16]
            filled = pick(chosen[0:128, :], sel_x[0])
            added = pick(unpack_rows(fix_sides), sel_yz[0])
            for s in range(8):
                part = slice(16 * s, 16 * s + 16)
                here = states[0, s, 8:24, :]
                states[0, s, 8:24, :] = jnp.where(inside, filled[part], here + added[part])


def shifted(block, axis, distance):
    devices = range(lax.axis_size(axis))
    return lax.ppermute(block, axis, [(i - distance, i) for i in devices if i - distance in devices])


def per_device(
    box_states, cell_code, diffusivity, reaction, coarse_child, coarse_octant, fine_parent, fine_octant, fine_count
):
    row = lax.axis_index("lev")
    count = lax.axis_size("box")
    swap = [(i, i ^ 1) for i in range(count)]
    vmem = pltpu.CompilerParams(vmem_limit_bytes=62 * 1024 * 1024)

    def whole(a):
        zeros = (0,) * a.ndim
        return pl.BlockSpec(a.shape, lambda i, *_: zeros)

    def each(shape):
        tail = (0,) * len(shape)
        return pl.BlockSpec((1,) + shape, lambda i, *_: (i,) + tail)

    smem = pl.BlockSpec(memory_space=pltpu.SMEM)
    hbm = pl.BlockSpec(memory_space=pl.ANY)
    previous = lambda i: jnp.maximum(i - 1, 0)
    following = lambda i: jnp.minimum(i + 1, SLOTS - 1)
    shape = jax.ShapeDtypeStruct
    sel_x, sel_yz = table(SEL_X), table(SEL_YZ)
    by_octant = lambda i, octants, *_: (octants[i], 0, 0)

    message, halo = pl.pallas_call(
        message_kernel,
        grid_spec=pltpu.PrefetchScalarGridSpec(
            num_scalar_prefetch=2,
            grid=(SLOTS,),
            in_specs=[
                smem,
                whole(reaction),
                each((8, 32, 1024)),
                each((32, 1024)),
                pl.BlockSpec((1, 1024, 256), by_octant),
                pl.BlockSpec((1, 1024, 128), lambda i, octants, *_: (octants[i] // 2, 0, 0)),
                pl.BlockSpec((1, 256, 128), by_octant),
            ],
            out_specs=[each((160, 128)), pl.BlockSpec((640, 128), lambda i, *_: (0, 0))],
            scratch_shapes=[pltpu.VMEM((2, 256, 256), BF16)],
        ),
        out_shape=[shape((SLOTS, 160, 128), F32), shape((640, 128), F32)],
        compiler_params=vmem,
        name="shells",
    )(
        coarse_octant, coarse_child, diffusivity, reaction, box_states, cell_code, sel_x, table(WINDOW_Z), table(CENTER)
    )

    updated, register = pl.pallas_call(
        first_kernel,
        grid_spec=pltpu.PrefetchScalarGridSpec(
            num_scalar_prefetch=2,
            grid=(SLOTS,),
            in_specs=[
                smem,
                whole(reaction),
                each((8, 32, 1024)),
                each((32, 1024)),
                pl.BlockSpec((1, 8, 8, 1024), lambda i, *_: (previous(i), 0, 3, 0)),
                pl.BlockSpec((1, 8, 1024), lambda i, *_: (previous(i), 3, 0)),
                pl.BlockSpec((1, 8, 8, 1024), lambda i, *_: (following(i), 0, 0, 0)),
                pl.BlockSpec((1, 8, 1024), lambda i, *_: (following(i), 0, 0)),
                pl.BlockSpec((1, 1024, 256), by_octant),
                pl.BlockSpec((1, 1024, 128), by_octant),
            ],
            out_specs=[each((8, 32, 1024)), each((64, 128))],
            scratch_shapes=[
                pltpu.VMEM((8, 10, 48, 128), F32),
                pltpu.VMEM((9, 8, 32, 128), F32),
                pltpu.VMEM((8, 8, 32, 128), F32),
                pltpu.VMEM((2, 256, 256), BF16),
            ],
        ),
        out_shape=[shape((SLOTS, 8, 32, 1024), F32), shape((SLOTS, 64, 128), F32)],
        compiler_params=vmem,
        cost_estimate=pl.CostEstimate(flops=10**9, bytes_accessed=40 * 10**6, transcendentals=0),
        name="first_step",
    )(
        coarse_octant, fine_count, diffusivity, reaction, box_states, cell_code, box_states, cell_code,
        box_states, cell_code, sel_x, sel_yz,
    )

    spread_out = [lax.ppermute(message, "lev", [(0, r)]) for r in (1, 3, 2)]
    *spread_out, updated = lax.optimization_barrier((*spread_out, updated))
    own = jnp.where(row == 0, halo.reshape(SLOTS, 160, 128), spread_out[0] + spread_out[1] + spread_out[2])
    own_low = shifted(own, "box", 2)
    own_high = shifted(own, "box", -2)
    other = lax.ppermute(own, "box", swap)
    other_low = lax.ppermute(own_low, "box", swap)
    other_high = lax.ppermute(own_high, "box", swap)

    def near(i, parents, *_):
        return (jnp.maximum(parents[i], 0) % SLOTS, 0, 0)

    up_x, up_y, up_z, twice = table(UP_X), table(UP_Y), table(UP_Z), table(TWICE)
    mean_x, mean_y, mean_z = table(0.25 * UP_X.T), table(0.25 * UP_Y.T), table(0.25 * UP_Z.T)
    couple = table(TWICE.T)
    constants = [up_x, up_y, up_z, twice, mean_x, mean_y, mean_z, couple]
    states, payload = pl.pallas_call(
        fine_kernel,
        grid_spec=pltpu.PrefetchScalarGridSpec(
            num_scalar_prefetch=3,
            grid=(SLOTS,),
            in_specs=[smem, whole(reaction), each((8, 32, 1024)), each((32, 1024))]
            + [pl.BlockSpec((1, 160, 128), near)] * 6
            + [whole(a) for a in constants]
            + [hbm],
            out_specs=[hbm, pl.BlockSpec((4, 1, 40, 256), lambda i, *_: (0, i, 0, 0))],
            scratch_shapes=[
                pltpu.VMEM((8, 10, 48, 128), F32),
                pltpu.VMEM((11, 8, 32, 128), F32),
                pltpu.VMEM((8, 8, 32, 128), F32),
                pltpu.VMEM((2, 256, 256), BF16),
                pltpu.VMEM((8, 8, 32, 128), F32),
                pltpu.VMEM((8, 8, 32, 128), F32),
                pltpu.VMEM((160, 128), F32),
                pltpu.VMEM((16, 1024), F32),
                pltpu.VMEM((2, 8, 32, 1024), F32),
                pltpu.VMEM((2, 8, 32, 1024), F32),
                pltpu.SemaphoreType.DMA((4,)),
            ],
        ),
        out_shape=[shape((SLOTS, 8, 32, 1024), F32), shape((4, SLOTS, 40, 256), F32)],
        input_output_aliases={3 + 4 + 6 + len(constants): 0},
        compiler_params=vmem,
        name="fine_steps",
    )(
        fine_parent, fine_octant, fine_count, diffusivity, reaction, box_states, cell_code, own, own_low,
        own_high, other, other_low, other_high, *constants, updated,
    )

    mine = lax.all_to_all(payload, "lev", 0, 0)
    others = lax.ppermute(mine, "box", swap)
    bundle = shape((SLOTS, 40, 256), F32)
    in_vmem = pl.BlockSpec(memory_space=pltpu.VMEM)
    to_low, stay, to_high = pl.pallas_call(
        route_kernel,
        in_specs=[hbm] * 5,
        out_specs=[in_vmem] * 3,
        scratch_shapes=[pltpu.SMEM((3, 8, 128), F32), pltpu.SemaphoreType.DMA((3 * SLOTS,))],
        out_shape=[bundle] * 3,
        compiler_params=vmem,
        name="route",
    )(own_low, own, own_high, mine, others)
    from_high = shifted(to_low, "box", -2)
    from_low = shifted(to_high, "box", 2)
    quarter = pl.pallas_call(
        choose_kernel,
        in_specs=[smem] + [in_vmem] * 3,
        out_specs=in_vmem,
        out_shape=bundle,
        compiler_params=vmem,
        name="choose",
    )(coarse_child, from_low, stay, from_high)
    quarters = [quarter] + [lax.ppermute(quarter, "lev", [(q, 0)]) for q in range(1, 4)]

    back_x, back_yz = table(SEL_X.transpose(0, 2, 1)), table(SEL_YZ.transpose(0, 2, 1))
    flat = [a.reshape(640, 128) for a in (other_low, other, other_high)]
    return pl.pallas_call(
        finish_kernel,
        grid_spec=pltpu.PrefetchScalarGridSpec(
            num_scalar_prefetch=2,
            grid=(SLOTS,),
            in_specs=[smem, each((8, 32, 1024)), each((160, 128)), each((64, 128)), each((32, 1024))]
            + [whole(halo)] * 4
            + [each((40, 256))] * 4
            + [pl.BlockSpec((1, 256, 1024), by_octant), pl.BlockSpec((1, 128, 1024), by_octant)],
            out_specs=each((8, 32, 1024)),
            scratch_shapes=[pltpu.VMEM((160, 256), F32)],
        ),
        out_shape=shape((SLOTS, 8, 32, 1024), F32),
        input_output_aliases={3: 0},
        compiler_params=vmem,
        name="finish",
    )(
        coarse_octant, coarse_child, diffusivity, states, message, register, cell_code, halo, *flat,
        *quarters, back_x, back_yz,
    )


def solution(mesh):
    return jax.shard_map(
        per_device,
        mesh=mesh,
        in_specs=(
            P(("lev", "box"), None, None, None),
            P(("lev", "box"), None, None),
            P(),
            P(),
            P("box"),
            P("box"),
            P(("lev", "box")),
            P(("lev", "box")),
            P(("lev", "box")),
        ),
        out_specs=P(("lev", "box"), None, None, None),
        check_vma=False,
    )
```

```python
import functools

import jax
import jax.numpy as jnp
import numpy as np
from jax import lax
from jax.experimental import pallas as pl
from jax.experimental.pallas import tpu as pltpu
from jax.sharding import PartitionSpec as P

ADVECT = 0.4
COARSE_STEP = 0.5
FLOOR = 0.5
LEVELS = 15.0
SLOTS = 4
REACH = 2
OFFSETS = 2 * REACH + 1
F32 = jnp.float32
BF16 = jnp.bfloat16


def selection_tables():
    lane = np.arange(1024)
    y, z = lane // 32, lane % 32
    place = np.arange(256)
    a, b = place // 16, place % 16
    i = np.arange(16)
    sel_x = np.zeros((4, 1024, 256), np.float32)
    sel_yz = np.zeros((4, 1024, 128), np.float32)
    for octant in range(4):
        y_half, z_half = octant % 2, octant // 2
        sel_x[octant, (16 * y_half + a) * 32 + 16 * z_half + b, place] = 1
        for g in range(4):
            sel_yz[octant, (16 - y_half) * 32 + 16 * z_half + i, 32 * g + i] = 1
            sel_yz[octant, (16 * y_half + i) * 32 + 16 - z_half, 32 * g + 16 + i] = 1
    up_x = np.zeros((256, 1024), np.float32)
    up_x[(y // 2) * 16 + z // 2, lane] = 1
    twice = np.zeros((256, 128), np.float32)
    rows = np.arange(256)
    twice[rows, rows // 32 * 16 + rows % 32 // 2] = 1
    window_z = np.zeros((2, 1024, 128), np.float32)
    for z_half in range(2):
        for step in range(3):
            rows = np.arange(32)
            window_z[z_half, rows * 32 + 15 - z_half + step, step * 32 + rows] = 1
    center = np.zeros((4, 256, 128), np.float32)
    for octant in range(4):
        for g in range(4):
            center[octant, 32 + 16 * (octant // 2) + i, 32 * g + i] = 1
            center[octant, 160 + 16 * (octant % 2) + i, 32 * g + 16 + i] = 1
    layers = np.zeros((4, 128, 1024), np.float32)
    line = np.arange(32)
    for octant in range(4):
        y_face, y_next = (0, 1) if octant % 2 else (31, 30)
        z_face, z_next = (0, 1) if octant // 2 else (31, 30)
        layers[octant, line, y_face * 32 + line] = 1
        layers[octant, 32 + line, y_next * 32 + line] = 1
        layers[octant, 64 + line, line * 32 + z_face] = 1
        layers[octant, 96 + line, line * 32 + z_next] = 1
    up_layer = np.zeros((128, 128), np.float32)
    for g in range(4):
        up_layer[32 * g + line // 2, line] = 1
        up_layer[32 * g + 16 + line // 2, 64 + line] = 1
    return sel_x, sel_yz, up_x, twice, window_z, center, layers, up_layer


SEL_X, SEL_YZ, UP_X, TWICE, WINDOW_Z, CENTER, LAYERS, UP_LAYER = selection_tables()


def table(values):
    return jnp.asarray(values.astype(jnp.bfloat16))


def halves(a):
    high = a.astype(BF16)
    return high, (a - high.astype(F32)).astype(BF16)


def dot(a, b):
    return jnp.dot(a, b, preferred_element_type=F32)


def pick(a, w):
    high, low = halves(a)
    return dot(high, w) + dot(low, w)


def left_pick(w, a):
    high, low = halves(a)
    return dot(w, high) + dot(w, low)


def iota(shape, dim):
    return lax.broadcasted_iota(jnp.int32, shape, dim)


def pack_rows(rows):
    group = iota((32, 128), 1) // 32
    out = rows[0:32]
    for g in range(1, 4):
        out = jnp.where(group == g, rows[32 * g : 32 * g + 32], out)
    return out


def unpack_rows(packed):
    group = iota((32, 128), 1) // 32
    return jnp.concatenate([jnp.where(group == g, packed, 0.0) for g in range(4)], axis=0)


def species_column(values_ref, factor, width):
    row = iota((8, width), 0)
    out = jnp.zeros((8, width), F32)
    for s in range(8):
        out = jnp.where(row == s, values_ref[s] * factor, out)
    return out


def set_rates(rates, reaction_ref, step):
    column = iota((1, 256), 1)
    for s in range(8):
        line = jnp.zeros((1, 256), F32)
        for t in range(8):
            line = jnp.where(column // 32 == t, reaction_ref[s, t] * step, line)
        high, low = halves(jnp.where(iota((32, 256), 0) == iota((32, 256), 1) % 32, line, 0.0))
        rates[0, 32 * s : 32 * s + 32] = high
        rates[1, 32 * s : 32 * s + 32] = low


def load_cells(cells, amounts):
    for t in range(8):
        cells[:, t + 1, 8:40, :] = amounts[:, :, 128 * t : 128 * t + 128]


def prepare(f, f_low, f_high, coef, scale):
    lane = iota((32, 1024), 1)
    row = iota((32, 1024), 0)
    depth = lane % 32
    scaling = scale / jnp.maximum(f, FLOOR)
    x_low = scaling * jnp.minimum(f, jnp.where(row == 0, f_low, pltpu.roll(f, 1, 0)))
    x_high = scaling * jnp.minimum(f, jnp.where(row == 31, f_high, pltpu.roll(f, 31, 0)))
    y_low = scaling * jnp.where(lane < 32, 0.0, jnp.minimum(f, pltpu.roll(f, 32, 1)))
    y_high = scaling * jnp.where(lane >= 992, 0.0, jnp.minimum(f, pltpu.roll(f, 992, 1)))
    z_low = scaling * jnp.where(depth == 0, 0.0, jnp.minimum(f, pltpu.roll(f, 1, 1)))
    z_high = scaling * jnp.where(depth == 31, 0.0, jnp.minimum(f, pltpu.roll(f, 1023, 1)))
    everything = x_low + x_high + y_low + y_high + z_low + z_high
    kinds = [x_low, x_high, y_low, y_high, z_low, z_high, everything, 1.0 - ADVECT * x_high, ADVECT * x_low]
    for k, kind in enumerate(kinds):
        for t in range(8):
            coef[k, t] = kind[:, 128 * t : 128 * t + 128]


def advance(cells, coef, reacted, rates, spread, store):
    lane = iota((8, 128), 1)

    def react(n, to):
        block = jnp.concatenate([cells[:, 2 * n + 1 + h, 8:40, :].reshape(256, 128) for h in range(2)], axis=1)
        high, low = halves(block)
        out = dot(rates[0], high) + dot(rates[1], high) + dot(rates[0], low)
        for h in range(2):
            to[:, h] = out[:, 128 * h : 128 * h + 128].reshape(8, 32, 128)

    def add(t, term):
        for xt in range(4):
            kinds = [coef[k, t, 8 * xt : 8 * xt + 8, :] for k in range(9)]
            x_low, x_high, y_low, y_high, z_low, z_high, everything, own, upwind = kinds
            at = 8 + 8 * xt
            for s in range(8):
                c = cells[s, t + 1, at : at + 8, :]
                below = cells[s, t + 1, at - 1 : at + 7, :]
                above = cells[s, t + 1, at + 1 : at + 9, :]
                left = pltpu.roll(jnp.where(lane >= 96, cells[s, t, at : at + 8, :], c), 32, 1)
                right = pltpu.roll(jnp.where(lane < 32, cells[s, t + 2, at : at + 8, :], c), 96, 1)
                change = x_low * below + x_high * above + y_low * left + y_high * right
                change = change + z_low * pltpu.roll(c, 1, 1) + z_high * pltpu.roll(c, 127, 1)
                change = change - everything * c
                result = own * c + upwind * below + spread[s] * change
                store(s, t, xt, result + term[s, 8 * xt : 8 * xt + 8, :])

    now, later = reacted
    react(0, now)

    def pair(m, carry):
        react(2 * m + 1, later)
        for h in range(2):
            add(4 * m + h, now.at[:, h])
        react(jnp.minimum(2 * m + 2, 3), now)
        for h in range(2):
            add(4 * m + 2 + h, later.at[:, h])
        return carry

    lax.fori_loop(0, 2, pair, 0)


def clear_rim(cells):
    cells[:, 0] = jnp.zeros((8, 48, 128), F32)
    cells[:, 9] = jnp.zeros((8, 48, 128), F32)
    cells[:, :, 0:8, :] = jnp.zeros((8, 10, 8, 128), F32)
    cells[:, :, 40:48, :] = jnp.zeros((8, 10, 8, 128), F32)


def message_kernel(
    octants, codes, spread_ref, reaction_smem, reaction_ref, boxes, words, sel_x_all, window_z_all, center_all, message,
    halo, rates, box_ref, code_ref, sel_x_ref, window_z_ref, center_ref, sems,
):
    def copies(i):
        octant = octants[i]
        pairs = (
            (boxes.at[i], box_ref.at[i]), (words.at[i], code_ref.at[i]), (window_z_all.at[octant // 2], window_z_ref.at[i]),
            (sel_x_all.at[octant], sel_x_ref.at[i]), (center_all.at[octant], center_ref.at[i]),
        )
        return [pltpu.make_async_copy(source, target, sems.at[i, n]) for n, (source, target) in enumerate(pairs)]

    def one_message(i, listed):
        y_half = octants[i] % 2
        box = box_ref.at[pl.ds(i, 1)]
        f = code_ref[i].astype(F32) / LEVELS
        lane = iota((32, 128), 1)
        place = lane % 32
        turn = 32 * (1 + y_half)
        spread = [spread_ref[s] for s in range(8)]

        def window_y(a, b):
            return jnp.where(iota(a.shape, 1) < turn, pltpu.roll(a, turn, 1), pltpu.roll(b, turn, 1))

        around_y = window_y(
            box[0, :, :, 384:512].reshape(256, 128), box[0, :, :, 512:640].reshape(256, 128)
        )
        around_z = pick(box[0].reshape(256, 1024), window_z_ref[i])
        f_windows = (window_y(f[:, 384:512], f[:, 512:640]), pick(f, window_z_ref[i]))
        both = jnp.concatenate([around_y, around_z], axis=1)
        high, low = halves(both)
        reacted = dot(rates[0], high) + dot(rates[1], high) + dot(rates[0], low)
        old_rows, new_rows = [[], []], [[], []]
        for w, (around, fw) in enumerate(zip((around_y, around_z), f_windows)):
            inner = fw[8:24]
            scaling = COARSE_STEP / jnp.maximum(inner, FLOOR)
            x_low = scaling * jnp.minimum(inner, pltpu.roll(fw, 1, 0)[8:24])
            x_high = scaling * jnp.minimum(inner, pltpu.roll(fw, 31, 0)[8:24])
            low_side = scaling * jnp.minimum(inner, pltpu.roll(inner, 32, 1))
            high_side = scaling * jnp.minimum(inner, pltpu.roll(inner, 96, 1))
            before = scaling * jnp.where(place[8:24] == 0, 0.0, jnp.minimum(inner, pltpu.roll(inner, 1, 1)))
            after = scaling * jnp.where(place[8:24] == 31, 0.0, jnp.minimum(inner, pltpu.roll(inner, 127, 1)))
            everything = x_low + x_high + low_side + high_side + before + after
            own = 1.0 - ADVECT * x_high
            upwind = ADVECT * x_low
            for s in range(8):
                rows = around[32 * s : 32 * s + 32]
                c = rows[8:24]
                below = pltpu.roll(rows, 1, 0)[8:24]
                above = pltpu.roll(rows, 31, 0)[8:24]
                change = x_low * below + x_high * above
                change = change + low_side * pltpu.roll(c, 32, 1) + high_side * pltpu.roll(c, 96, 1)
                change = change + before * pltpu.roll(c, 1, 1) + after * pltpu.roll(c, 127, 1) - everything * c
                term = reacted[32 * s + 8 : 32 * s + 24, 128 * w : 128 * w + 128]
                old_rows[w].append(c)
                new_rows[w].append(own * c + upwind * below + spread[s] * change + term)
        fractions = jnp.concatenate([fw[8:24] for fw in f_windows], axis=1)
        sides = [
            jnp.concatenate([jnp.concatenate(part[0], axis=0), jnp.concatenate(part[1], axis=0)], axis=1)
            for part in (old_rows, new_rows)
        ]
        side_parts = pick(jnp.concatenate(sides + [fractions], axis=0), center_ref[i])

        wide = species_column(spread_ref, 1.0, 1024)
        long = iota((1, 1024), 1)
        planes = [box[0, :, x, :] for x in (7, 24)]
        mixed = jnp.dot(
            reaction_ref[...], jnp.concatenate(planes, axis=1), precision=lax.Precision.HIGHEST,
            preferred_element_type=F32,
        )
        new_planes = []
        for n, x in enumerate((7, 24)):
            fx = f[x : x + 1]
            scaling = COARSE_STEP / jnp.maximum(fx, FLOOR)
            x_low = scaling * jnp.minimum(fx, f[x - 1 : x])
            x_high = scaling * jnp.minimum(fx, f[x + 1 : x + 2])
            shifts = ((32, long < 32), (992, long >= 992), (1, long % 32 == 0), (1023, long % 32 == 31))
            c = planes[n]
            below = box[0, :, x - 1, :]
            change = x_low * below + x_high * box[0, :, x + 1, :]
            everything = x_low + x_high
            for amount, wall in shifts:
                factor = scaling * jnp.where(wall, 0.0, jnp.minimum(fx, pltpu.roll(fx, amount, 1)))
                change = change + factor * pltpu.roll(c, amount, 1)
                everything = everything + factor
            change = change - everything * c
            moved = (1.0 - ADVECT * x_high) * c + ADVECT * x_low * below + wide * change
            new_planes.append(moved + COARSE_STEP * mixed[:, 1024 * n : 1024 * n + 1024])
        sublane = iota((8, 1024), 0)
        faces = jnp.where(sublane == 0, f[7:8], jnp.where(sublane == 1, f[24:25], 0.0))
        blank = jnp.zeros((8, 1024), F32)
        x_parts = pick(jnp.concatenate(planes + [faces] + new_planes + [blank], axis=0), sel_x_ref[i])

        message[i, 0:16, :] = x_parts[0:16, 0:128]
        message[i, 16:24, :] = jnp.where(iota((8, 128), 0) == 7, listed, x_parts[16:24, 0:128])
        message[i, 24:48, :] = x_parts[0:24, 128:256]
        message[i, 48:80, :] = pack_rows(side_parts[0:128])
        message[i, 80:96, :] = side_parts[256:272]
        message[i, 96:112, :] = x_parts[24:40, 0:128]
        message[i, 112:128, :] = x_parts[24:40, 128:256]
        message[i, 128:160, :] = pack_rows(side_parts[128:256])

        def put_plane(p, x):
            plane = box[0, :, x, :]
            for t in range(8):
                base = 32 + (p * 8 + t) * 16
                halo[base : base + 8, :] = plane[:, 128 * t : 128 * t + 128]
                halo[base + 8 : base + 16, :] = jnp.broadcast_to(f[x : x + 1, 128 * t : 128 * t + 128], (8, 128))

        @pl.when(i == 0)
        def _():
            put_plane(0, 0)

        @pl.when(i == SLOTS - 1)
        def _():
            put_plane(1, 31)

    @pl.when(lax.axis_index("lev") == 0)
    def _():
        for i in range(SLOTS):
            for copy in copies(i):
                copy.start()
        set_rates(rates, reaction_smem, COARSE_STEP)
        where = iota((8, 128), 1)
        listed = jnp.zeros((8, 128), F32)
        for j in range(SLOTS):
            listed = jnp.where(where == j, codes[j].astype(F32), listed)
        halo[...] = jnp.zeros((640, 128), F32)
        halo[16:24, :] = listed

        def each(i, carry):
            for copy in copies(i):
                copy.wait()
            one_message(i, listed)
            return carry

        lax.fori_loop(0, SLOTS, each, 0)


def early_kernel(
    base, again, octants, fine_octants, counts, spread_ref, reaction_smem, box, code, before, code_before, after,
    code_after, sel_x, sel_yz, layers, mean_x, couple, *refs,
):
    states, register, edges, ends, average, cells, later, coef, now, then, rates = refs[5 * again :]
    i = pl.program_id(0)
    at = base + i
    coarse = lax.axis_index("lev") == 0
    used = coarse | (at < counts[0])

    @pl.when(jnp.logical_not(used))
    def _():
        states[0] = box[0]

    @pl.when(used)
    def _():
        @pl.when(i == 0)
        def _():
            set_rates(rates, reaction_smem, jnp.where(coarse, COARSE_STEP, 0.5 * COARSE_STEP))
            clear_rim(cells)
            clear_rim(later)

        f = code[0].astype(F32) / LEVELS
        f_before = jnp.where(coarse & (at > 0), code_before[0, 7:8, :].astype(F32) / LEVELS, 0.0)
        f_after = jnp.where(coarse & (at < SLOTS - 1), code_after[0, 0:1, :].astype(F32) / LEVELS, 0.0)
        load_cells(cells, box[0])
        for t in range(8):
            cells[:, t + 1, 7, :] = before[0, :, 7, 128 * t : 128 * t + 128]
            cells[:, t + 1, 40, :] = after[0, :, 0, 128 * t : 128 * t + 128]
        prepare(f, f_before, f_after, coef, COARSE_STEP)

        def store(s, t, xt, value):
            states[0, s, 8 * xt : 8 * xt + 8, pl.ds(pl.multiple_of(128 * t, 128), 128)] = value

        def store_later(s, t, xt, value):
            later[s, t + 1, 8 + 8 * xt : 16 + 8 * xt, :] = value

        @pl.when(coarse)
        def _():
            spread = [spread_ref[s] for s in range(8)]
            advance(cells, coef, (now, then), rates, spread, store)
            octant = octants[at]
            y_half = octant % 2
            z_half = octant // 2
            wide = species_column(spread_ref, 1.0, 1024)
            c7, c8 = box[0, :, 7, :], box[0, :, 8, :]
            c23, c24 = box[0, :, 23, :], box[0, :, 24, :]
            low_flux = -jnp.minimum(f[7:8], f[8:9]) * (ADVECT * c7 - wide * (c8 - c7))
            high_flux = jnp.minimum(f[23:24], f[24:25]) * (ADVECT * c23 - wide * (c24 - c23))
            x_parts = pick(jnp.concatenate([low_flux, high_flux], axis=0), sel_x[0])

            lane = iota((1, 1024), 1)
            y_row = lane // 32 == 16 - y_half
            y_roll = jnp.where(y_half == 0, 32, 992)
            z_roll = jnp.where(z_half == 0, 1, 1023)
            middle = f[8:24]
            inner_f = jnp.where(y_row, pltpu.roll(middle, y_roll, 1), pltpu.roll(middle, z_roll, 1))
            weight = -jnp.minimum(middle, inner_f)
            fluxes = []
            for s in range(8):
                c = box[0, s, 8:24, :]
                inner = jnp.where(y_row, pltpu.roll(c, y_roll, 1), pltpu.roll(c, z_roll, 1))
                fluxes.append(spread[s] * weight * (c - inner))
            side_parts = pick(jnp.concatenate(fluxes, axis=0), sel_yz[0])
            register[0, 0:16, :] = x_parts[:, 0:128]
            register[0, 16:32, :] = x_parts[:, 128:256]
            register[0, 32:64, :] = pack_rows(side_parts)

        @pl.when(jnp.logical_not(coarse))
        def _():
            spread = [spread_ref[s] * 2.0 for s in range(8)]
            advance(cells, coef, (now, then), rates, spread, store_later)
            advance(later, coef, (now, then), rates, spread, store)
            edges[0, 0:256] = pick(box[0].reshape(256, 1024), layers[0])
            middle = jnp.concatenate([later[:, t + 1, 8:40, :].reshape(256, 128) for t in range(8)], axis=1)
            edges[0, 256:512] = pick(middle, layers[0])
            edges[0, 512:544] = pick(f, layers[0])
            ends[0, 0:8] = box[0, :, 0, :]
            ends[0, 8:16] = box[0, :, 31, :]
            for t in range(8):
                ends[0, 16:24, 128 * t : 128 * t + 128] = later[:, t + 1, 8, :]
                ends[0, 24:32, 128 * t : 128 * t + 128] = later[:, t + 1, 39, :]
            average[0] = 0.5 * left_pick(couple[...], pick(states[0].reshape(256, 1024), mean_x[...]))


def interface_kernel(
    parents, octants, counts, spread_ref, reaction_smem, reaction_ref, words, edges_all, ends_all, average_all, up_x_all,
    up_layer_all, twice_all, mean_x_all, mean_layer_all, couple_all, layers_all, layers_t_all, mean_layers_all,
    own, own_low, own_high, other, other_low, other_high, started, states, payload, codes, rates, messages, taken, coarse,
    first, code, edges, ends, average, up_x, up_layer, twice, mean_x, mean_layer, couple, layers, layers_t, mean_layers,
    sems, fixed_sems,
):
    column = lax.axis_index("box")
    lists = [
        pltpu.make_async_copy(source.at[0, 16:24], codes.at[n], fixed_sems.at[n])
        for n, source in enumerate((own_low, own, own_high))
    ]
    fixed = [
        pltpu.make_async_copy(source, target, fixed_sems.at[3 + n])
        for n, (source, target) in enumerate((
            (up_x_all, up_x), (up_layer_all, up_layer), (twice_all, twice), (mean_x_all, mean_x),
            (mean_layer_all, mean_layer), (couple_all, couple),
        ))
    ]

    def copies(n, last):
        octant = octants[n]
        pairs = (
            (words, code, n), (edges_all, edges, n), (ends_all, ends, n), (average_all, average, n),
            (layers_all, layers, octant), (layers_t_all, layers_t, octant), (mean_layers_all, mean_layers, octant),
            (started, first, n),
        )
        return [
            pltpu.make_async_copy(source.at[index], target.at[n], sems.at[n, k])
            for k, (source, target, index) in enumerate(pairs)
            if last is None or last == (k == 7)
        ]

    def message_copy(source, box, n):
        return pltpu.make_async_copy(source.at[box], messages.at[n], sems.at[n, 8])

    def result_copy(n):
        return pltpu.make_async_copy(first.at[n], states.at[n], sems.at[n, 9])

    for copy in lists:
        copy.start()

    def one_slot(i, carry):
        for copy in copies(i, False):
            copy.wait()
        message_copy(own, 0, i).wait()
        chosen = messages.at[i]
        octant = octants[i]
        y_half = octant % 2
        z_half = octant // 2
        spread = [spread_ref[s] * 2.0 for s in range(8)]
        wide = species_column(spread_ref, 2.0, 1024)
        f = code[i].astype(F32) / LEVELS

        x_old = jnp.concatenate([chosen[0:24], chosen[24:48]], axis=1)
        x_new = jnp.concatenate([chosen[96:112], chosen[112:128]], axis=1)
        x_mid = 0.5 * (x_old[0:16] + x_new)
        ghosts = pick(jnp.concatenate([x_old, x_mid, jnp.zeros((8, 256), F32)], axis=0), up_x[...])
        side_old = chosen[48:80]
        side_mid = 0.5 * (side_old + chosen[128:160])

        def side_ghosts(side):
            high, low = halves(unpack_rows(side))
            high = dot(twice[...], high).astype(BF16)
            low = dot(twice[...], low).astype(BF16)
            return dot(high, up_layer[...]) + dot(low, up_layer[...])

        ghost_old = side_ghosts(side_old)
        ghost_mid = side_ghosts(side_mid)
        high, low = halves(jnp.where(iota((16, 128), 1) < 32, chosen[80:96], 0.0))
        high = dot(twice[0:32, 0:16], high).astype(BF16)
        low = dot(twice[0:32, 0:16], low).astype(BF16)
        f_ghost = dot(high, up_layer[...]) + dot(low, up_layer[...])

        lane = iota((32, 128), 1)
        row = iota((32, 128), 0)
        face = lane // 32 % 2 == 0
        place = lane % 32
        fl = edges[i, 512:544]
        scaling = COARSE_STEP / jnp.maximum(fl, FLOOR)
        at_face = jnp.where(face, scaling, 0.0)
        through = jnp.where(face, jnp.minimum(fl, f_ghost), 0.0)
        x_low = at_face * jnp.where(row == 0, 0.0, jnp.minimum(fl, pltpu.roll(fl, 1, 0)))
        x_high = at_face * jnp.where(row == 31, 0.0, jnp.minimum(fl, pltpu.roll(fl, 31, 0)))
        t_low = at_face * jnp.where(place == 0, 0.0, jnp.minimum(fl, pltpu.roll(fl, 1, 1)))
        t_high = at_face * jnp.where(place == 31, 0.0, jnp.minimum(fl, pltpu.roll(fl, 127, 1)))
        behind = at_face * jnp.minimum(fl, pltpu.roll(fl, 96, 1))
        ahead = jnp.where(face, 0.0, scaling * jnp.minimum(fl, pltpu.roll(fl, 32, 1)))
        everything = x_low + x_high + t_low + t_high + behind
        own_part = 1.0 - ADVECT * x_high
        upwind = ADVECT * x_low
        flux_one = []
        for s in range(8):
            part = slice(32 * s, 32 * s + 32)
            q = through * (ghost_old[part] - edges[i, part])
            flux_one.append(q)
            taken[s] = spread[s] * (scaling * q)

        long = iota((1, 1024), 1)
        f_low, f_high = ghosts[16:17], ghosts[17:18]
        m_low = jnp.minimum(f[0:1], f_low)
        m_high = jnp.minimum(f[31:32], f_high)
        scale_low = COARSE_STEP / jnp.maximum(f[0:1], FLOOR)
        scale_high = COARSE_STEP / jnp.maximum(f[31:32], FLOOR)

        def end_fluxes(low, high, c_low, c_high):
            low_flux = -m_low * (ADVECT * low - wide * (c_low - low))
            high_flux = m_high * (ADVECT * c_high - wide * (high - c_high))
            return low_flux, high_flux

        low_one, high_one = end_fluxes(ghosts[0:8], ghosts[8:16], ends[i, 0:8], ends[i, 8:16])
        end_low = -scale_low * low_one
        end_high = -scale_high * high_one

        crossed = pick(jnp.concatenate([taken[:, 0, :], taken[:, 31, :]], axis=0), layers[i])
        ends_there = pick(jnp.concatenate([end_low, end_high], axis=0), layers_t[i])
        corner_y = jnp.where(z_half == 1, 0, 31)
        corner_z = 64 + jnp.where(y_half == 1, 0, 31)
        turn = corner_y - corner_z + 128
        back = corner_z - corner_y
        flux_two = []
        for s in range(8):
            part = slice(32 * s, 32 * s + 32)
            v = taken[s]
            c = edges[i, 256 + 32 * s : 288 + 32 * s] + v
            c = c + jnp.where(lane == corner_y, pltpu.roll(v, turn, 1), 0.0)
            c = c + jnp.where(lane == corner_z, pltpu.roll(v, back, 1), 0.0)
            c = c + jnp.where(row == 0, ends_there[s : s + 1], jnp.where(row == 31, ends_there[8 + s : 9 + s], 0.0))
            flux_two.append(through * (ghost_mid[part] - c))
        low_two, high_two = end_fluxes(
            ghosts[24:32], ghosts[32:40], ends[i, 16:24] + end_low + crossed[0:8],
            ends[i, 24:32] + end_high + crossed[8:16],
        )

        high, low = halves(taken[...].reshape(256, 128))
        mixed = dot(rates[0], high) + dot(rates[1], high) + dot(rates[0], low)
        totals = []
        for s in range(8):
            v = taken[s]
            below = pltpu.roll(v, 1, 0)
            change = x_low * below + x_high * pltpu.roll(v, 31, 0)
            change = change + t_low * pltpu.roll(v, 1, 1) + t_high * pltpu.roll(v, 127, 1)
            change = change + ahead * pltpu.roll(v, 32, 1) - everything * v + scaling * flux_two[s]
            totals.append(own_part * v + upwind * below + spread[s] * change + mixed[32 * s : 32 * s + 32])
        total = jnp.concatenate(totals, axis=0)

        def tangential(c, fx, scale, inner):
            change = jnp.zeros_like(c)
            everything = inner
            for amount, wall in ((32, long < 32), (992, long >= 992), (1, long % 32 == 0), (1023, long % 32 == 31)):
                factor = scale * jnp.where(wall, 0.0, jnp.minimum(fx, pltpu.roll(fx, amount, 1)))
                change = change + factor * pltpu.roll(c, amount, 1)
                everything = everything + factor
            return change - everything * c

        end_mixed = 0.5 * COARSE_STEP * jnp.dot(
            reaction_ref[...], jnp.concatenate([end_low, end_high], axis=1), precision=lax.Precision.HIGHEST,
            preferred_element_type=F32,
        )
        inner_low = jnp.minimum(f[0:1], f[1:2])
        inner_high = jnp.minimum(f[30:31], f[31:32])
        row0 = (1.0 - ADVECT * (scale_low * inner_low)) * end_low - scale_low * low_two + end_mixed[:, 0:1024]
        row0 = row0 + wide * tangential(end_low, f[0:1], scale_low, scale_low * inner_low)
        row1 = (wide + ADVECT) * (COARSE_STEP / jnp.maximum(f[1:2], FLOOR) * inner_low) * end_low
        row30 = wide * (COARSE_STEP / jnp.maximum(f[30:31], FLOOR) * inner_high) * end_high
        row31 = end_high - scale_high * high_two + end_mixed[:, 1024:2048]
        row31 = row31 + wide * tangential(end_high, f[31:32], scale_high, scale_high * inner_high)

        x_parts = pick(
            jnp.concatenate([low_one + low_two, high_one + high_two, row0 + row1, row30 + row31], axis=0), mean_x[...]
        )
        coarse[...] = (average[i] + 0.5 * left_pick(couple[...], pick(total, mean_layers[i]))).reshape(8, 16, 256)
        coarse[:, 0, :] += 0.5 * x_parts[16:24]
        coarse[:, 15, :] += 0.5 * x_parts[24:32]
        for q in range(3):
            payload[q, i] = coarse[...].reshape(128, 256)[40 * q : 40 * q + 40]
        payload[3, i, 0:8] = coarse[...].reshape(128, 256)[120:128]
        payload[3, i, 8:24] = 0.5 * x_parts[0:16]
        fluxes = jnp.concatenate([flux_one[s] + flux_two[s] for s in range(8)], axis=0)
        sides = left_pick(couple[...], pick(fluxes, mean_layer[...])).reshape(8, 16, 128)
        sides = jnp.concatenate([(-0.5 * spread[s]) * sides[s] for s in range(8)], axis=0)
        sides = pack_rows(sides)
        payload[3, i, 24:40, 0:128] = sides[0:16]
        payload[3, i, 24:40, 128:256] = sides[16:32]

        copies(i, True)[0].wait()
        high, low = halves(total)
        for n in range(4):
            part = slice(256 * n, 256 * n + 256)
            added = dot(high, layers[i, :, part]) + dot(low, layers[i, :, part])
            first[i, :, :, part] += added.reshape(8, 32, 256)
        first[i, :, 0, :] += row0
        first[i, :, 1, :] += row1
        first[i, :, 30, :] += row30
        first[i, :, 31, :] += row31
        result_copy(i).start()
        return carry

    @pl.when(counts[0] > 0)
    def _():
        for copy in fixed:
            copy.start()
        for n in range(SLOTS):

            @pl.when(n < counts[0])
            def _():
                for copy in copies(n, None):
                    copy.start()
                home = parents[n] // SLOTS
                away = (home >> 1) - (column >> 1)
                same = ((home - column) & 1) == 0
                for source, is_same, step in (
                    (own_low, True, -1), (own, True, 0), (own_high, True, 1),
                    (other_low, False, -1), (other, False, 0), (other_high, False, 1),
                ):

                    @pl.when((same == is_same) & (away == step))
                    def _():
                        message_copy(source, parents[n] % SLOTS, n).start()

        set_rates(rates, reaction_smem, 0.5 * COARSE_STEP)
        for copy in fixed:
            copy.wait()
        lax.fori_loop(0, counts[0], one_slot, 0)
        for n in range(SLOTS):

            @pl.when(n < counts[0])
            def _():
                result_copy(n).wait()

    for copy in lists:
        copy.wait()


def decode(code):
    safe = jnp.maximum(code, 0)
    return safe // (OFFSETS * SLOTS) + 1, safe // SLOTS % OFFSETS - REACH, safe % SLOTS


def route_kernel(codes, mine, others, to_low, stay, to_high):
    column = lax.axis_index("box")
    for n, (step, target) in enumerate(((-1, to_low), (0, stay), (1, to_high))):
        for j in range(SLOTS):
            row, offset, slot = decode(codes[n, 7, j].astype(jnp.int32))
            child = column + 2 * step + offset
            target[j] = jnp.where(((child - column) & 1) == 0, mine[row, slot], others[row, slot])


def choose_kernel(codes, from_low, stay, from_high, chosen):
    column = lax.axis_index("box")
    for j in range(SLOTS):
        _, offset, _ = decode(codes[j])
        away = ((column + offset) >> 1) - (column >> 1)
        chosen[j] = jnp.where(away < 0, from_low[j], jnp.where(away == 0, stay[j], from_high[j]))


def finish_kernel(
    octants, codes, spread_ref, updated, message, register, code_words, halo, other_low, other, other_high,
    part0, part1, part2, part3, sel_x, sel_yz, states, chosen,
):
    i = pl.program_id(0)
    column = lax.axis_index("box")
    states[...] = updated[...]

    @pl.when(lax.axis_index("lev") == 0)
    def _():
        wide = species_column(spread_ref, 1.0, 128)
        odd = (column & 1) == 1

        def end_plane(x, p, neighbour_p, neighbour):
            f = code_words[0, x : x + 1, :].astype(F32) / LEVELS
            scaling = COARSE_STEP / jnp.maximum(f, FLOOR)
            for t in range(8):
                part = slice(128 * t, 128 * t + 128)
                base = 32 + (p * 8 + t) * 16
                there = 32 + (neighbour_p * 8 + t) * 16
                c = halo[base : base + 8, :]
                g = neighbour(there, there + 8)
                m = jnp.minimum(f[:, part], neighbour(there + 8, there + 9))
                if p == 0:
                    gain = m * (ADVECT * g - wide * (c - g))
                else:
                    gain = -m * (ADVECT * c - wide * (g - c))
                states[0, :, x, part] += scaling[:, part] * gain

        @pl.when(i == 0)
        def _():
            end_plane(0, 0, 1, lambda a, b: jnp.where(odd, other[a:b, :], other_low[a:b, :]))

        @pl.when(i == SLOTS - 1)
        def _():
            end_plane(31, 1, 0, lambda a, b: jnp.where(odd, other_high[a:b, :], other[a:b, :]))

        child = codes[i]

        @pl.when(child >= 0)
        def _():
            for q, part in enumerate((part0, part1, part2, part3)):
                chosen[40 * q : 40 * q + 40, :] = part[0]
            octant = octants[i]
            y_half = octant % 2
            z_half = octant // 2
            lane = iota((1, 1024), 1)
            inside = (lane // 512 == y_half) & (lane % 32 // 16 == z_half)
            own_f = jnp.concatenate([message[0, 0:24, :], message[0, 24:48, :]], axis=1)
            half = iota((16, 256), 0) < 8
            x_f = jnp.where(half, own_f[16:17], own_f[17:18])
            reg_x = jnp.concatenate([register[0, 0:16, :], register[0, 16:32, :]], axis=1)
            fix_x = COARSE_STEP / jnp.maximum(x_f, FLOOR) * (chosen[128:144, :] - reg_x)
            side_f = jnp.concatenate([message[0, 80:96, :]] * 2, axis=0)
            sides = jnp.concatenate([chosen[144:160, 0:128], chosen[144:160, 128:256]], axis=0)
            fix_sides = COARSE_STEP / jnp.maximum(side_f, FLOOR) * (sides - register[0, 32:64, :])
            planes = pick(fix_x, sel_x[0])
            states[0, :, 7, :] += planes[0:8]
            states[0, :, 24, :] += planes[8:16]
            filled = pick(chosen[0:128, :], sel_x[0])
            added = pick(unpack_rows(fix_sides), sel_yz[0])
            for s in range(8):
                part = slice(16 * s, 16 * s + 16)
                here = states[0, s, 8:24, :]
                states[0, s, 8:24, :] = jnp.where(inside, filled[part], here + added[part])


def shifted(block, axis, distance):
    devices = range(lax.axis_size(axis))
    return lax.ppermute(block, axis, [(i - distance, i) for i in devices if i - distance in devices])


def per_device(
    box_states, cell_code, diffusivity, reaction, coarse_child, coarse_octant, fine_parent, fine_octant, fine_count
):
    row = lax.axis_index("lev")
    count = lax.axis_size("box")
    swap = [(i, i ^ 1) for i in range(count)]
    vmem = pltpu.CompilerParams(vmem_limit_bytes=62 * 1024 * 1024)
    small = pltpu.CompilerParams(vmem_limit_bytes=8 * 1024 * 1024)

    def whole(a):
        zeros = (0,) * a.ndim
        return pl.BlockSpec(a.shape, lambda i, *_: zeros)

    def each(shape):
        tail = (0,) * len(shape)
        return pl.BlockSpec((1,) + shape, lambda i, *_: (i,) + tail)

    smem = pl.BlockSpec(memory_space=pltpu.SMEM)
    hbm = pl.BlockSpec(memory_space=pl.ANY)
    in_vmem = pl.BlockSpec(memory_space=pltpu.VMEM)
    previous = lambda i: jnp.maximum(i - 1, 0)
    following = lambda i: jnp.minimum(i + 1, SLOTS - 1)
    shape = jax.ShapeDtypeStruct
    sel_x, sel_yz = table(SEL_X), table(SEL_YZ)
    by_octant = lambda i, octants, *_: (octants[i], 0, 0)

    message, halo = pl.pallas_call(
        message_kernel,
        in_specs=[smem] * 4 + [in_vmem] + [hbm] * 5,
        out_specs=[in_vmem, in_vmem],
        scratch_shapes=[
            pltpu.VMEM((2, 256, 256), BF16),
            pltpu.VMEM((SLOTS, 8, 32, 1024), F32),
            pltpu.VMEM((SLOTS, 32, 1024), jnp.int32),
            pltpu.VMEM((SLOTS, 1024, 256), BF16),
            pltpu.VMEM((SLOTS, 1024, 128), BF16),
            pltpu.VMEM((SLOTS, 256, 128), BF16),
            pltpu.SemaphoreType.DMA((SLOTS, 5)),
        ],
        out_shape=[shape((SLOTS, 160, 128), F32), shape((640, 128), F32)],
        compiler_params=vmem,
        name="shells",
    )(
        coarse_octant, coarse_child, diffusivity, reaction, reaction, box_states, cell_code, sel_x, table(WINDOW_Z),
        table(CENTER),
    )

    mean_x, couple = table(0.25 * UP_X.T), table(TWICE.T)
    layers, layers_t = table(LAYERS), table(LAYERS.transpose(0, 2, 1))

    def early(base, boxes, *carried):
        def at(dims):
            tail = (0,) * len(dims)
            return pl.BlockSpec((1,) + dims, lambda i, *_: (base + i,) + tail)

        def for_octant(dims):
            return pl.BlockSpec((1,) + dims, lambda i, octants, *_: (octants[base + i], 0, 0))

        blocks = [(8, 32, 1024), (64, 128), (544, 128), (32, 1024), (128, 256)]
        return pl.pallas_call(
            functools.partial(early_kernel, base, len(carried) > 0),
            grid_spec=pltpu.PrefetchScalarGridSpec(
                num_scalar_prefetch=3,
                grid=(boxes,),
                in_specs=[
                    smem,
                    smem,
                    at((8, 32, 1024)),
                    at((32, 1024)),
                    pl.BlockSpec((1, 8, 8, 1024), lambda i, *_: (previous(base + i), 0, 3, 0)),
                    pl.BlockSpec((1, 8, 1024), lambda i, *_: (previous(base + i), 3, 0)),
                    pl.BlockSpec((1, 8, 8, 1024), lambda i, *_: (following(base + i), 0, 0, 0)),
                    pl.BlockSpec((1, 8, 1024), lambda i, *_: (following(base + i), 0, 0)),
                    for_octant((1024, 256)),
                    for_octant((1024, 128)),
                    pl.BlockSpec((1, 1024, 128), lambda i, octants, fine, *_: (fine[base + i], 0, 0)),
                    whole(mean_x),
                    whole(couple),
                ]
                + [hbm] * len(carried),
                out_specs=[at(dims) for dims in blocks],
                scratch_shapes=[
                    pltpu.VMEM((8, 10, 48, 128), F32),
                    pltpu.VMEM((8, 10, 48, 128), F32),
                    pltpu.VMEM((9, 8, 32, 128), F32),
                    pltpu.VMEM((8, 2, 32, 128), F32),
                    pltpu.VMEM((8, 2, 32, 128), F32),
                    pltpu.VMEM((2, 256, 256), BF16),
                ],
            ),
            out_shape=[shape((SLOTS,) + dims, F32) for dims in blocks],
            input_output_aliases={16 + n: n for n in range(len(carried))},
            compiler_params=vmem,
            cost_estimate=pl.CostEstimate(flops=10**9, bytes_accessed=30 * 10**6, transcendentals=0),
            name=f"early_{base}",
        )(
            coarse_octant, fine_octant, fine_count, diffusivity, reaction, box_states, cell_code, box_states, cell_code,
            box_states, cell_code, sel_x, sel_yz, layers_t, mean_x, couple, *carried,
        )

    updated, *carried = early(0, 3)
    spread_out = [lax.ppermute(message, "lev", [(0, r)]) for r in (1, 3, 2)]
    *spread_out, updated = lax.optimization_barrier((*spread_out, updated))
    own = jnp.where(row == 0, halo.reshape(SLOTS, 160, 128), spread_out[0] + spread_out[1] + spread_out[2])
    own_low = shifted(own, "box", 2)
    own_high = shifted(own, "box", -2)
    updated, register, *carried = early(3, 1, updated, *carried)
    own_low, own_high, updated = lax.optimization_barrier((own_low, own_high, updated))
    other = lax.ppermute(own, "box", swap)
    other_low = lax.ppermute(own_low, "box", swap)
    other_high = lax.ppermute(own_high, "box", swap)

    up_x, up_layer, twice, mean_layer = table(UP_X), table(UP_LAYER), table(TWICE), table(0.25 * UP_LAYER.T)
    mean_layers = table(LAYERS @ (0.25 * UP_X.T))
    constants = [up_x, up_layer, twice, mean_x, mean_layer, couple]
    states, payload, codes = pl.pallas_call(
        interface_kernel,
        in_specs=[smem] * 5 + [in_vmem] + [hbm] * 20,
        out_specs=[hbm, in_vmem, smem],
        scratch_shapes=[
            pltpu.VMEM((2, 256, 256), BF16),
            pltpu.VMEM((SLOTS, 160, 128), F32),
            pltpu.VMEM((8, 32, 128), F32),
            pltpu.VMEM((8, 16, 256), F32),
            pltpu.VMEM((SLOTS, 8, 32, 1024), F32),
            pltpu.VMEM((SLOTS, 32, 1024), jnp.int32),
            pltpu.VMEM((SLOTS, 544, 128), F32),
            pltpu.VMEM((SLOTS, 32, 1024), F32),
            pltpu.VMEM((SLOTS, 128, 256), F32),
        ]
        + [pltpu.VMEM(a.shape, BF16) for a in constants]
        + [
            pltpu.VMEM((SLOTS, 128, 1024), BF16),
            pltpu.VMEM((SLOTS, 1024, 128), BF16),
            pltpu.VMEM((SLOTS, 128, 256), BF16),
            pltpu.SemaphoreType.DMA((SLOTS, 10)),
            pltpu.SemaphoreType.DMA((9,)),
        ],
        out_shape=[
            shape((SLOTS, 8, 32, 1024), F32), shape((4, SLOTS, 40, 256), F32), shape((3, 8, 128), F32)
        ],
        input_output_aliases={25: 0},
        compiler_params=vmem,
        name="interfaces",
    )(
        fine_parent, fine_octant, fine_count, diffusivity, reaction, reaction, cell_code, *carried, *constants, layers,
        layers_t, mean_layers, own, own_low, own_high, other, other_low, other_high, updated,
    )

    mine = lax.all_to_all(payload, "lev", 0, 0)
    others = lax.ppermute(mine, "box", swap)
    bundle = shape((SLOTS, 40, 256), F32)
    to_low, stay, to_high = pl.pallas_call(
        route_kernel,
        in_specs=[smem] + [in_vmem] * 2,
        out_specs=[in_vmem] * 3,
        out_shape=[bundle] * 3,
        compiler_params=small,
        name="route",
    )(codes, mine, others)
    from_high = shifted(to_low, "box", -2)
    from_low = shifted(to_high, "box", 2)
    quarter = pl.pallas_call(
        choose_kernel,
        in_specs=[smem] + [in_vmem] * 3,
        out_specs=in_vmem,
        out_shape=bundle,
        compiler_params=small,
        name="choose",
    )(coarse_child, from_low, stay, from_high)
    quarters = [quarter] + [lax.ppermute(quarter, "lev", [(q, 0)]) for q in range(1, 4)]

    back_x, back_yz = table(SEL_X.transpose(0, 2, 1)), table(SEL_YZ.transpose(0, 2, 1))
    flat = [a.reshape(640, 128) for a in (other_low, other, other_high)]
    return pl.pallas_call(
        finish_kernel,
        grid_spec=pltpu.PrefetchScalarGridSpec(
            num_scalar_prefetch=2,
            grid=(SLOTS,),
            in_specs=[smem, each((8, 32, 1024)), each((160, 128)), each((64, 128)), each((32, 1024))]
            + [whole(halo)] * 4
            + [each((40, 256))] * 4
            + [pl.BlockSpec((1, 256, 1024), by_octant), pl.BlockSpec((1, 128, 1024), by_octant)],
            out_specs=each((8, 32, 1024)),
            scratch_shapes=[pltpu.VMEM((160, 256), F32)],
        ),
        out_shape=shape((SLOTS, 8, 32, 1024), F32),
        input_output_aliases={3: 0},
        compiler_params=vmem,
        name="finish",
    )(
        coarse_octant, coarse_child, diffusivity, states, message, register, cell_code, halo, *flat,
        *quarters, back_x, back_yz,
    )


def solution(mesh):
    return jax.shard_map(
        per_device,
        mesh=mesh,
        in_specs=(
            P(("lev", "box"), None, None, None),
            P(("lev", "box"), None, None),
            P(),
            P(),
            P("box"),
            P("box"),
            P(("lev", "box")),
            P(("lev", "box")),
            P(("lev", "box")),
        ),
        out_specs=P(("lev", "box"), None, None, None),
        check_vma=False,
    )
```

```python
import functools

import jax
import jax.numpy as jnp
import numpy as np
from jax import lax
from jax.experimental import pallas as pl
from jax.experimental.pallas import tpu as pltpu
from jax.sharding import PartitionSpec as P

ADVECT = 0.4
COARSE_STEP = 0.5
FLOOR = 0.5
LEVELS = 15.0
SLOTS = 4
REACH = 2
OFFSETS = 2 * REACH + 1
F32 = jnp.float32
BF16 = jnp.bfloat16


def selection_tables():
    lane = np.arange(1024)
    y, z = lane // 32, lane % 32
    place = np.arange(256)
    a, b = place // 16, place % 16
    i = np.arange(16)
    sel_x = np.zeros((4, 1024, 256), np.float32)
    sel_yz = np.zeros((4, 1024, 128), np.float32)
    for octant in range(4):
        y_half, z_half = octant % 2, octant // 2
        sel_x[octant, (16 * y_half + a) * 32 + 16 * z_half + b, place] = 1
        for g in range(4):
            sel_yz[octant, (16 - y_half) * 32 + 16 * z_half + i, 32 * g + i] = 1
            sel_yz[octant, (16 * y_half + i) * 32 + 16 - z_half, 32 * g + 16 + i] = 1
    up_x = np.zeros((256, 1024), np.float32)
    up_x[(y // 2) * 16 + z // 2, lane] = 1
    twice = np.zeros((256, 128), np.float32)
    rows = np.arange(256)
    twice[rows, rows // 32 * 16 + rows % 32 // 2] = 1
    window_z = np.zeros((2, 1024, 128), np.float32)
    for z_half in range(2):
        for step in range(3):
            rows = np.arange(32)
            window_z[z_half, rows * 32 + 15 - z_half + step, step * 32 + rows] = 1
    center = np.zeros((4, 256, 128), np.float32)
    for octant in range(4):
        for g in range(4):
            center[octant, 32 + 16 * (octant // 2) + i, 32 * g + i] = 1
            center[octant, 160 + 16 * (octant % 2) + i, 32 * g + 16 + i] = 1
    layers = np.zeros((4, 128, 1024), np.float32)
    line = np.arange(32)
    for octant in range(4):
        y_face, y_next = (0, 1) if octant % 2 else (31, 30)
        z_face, z_next = (0, 1) if octant // 2 else (31, 30)
        layers[octant, line, y_face * 32 + line] = 1
        layers[octant, 32 + line, y_next * 32 + line] = 1
        layers[octant, 64 + line, line * 32 + z_face] = 1
        layers[octant, 96 + line, line * 32 + z_next] = 1
    up_layer = np.zeros((128, 128), np.float32)
    for g in range(4):
        up_layer[32 * g + line // 2, line] = 1
        up_layer[32 * g + 16 + line // 2, 64 + line] = 1
    fill = np.zeros((2, 256, 512), np.float32)
    z_column = np.zeros((2, 128, 512), np.float32)
    y_row = np.zeros((4, 128, 128), np.float32)
    for g in range(4):
        for z_half in range(2):
            fill[z_half, place, a * 32 + 16 * z_half + b] = 1
            z_column[z_half, 32 * g + 16 + i, i * 32 + 16 - z_half] = 1
        for octant in range(4):
            y_row[octant, 32 * g + i, 96 * (octant % 2) + 16 * (octant // 2) + i] = 1
    return sel_x, sel_yz, up_x, twice, window_z, center, layers, up_layer, fill, z_column, y_row


SEL_X, SEL_YZ, UP_X, TWICE, WINDOW_Z, CENTER, LAYERS, UP_LAYER, FILL, Z_COLUMN, Y_ROW = selection_tables()


def table(values):
    return jnp.asarray(values.astype(jnp.bfloat16))


def halves(a):
    high = a.astype(BF16)
    return high, (a - high.astype(F32)).astype(BF16)


def dot(a, b):
    return jnp.dot(a, b, preferred_element_type=F32)


def pick(a, w):
    high, low = halves(a)
    return dot(high, w) + dot(low, w)


def left_pick(w, a):
    high, low = halves(a)
    return dot(w, high) + dot(w, low)


def iota(shape, dim):
    return lax.broadcasted_iota(jnp.int32, shape, dim)


def pack_rows(rows):
    group = iota((32, 128), 1) // 32
    out = rows[0:32]
    for g in range(1, 4):
        out = jnp.where(group == g, rows[32 * g : 32 * g + 32], out)
    return out


def unpack_rows(packed):
    group = iota((32, 128), 1) // 32
    return jnp.concatenate([jnp.where(group == g, packed, 0.0) for g in range(4)], axis=0)


def species_column(values_ref, factor, width):
    row = iota((8, width), 0)
    out = jnp.zeros((8, width), F32)
    for s in range(8):
        out = jnp.where(row == s, values_ref[s] * factor, out)
    return out


def set_rates(rates, reaction_ref, step):
    column = iota((1, 256), 1)
    for s in range(8):
        line = jnp.zeros((1, 256), F32)
        for t in range(8):
            line = jnp.where(column // 32 == t, reaction_ref[s, t] * step, line)
        high, low = halves(jnp.where(iota((32, 256), 0) == iota((32, 256), 1) % 32, line, 0.0))
        rates[0, 32 * s : 32 * s + 32] = high
        rates[1, 32 * s : 32 * s + 32] = low


def load_cells(cells, amounts):
    for t in range(8):
        cells[:, t + 1, 8:40, :] = amounts[:, :, 128 * t : 128 * t + 128]


def prepare(f, f_low, f_high, coef, scale):
    lane = iota((32, 1024), 1)
    row = iota((32, 1024), 0)
    depth = lane % 32
    scaling = scale / jnp.maximum(f, FLOOR)
    x_low = scaling * jnp.minimum(f, jnp.where(row == 0, f_low, pltpu.roll(f, 1, 0)))
    x_high = scaling * jnp.minimum(f, jnp.where(row == 31, f_high, pltpu.roll(f, 31, 0)))
    y_low = scaling * jnp.where(lane < 32, 0.0, jnp.minimum(f, pltpu.roll(f, 32, 1)))
    y_high = scaling * jnp.where(lane >= 992, 0.0, jnp.minimum(f, pltpu.roll(f, 992, 1)))
    z_low = scaling * jnp.where(depth == 0, 0.0, jnp.minimum(f, pltpu.roll(f, 1, 1)))
    z_high = scaling * jnp.where(depth == 31, 0.0, jnp.minimum(f, pltpu.roll(f, 1023, 1)))
    everything = x_low + x_high + y_low + y_high + z_low + z_high
    kinds = [x_low, x_high, y_low, y_high, z_low, z_high, everything, 1.0 - ADVECT * x_high, ADVECT * x_low]
    for k, kind in enumerate(kinds):
        for t in range(8):
            coef[k, t] = kind[:, 128 * t : 128 * t + 128]


def advance(cells, coef, reacted, rates, spread, store, layers=None, parts=None):
    lane = iota((8, 128), 1)

    def react(n, to):
        block = jnp.concatenate([cells[:, 2 * n + 1 + h, 8:40, :].reshape(256, 128) for h in range(2)], axis=1)
        high, low = halves(block)
        out = dot(rates[0], high) + dot(rates[1], high) + dot(rates[0], low)
        for h in range(2):
            to[:, h] = out[:, 128 * h : 128 * h + 128].reshape(8, 32, 128)
        if layers is not None:
            rows = layers[0, pl.ds(pl.multiple_of(256 * n, 256), 256), :]
            parts[n] = dot(high, rows) + dot(low, rows)

    def add(t, term):
        for xt in range(4):
            kinds = [coef[k, t, 8 * xt : 8 * xt + 8, :] for k in range(9)]
            x_low, x_high, y_low, y_high, z_low, z_high, everything, own, upwind = kinds
            at = 8 + 8 * xt
            for s in range(8):
                c = cells[s, t + 1, at : at + 8, :]
                below = cells[s, t + 1, at - 1 : at + 7, :]
                above = cells[s, t + 1, at + 1 : at + 9, :]
                left = pltpu.roll(jnp.where(lane >= 96, cells[s, t, at : at + 8, :], c), 32, 1)
                right = pltpu.roll(jnp.where(lane < 32, cells[s, t + 2, at : at + 8, :], c), 96, 1)
                change = x_low * below + x_high * above + y_low * left + y_high * right
                change = change + z_low * pltpu.roll(c, 1, 1) + z_high * pltpu.roll(c, 127, 1)
                change = change - everything * c
                result = own * c + upwind * below + spread[s] * change
                store(s, t, xt, result + term[s, 8 * xt : 8 * xt + 8, :])

    now, later = reacted
    react(0, now)

    def pair(m, carry):
        react(2 * m + 1, later)
        for h in range(2):
            add(4 * m + h, now.at[:, h])
        react(jnp.minimum(2 * m + 2, 3), now)
        for h in range(2):
            add(4 * m + 2 + h, later.at[:, h])
        return carry

    lax.fori_loop(0, 2, pair, 0)


def clear_rim(cells):
    cells[:, 0] = jnp.zeros((8, 48, 128), F32)
    cells[:, 9] = jnp.zeros((8, 48, 128), F32)
    cells[:, :, 0:8, :] = jnp.zeros((8, 10, 8, 128), F32)
    cells[:, :, 40:48, :] = jnp.zeros((8, 10, 8, 128), F32)


def message_kernel(
    octants, codes, spread_ref, reaction_smem, reaction_ref, boxes, words, sel_x_all, window_z_all, center_all, message,
    halo, rates, box_ref, code_ref, sel_x_ref, window_z_ref, center_ref, sems,
):
    def copies(i):
        octant = octants[i]
        pairs = (
            (boxes.at[i], box_ref.at[i]), (words.at[i], code_ref.at[i]), (window_z_all.at[octant // 2], window_z_ref.at[i]),
            (sel_x_all.at[octant], sel_x_ref.at[i]), (center_all.at[octant], center_ref.at[i]),
        )
        return [pltpu.make_async_copy(source, target, sems.at[i, n]) for n, (source, target) in enumerate(pairs)]

    def one_message(i, listed):
        y_half = octants[i] % 2
        box = box_ref.at[pl.ds(i, 1)]
        f = code_ref[i].astype(F32) / LEVELS
        lane = iota((32, 128), 1)
        place = lane % 32
        turn = 32 * (1 + y_half)
        spread = [spread_ref[s] for s in range(8)]

        def window_y(a, b):
            return jnp.where(iota(a.shape, 1) < turn, pltpu.roll(a, turn, 1), pltpu.roll(b, turn, 1))

        around_y = window_y(
            box[0, :, :, 384:512].reshape(256, 128), box[0, :, :, 512:640].reshape(256, 128)
        )
        around_z = pick(box[0].reshape(256, 1024), window_z_ref[i])
        f_windows = (window_y(f[:, 384:512], f[:, 512:640]), pick(f, window_z_ref[i]))
        both = jnp.concatenate([around_y, around_z], axis=1)
        high, low = halves(both)
        reacted = dot(rates[0], high) + dot(rates[1], high) + dot(rates[0], low)
        old_rows, new_rows = [[], []], [[], []]
        for w, (around, fw) in enumerate(zip((around_y, around_z), f_windows)):
            inner = fw[8:24]
            scaling = COARSE_STEP / jnp.maximum(inner, FLOOR)
            x_low = scaling * jnp.minimum(inner, pltpu.roll(fw, 1, 0)[8:24])
            x_high = scaling * jnp.minimum(inner, pltpu.roll(fw, 31, 0)[8:24])
            low_side = scaling * jnp.minimum(inner, pltpu.roll(inner, 32, 1))
            high_side = scaling * jnp.minimum(inner, pltpu.roll(inner, 96, 1))
            before = scaling * jnp.where(place[8:24] == 0, 0.0, jnp.minimum(inner, pltpu.roll(inner, 1, 1)))
            after = scaling * jnp.where(place[8:24] == 31, 0.0, jnp.minimum(inner, pltpu.roll(inner, 127, 1)))
            everything = x_low + x_high + low_side + high_side + before + after
            own = 1.0 - ADVECT * x_high
            upwind = ADVECT * x_low
            for s in range(8):
                rows = around[32 * s : 32 * s + 32]
                c = rows[8:24]
                below = pltpu.roll(rows, 1, 0)[8:24]
                above = pltpu.roll(rows, 31, 0)[8:24]
                change = x_low * below + x_high * above
                change = change + low_side * pltpu.roll(c, 32, 1) + high_side * pltpu.roll(c, 96, 1)
                change = change + before * pltpu.roll(c, 1, 1) + after * pltpu.roll(c, 127, 1) - everything * c
                term = reacted[32 * s + 8 : 32 * s + 24, 128 * w : 128 * w + 128]
                old_rows[w].append(c)
                new_rows[w].append(own * c + upwind * below + spread[s] * change + term)
        fractions = jnp.concatenate([fw[8:24] for fw in f_windows], axis=1)
        sides = [
            jnp.concatenate([jnp.concatenate(part[0], axis=0), jnp.concatenate(part[1], axis=0)], axis=1)
            for part in (old_rows, new_rows)
        ]
        side_parts = pick(jnp.concatenate(sides + [fractions], axis=0), center_ref[i])

        wide = species_column(spread_ref, 1.0, 1024)
        long = iota((1, 1024), 1)
        planes = [box[0, :, x, :] for x in (7, 24)]
        mixed = jnp.dot(
            reaction_ref[...], jnp.concatenate(planes, axis=1), precision=lax.Precision.HIGHEST,
            preferred_element_type=F32,
        )
        new_planes = []
        for n, x in enumerate((7, 24)):
            fx = f[x : x + 1]
            scaling = COARSE_STEP / jnp.maximum(fx, FLOOR)
            x_low = scaling * jnp.minimum(fx, f[x - 1 : x])
            x_high = scaling * jnp.minimum(fx, f[x + 1 : x + 2])
            shifts = ((32, long < 32), (992, long >= 992), (1, long % 32 == 0), (1023, long % 32 == 31))
            c = planes[n]
            below = box[0, :, x - 1, :]
            change = x_low * below + x_high * box[0, :, x + 1, :]
            everything = x_low + x_high
            for amount, wall in shifts:
                factor = scaling * jnp.where(wall, 0.0, jnp.minimum(fx, pltpu.roll(fx, amount, 1)))
                change = change + factor * pltpu.roll(c, amount, 1)
                everything = everything + factor
            change = change - everything * c
            moved = (1.0 - ADVECT * x_high) * c + ADVECT * x_low * below + wide * change
            new_planes.append(moved + COARSE_STEP * mixed[:, 1024 * n : 1024 * n + 1024])
        sublane = iota((8, 1024), 0)
        faces = jnp.where(sublane == 0, f[7:8], jnp.where(sublane == 1, f[24:25], 0.0))
        blank = jnp.zeros((8, 1024), F32)
        x_parts = pick(jnp.concatenate(planes + [faces] + new_planes + [blank], axis=0), sel_x_ref[i])

        message[i, 0:16, :] = x_parts[0:16, 0:128]
        message[i, 16:24, :] = jnp.where(iota((8, 128), 0) == 7, listed, x_parts[16:24, 0:128])
        message[i, 24:48, :] = x_parts[0:24, 128:256]
        message[i, 48:80, :] = pack_rows(side_parts[0:128])
        message[i, 80:96, :] = side_parts[256:272]
        message[i, 96:112, :] = x_parts[24:40, 0:128]
        message[i, 112:128, :] = x_parts[24:40, 128:256]
        message[i, 128:160, :] = pack_rows(side_parts[128:256])

        def put_plane(p, x):
            plane = box[0, :, x, :]
            for t in range(8):
                base = 32 + (p * 8 + t) * 16
                halo[base : base + 8, :] = plane[:, 128 * t : 128 * t + 128]
                halo[base + 8 : base + 16, :] = jnp.broadcast_to(f[x : x + 1, 128 * t : 128 * t + 128], (8, 128))

        @pl.when(i == 0)
        def _():
            put_plane(0, 0)

        @pl.when(i == SLOTS - 1)
        def _():
            put_plane(1, 31)

    @pl.when(lax.axis_index("lev") == 0)
    def _():
        for i in range(SLOTS):
            for copy in copies(i):
                copy.start()
        set_rates(rates, reaction_smem, COARSE_STEP)
        where = iota((8, 128), 1)
        listed = jnp.zeros((8, 128), F32)
        for j in range(SLOTS):
            listed = jnp.where(where == j, codes[j].astype(F32), listed)
        halo[...] = jnp.zeros((640, 128), F32)
        halo[16:24, :] = listed

        def each(i, carry):
            for copy in copies(i):
                copy.wait()
            one_message(i, listed)
            return carry

        lax.fori_loop(0, SLOTS, each, 0)


def early_kernel(
    base, again, octants, fine_octants, counts, spread_ref, reaction_smem, box, code, before, code_before, after,
    code_after, sel_x, sel_yz, layers, mean_x, couple, *refs,
):
    states, register, edges, ends, average, cells, later, coef, now, then, rates, parts = refs[5 * again :]
    i = pl.program_id(0)
    at = base + i
    coarse = lax.axis_index("lev") == 0
    used = coarse | (at < counts[0])

    @pl.when(jnp.logical_not(used))
    def _():
        states[0] = box[0]

    @pl.when(used)
    def _():
        @pl.when(i == 0)
        def _():
            set_rates(rates, reaction_smem, jnp.where(coarse, COARSE_STEP, 0.5 * COARSE_STEP))
            clear_rim(cells)
            clear_rim(later)

        f = code[0].astype(F32) / LEVELS
        f_before = jnp.where(coarse & (at > 0), code_before[0, 7:8, :].astype(F32) / LEVELS, 0.0)
        f_after = jnp.where(coarse & (at < SLOTS - 1), code_after[0, 0:1, :].astype(F32) / LEVELS, 0.0)
        load_cells(cells, box[0])
        for t in range(8):
            cells[:, t + 1, 7, :] = before[0, :, 7, 128 * t : 128 * t + 128]
            cells[:, t + 1, 40, :] = after[0, :, 0, 128 * t : 128 * t + 128]
        prepare(f, f_before, f_after, coef, COARSE_STEP)

        def store(s, t, xt, value):
            states[0, s, 8 * xt : 8 * xt + 8, pl.ds(pl.multiple_of(128 * t, 128), 128)] = value

        def store_later(s, t, xt, value):
            later[s, t + 1, 8 + 8 * xt : 16 + 8 * xt, :] = value

        @pl.when(coarse)
        def _():
            spread = [spread_ref[s] for s in range(8)]
            advance(cells, coef, (now, then), rates, spread, store)
            octant = octants[at]
            y_half = octant % 2
            z_half = octant // 2
            wide = species_column(spread_ref, 1.0, 1024)
            c7, c8 = box[0, :, 7, :], box[0, :, 8, :]
            c23, c24 = box[0, :, 23, :], box[0, :, 24, :]
            low_flux = -jnp.minimum(f[7:8], f[8:9]) * (ADVECT * c7 - wide * (c8 - c7))
            high_flux = jnp.minimum(f[23:24], f[24:25]) * (ADVECT * c23 - wide * (c24 - c23))
            x_parts = pick(jnp.concatenate([low_flux, high_flux], axis=0), sel_x[0])

            lane = iota((1, 1024), 1)
            y_row = lane // 32 == 16 - y_half
            y_roll = jnp.where(y_half == 0, 32, 992)
            z_roll = jnp.where(z_half == 0, 1, 1023)
            middle = f[8:24]
            inner_f = jnp.where(y_row, pltpu.roll(middle, y_roll, 1), pltpu.roll(middle, z_roll, 1))
            weight = -jnp.minimum(middle, inner_f)
            fluxes = []
            for s in range(8):
                c = box[0, s, 8:24, :]
                inner = jnp.where(y_row, pltpu.roll(c, y_roll, 1), pltpu.roll(c, z_roll, 1))
                fluxes.append(spread[s] * weight * (c - inner))
            side_parts = pick(jnp.concatenate(fluxes, axis=0), sel_yz[0])
            register[0, 0:16, :] = x_parts[:, 0:128]
            register[0, 16:32, :] = x_parts[:, 128:256]
            register[0, 32:64, :] = pack_rows(side_parts)

        @pl.when(jnp.logical_not(coarse))
        def _():
            spread = [spread_ref[s] * 2.0 for s in range(8)]
            advance(cells, coef, (now, then), rates, spread, store_later, layers, parts)
            edges[0, 0:256] = parts[0] + parts[1] + parts[2] + parts[3]
            advance(later, coef, (now, then), rates, spread, store, layers, parts)
            edges[0, 256:512] = parts[0] + parts[1] + parts[2] + parts[3]
            edges[0, 512:544] = pick(f, layers[0])
            ends[0, 0:8] = box[0, :, 0, :]
            ends[0, 8:16] = box[0, :, 31, :]
            for t in range(8):
                ends[0, 16:24, 128 * t : 128 * t + 128] = later[:, t + 1, 8, :]
                ends[0, 24:32, 128 * t : 128 * t + 128] = later[:, t + 1, 39, :]
            average[0] = 0.5 * left_pick(couple[...], pick(states[0].reshape(256, 1024), mean_x[...]))


def interface_kernel(
    parents, octants, counts, spread_ref, reaction_smem, reaction_ref, words, edges_all, ends_all, average_all, up_x_all,
    up_layer_all, twice_all, mean_x_all, mean_layer_all, couple_all, layers_all, layers_t_all, mean_layers_all,
    own, own_low, own_high, other, other_low, other_high, started, states, payload, codes, rates, messages, taken, coarse,
    first, code, edges, ends, average, up_x, up_layer, twice, mean_x, mean_layer, couple, layers, layers_t, mean_layers,
    rim, sems, fixed_sems,
):
    column = lax.axis_index("box")
    lists = [
        pltpu.make_async_copy(source.at[0, 16:24], codes.at[n], fixed_sems.at[n])
        for n, source in enumerate((own_low, own, own_high))
    ]
    fixed = [
        pltpu.make_async_copy(source, target, fixed_sems.at[3 + n])
        for n, (source, target) in enumerate((
            (up_x_all, up_x), (up_layer_all, up_layer), (twice_all, twice), (mean_x_all, mean_x),
            (mean_layer_all, mean_layer), (couple_all, couple),
        ))
    ]

    def copies(n, last):
        octant = octants[n]
        pairs = (
            (words, code, n), (edges_all, edges, n), (ends_all, ends, n), (average_all, average, n),
            (layers_all, layers, octant), (layers_t_all, layers_t, octant), (mean_layers_all, mean_layers, octant),
            (started, first, n),
        )
        return [
            pltpu.make_async_copy(source.at[index], target.at[n], sems.at[n, k])
            for k, (source, target, index) in enumerate(pairs)
            if last is None or last == (k == 7)
        ]

    def message_copy(source, box, n):
        return pltpu.make_async_copy(source.at[box], messages.at[n], sems.at[n, 8])

    def result_copy(n):
        return pltpu.make_async_copy(first.at[n], states.at[n], sems.at[n, 9])

    for copy in lists:
        copy.start()

    def row_ends():
        odd = (column & 1) == 1
        wide = species_column(spread_ref, 1.0, 128)
        ends_at = ((0, 0), (SLOTS - 1, 24))
        loads = [pltpu.make_async_copy(own.at[pl.ds(0, 2)], rim.at[0], sems.at[0, 0])]
        for p, (box, x) in enumerate(ends_at):
            loads.append(pltpu.make_async_copy(words.at[box, pl.ds(x, 8)], code.at[p, pl.ds(0, 8)], sems.at[1, p]))
            loads.append(pltpu.make_async_copy(states.at[box, :, pl.ds(x, 8)], first.at[p, :, pl.ds(0, 8)], sems.at[2, p]))
        for p, (even_from, odd_from) in enumerate(((other_low, other), (other, other_high))):

            @pl.when(odd)
            def _():
                pltpu.make_async_copy(odd_from.at[pl.ds(0, 2)], rim.at[1 + p], sems.at[3, p]).start()

            @pl.when(jnp.logical_not(odd))
            def _():
                pltpu.make_async_copy(even_from.at[pl.ds(0, 2)], rim.at[1 + p], sems.at[3, p]).start()

        for copy in loads:
            copy.start()
        for copy in loads:
            copy.wait()
        saves = []
        for p, (box, x) in enumerate(ends_at):
            pltpu.make_async_copy(other.at[pl.ds(0, 2)], rim.at[1 + p], sems.at[3, p]).wait()
            at = 7 * p
            f = code[p, at : at + 1, :].astype(F32) / LEVELS
            scaling = COARSE_STEP / jnp.maximum(f, FLOOR)
            for t in range(8):
                part = slice(128 * t, 128 * t + 128)
                here = 32 + (p * 8 + t) * 16
                there = 32 + ((1 - p) * 8 + t) * 16
                c = rim[0, here // 160, here % 160 : here % 160 + 8, :]
                g = rim[1 + p, there // 160, there % 160 : there % 160 + 8, :]
                g_f = rim[1 + p, there // 160, there % 160 + 8 : there % 160 + 9, :]
                m = jnp.minimum(f[:, part], g_f)
                if p == 0:
                    gain = m * (ADVECT * g - wide * (c - g))
                else:
                    gain = -m * (ADVECT * c - wide * (g - c))
                first[p, :, at, part] += scaling[:, part] * gain
            saves.append(
                pltpu.make_async_copy(first.at[p, :, pl.ds(0, 8)], states.at[box, :, pl.ds(x, 8)], sems.at[2, p])
            )
            saves[-1].start()
        for copy in saves:
            copy.wait()

    pl.when(lax.axis_index("lev") == 0)(row_ends)

    def fetch(n):
        for copy in copies(n, None):
            copy.start()
        home = parents[n] // SLOTS
        away = (home >> 1) - (column >> 1)
        same = ((home - column) & 1) == 0
        for source, is_same, step in (
            (own_low, True, -1), (own, True, 0), (own_high, True, 1),
            (other_low, False, -1), (other, False, 0), (other_high, False, 1),
        ):

            @pl.when((same == is_same) & (away == step))
            def _():
                message_copy(source, parents[n] % SLOTS, n).start()

    def one_slot(i, carry):
        @pl.when(i + 1 < counts[0])
        def _():
            fetch(i + 1)

        for copy in copies(i, False):
            copy.wait()
        message_copy(own, 0, i).wait()
        chosen = messages.at[i]
        octant = octants[i]
        y_half = octant % 2
        z_half = octant // 2
        spread = [spread_ref[s] * 2.0 for s in range(8)]
        wide = species_column(spread_ref, 2.0, 1024)
        f = code[i].astype(F32) / LEVELS

        x_old = jnp.concatenate([chosen[0:24], chosen[24:48]], axis=1)
        x_new = jnp.concatenate([chosen[96:112], chosen[112:128]], axis=1)
        x_mid = 0.5 * (x_old[0:16] + x_new)
        ghosts = pick(jnp.concatenate([x_old, x_mid, jnp.zeros((8, 256), F32)], axis=0), up_x[...])
        side_old = chosen[48:80]
        side_mid = 0.5 * (side_old + chosen[128:160])

        def side_ghosts(side):
            high, low = halves(unpack_rows(side))
            high = dot(twice[...], high).astype(BF16)
            low = dot(twice[...], low).astype(BF16)
            return dot(high, up_layer[...]) + dot(low, up_layer[...])

        ghost_old = side_ghosts(side_old)
        ghost_mid = side_ghosts(side_mid)
        high, low = halves(jnp.where(iota((16, 128), 1) < 32, chosen[80:96], 0.0))
        high = dot(twice[0:32, 0:16], high).astype(BF16)
        low = dot(twice[0:32, 0:16], low).astype(BF16)
        f_ghost = dot(high, up_layer[...]) + dot(low, up_layer[...])

        lane = iota((32, 128), 1)
        row = iota((32, 128), 0)
        face = lane // 32 % 2 == 0
        place = lane % 32
        fl = edges[i, 512:544]
        scaling = COARSE_STEP / jnp.maximum(fl, FLOOR)
        at_face = jnp.where(face, scaling, 0.0)
        through = jnp.where(face, jnp.minimum(fl, f_ghost), 0.0)
        x_low = at_face * jnp.where(row == 0, 0.0, jnp.minimum(fl, pltpu.roll(fl, 1, 0)))
        x_high = at_face * jnp.where(row == 31, 0.0, jnp.minimum(fl, pltpu.roll(fl, 31, 0)))
        t_low = at_face * jnp.where(place == 0, 0.0, jnp.minimum(fl, pltpu.roll(fl, 1, 1)))
        t_high = at_face * jnp.where(place == 31, 0.0, jnp.minimum(fl, pltpu.roll(fl, 127, 1)))
        behind = at_face * jnp.minimum(fl, pltpu.roll(fl, 96, 1))
        ahead = jnp.where(face, 0.0, scaling * jnp.minimum(fl, pltpu.roll(fl, 32, 1)))
        everything = x_low + x_high + t_low + t_high + behind
        own_part = 1.0 - ADVECT * x_high
        upwind = ADVECT * x_low
        flux_one = []
        for s in range(8):
            part = slice(32 * s, 32 * s + 32)
            q = through * (ghost_old[part] - edges[i, part])
            flux_one.append(q)
            taken[s] = spread[s] * (scaling * q)

        long = iota((1, 1024), 1)
        f_low, f_high = ghosts[16:17], ghosts[17:18]
        m_low = jnp.minimum(f[0:1], f_low)
        m_high = jnp.minimum(f[31:32], f_high)
        scale_low = COARSE_STEP / jnp.maximum(f[0:1], FLOOR)
        scale_high = COARSE_STEP / jnp.maximum(f[31:32], FLOOR)

        def end_fluxes(low, high, c_low, c_high):
            low_flux = -m_low * (ADVECT * low - wide * (c_low - low))
            high_flux = m_high * (ADVECT * c_high - wide * (high - c_high))
            return low_flux, high_flux

        low_one, high_one = end_fluxes(ghosts[0:8], ghosts[8:16], ends[i, 0:8], ends[i, 8:16])
        end_low = -scale_low * low_one
        end_high = -scale_high * high_one

        crossed = pick(jnp.concatenate([taken[:, 0, :], taken[:, 31, :]], axis=0), layers[i])
        ends_there = pick(jnp.concatenate([end_low, end_high], axis=0), layers_t[i])
        corner_y = jnp.where(z_half == 1, 0, 31)
        corner_z = 64 + jnp.where(y_half == 1, 0, 31)
        turn = corner_y - corner_z + 128
        back = corner_z - corner_y
        flux_two = []
        for s in range(8):
            part = slice(32 * s, 32 * s + 32)
            v = taken[s]
            c = edges[i, 256 + 32 * s : 288 + 32 * s] + v
            c = c + jnp.where(lane == corner_y, pltpu.roll(v, turn, 1), 0.0)
            c = c + jnp.where(lane == corner_z, pltpu.roll(v, back, 1), 0.0)
            c = c + jnp.where(row == 0, ends_there[s : s + 1], jnp.where(row == 31, ends_there[8 + s : 9 + s], 0.0))
            flux_two.append(through * (ghost_mid[part] - c))
        low_two, high_two = end_fluxes(
            ghosts[24:32], ghosts[32:40], ends[i, 16:24] + end_low + crossed[0:8],
            ends[i, 24:32] + end_high + crossed[8:16],
        )

        high, low = halves(taken[...].reshape(256, 128))
        mixed = dot(rates[0], high) + dot(rates[1], high) + dot(rates[0], low)
        totals = []
        for s in range(8):
            v = taken[s]
            below = pltpu.roll(v, 1, 0)
            change = x_low * below + x_high * pltpu.roll(v, 31, 0)
            change = change + t_low * pltpu.roll(v, 1, 1) + t_high * pltpu.roll(v, 127, 1)
            change = change + ahead * pltpu.roll(v, 32, 1) - everything * v + scaling * flux_two[s]
            totals.append(own_part * v + upwind * below + spread[s] * change + mixed[32 * s : 32 * s + 32])
        total = jnp.concatenate(totals, axis=0)

        def tangential(c, fx, scale, inner):
            change = jnp.zeros_like(c)
            everything = inner
            for amount, wall in ((32, long < 32), (992, long >= 992), (1, long % 32 == 0), (1023, long % 32 == 31)):
                factor = scale * jnp.where(wall, 0.0, jnp.minimum(fx, pltpu.roll(fx, amount, 1)))
                change = change + factor * pltpu.roll(c, amount, 1)
                everything = everything + factor
            return change - everything * c

        end_mixed = 0.5 * COARSE_STEP * jnp.dot(
            reaction_ref[...], jnp.concatenate([end_low, end_high], axis=1), precision=lax.Precision.HIGHEST,
            preferred_element_type=F32,
        )
        inner_low = jnp.minimum(f[0:1], f[1:2])
        inner_high = jnp.minimum(f[30:31], f[31:32])
        row0 = (1.0 - ADVECT * (scale_low * inner_low)) * end_low - scale_low * low_two + end_mixed[:, 0:1024]
        row0 = row0 + wide * tangential(end_low, f[0:1], scale_low, scale_low * inner_low)
        row1 = (wide + ADVECT) * (COARSE_STEP / jnp.maximum(f[1:2], FLOOR) * inner_low) * end_low
        row30 = wide * (COARSE_STEP / jnp.maximum(f[30:31], FLOOR) * inner_high) * end_high
        row31 = end_high - scale_high * high_two + end_mixed[:, 1024:2048]
        row31 = row31 + wide * tangential(end_high, f[31:32], scale_high, scale_high * inner_high)

        x_parts = pick(
            jnp.concatenate([low_one + low_two, high_one + high_two, row0 + row1, row30 + row31], axis=0), mean_x[...]
        )
        coarse[...] = (average[i] + 0.5 * left_pick(couple[...], pick(total, mean_layers[i]))).reshape(8, 16, 256)
        coarse[:, 0, :] += 0.5 * x_parts[16:24]
        coarse[:, 15, :] += 0.5 * x_parts[24:32]
        for q in range(3):
            payload[q, i] = coarse[...].reshape(128, 256)[40 * q : 40 * q + 40]
        payload[3, i, 0:8] = coarse[...].reshape(128, 256)[120:128]
        payload[3, i, 8:24] = 0.5 * x_parts[0:16]
        fluxes = jnp.concatenate([flux_one[s] + flux_two[s] for s in range(8)], axis=0)
        sides = left_pick(couple[...], pick(fluxes, mean_layer[...])).reshape(8, 16, 128)
        sides = jnp.concatenate([(-0.5 * spread[s]) * sides[s] for s in range(8)], axis=0)
        sides = pack_rows(sides)
        payload[3, i, 24:40, 0:128] = sides[0:16]
        payload[3, i, 24:40, 128:256] = sides[16:32]

        copies(i, True)[0].wait()
        high, low = halves(total)
        for n in range(4):
            part = slice(256 * n, 256 * n + 256)
            added = dot(high, layers[i, :, part]) + dot(low, layers[i, :, part])
            first[i, :, :, part] += added.reshape(8, 32, 256)
        first[i, :, 0, :] += row0
        first[i, :, 1, :] += row1
        first[i, :, 30, :] += row30
        first[i, :, 31, :] += row31
        result_copy(i).start()
        return carry

    @pl.when(counts[0] > 0)
    def _():
        for copy in fixed:
            copy.start()
        fetch(0)
        set_rates(rates, reaction_smem, 0.5 * COARSE_STEP)
        for copy in fixed:
            copy.wait()
        lax.fori_loop(0, counts[0], one_slot, 0)
        for n in range(SLOTS):

            @pl.when(n < counts[0])
            def _():
                result_copy(n).wait()

    for copy in lists:
        copy.wait()


def decode(code):
    safe = jnp.maximum(code, 0)
    return safe // (OFFSETS * SLOTS) + 1, safe // SLOTS % OFFSETS - REACH, safe % SLOTS


def route_kernel(codes, mine, others, to_low, stay, to_high):
    column = lax.axis_index("box")
    for n, (step, target) in enumerate(((-1, to_low), (0, stay), (1, to_high))):
        for j in range(SLOTS):
            row, offset, slot = decode(codes[n, 7, j].astype(jnp.int32))
            child = column + 2 * step + offset
            target[j] = jnp.where(((child - column) & 1) == 0, mine[row, slot], others[row, slot])


def choose_kernel(codes, from_low, stay, from_high, chosen):
    column = lax.axis_index("box")
    for j in range(SLOTS):
        _, offset, _ = decode(codes[j])
        away = ((column + offset) >> 1) - (column >> 1)
        chosen[0, j] = jnp.where(away < 0, from_low[j], jnp.where(away == 0, stay[j], from_high[j]))


def finish_kernel(
    octants, codes, message, register, parts, fill, z_column, y_row, updated, states, window, beside, sems
):
    def copies(i, out):
        y_half = octants[i] % 2
        pairs = (
            (pl.ds(pl.multiple_of(512 * y_half, 512), 512), window.at[i]),
            (pl.ds(pl.multiple_of(512 - 128 * y_half, 128), 128), beside.at[i]),
        )
        result = []
        for n, (lanes, here) in enumerate(pairs):
            there = states.at[i, :, :, lanes]
            source, target = (here, there) if out else (there, here)
            result.append(pltpu.make_async_copy(source, target, sems.at[i, n]))
        return result

    def one_box(i):
        octant = octants[i]
        z_half = octant // 2
        inside = iota((1, 512), 1) % 32 // 16 == z_half
        own_f = jnp.concatenate([message[i, 0:24, :], message[i, 24:48, :]], axis=1)
        x_f = jnp.where(iota((16, 256), 0) < 8, own_f[16:17], own_f[17:18])
        reg_x = jnp.concatenate([register[i, 0:16, :], register[i, 16:32, :]], axis=1)
        fix_x = COARSE_STEP / jnp.maximum(x_f, FLOOR) * (parts[3, i, 8:24, :] - reg_x)
        side_f = jnp.concatenate([message[i, 80:96, :]] * 2, axis=0)
        sides = jnp.concatenate([parts[3, i, 24:40, 0:128], parts[3, i, 24:40, 128:256]], axis=0)
        fix_sides = unpack_rows(COARSE_STEP / jnp.maximum(side_f, FLOOR) * (sides - register[i, 32:64, :]))
        average = jnp.concatenate([parts[q, i] for q in range(3)] + [parts[3, i, 0:8, :]], axis=0)
        planes = pick(fix_x, fill[z_half])
        filled = pick(average, fill[z_half])
        along = pick(fix_sides, z_column[z_half])
        across = pick(fix_sides, y_row[octant])
        for copy in copies(i, False):
            copy.wait()
        window[i, :, 7, :] += planes[0:8]
        window[i, :, 24, :] += planes[8:16]
        for s in range(8):
            part = slice(16 * s, 16 * s + 16)
            window[i, s, 8:24, :] = jnp.where(inside, filled[part], window[i, s, 8:24, :] + along[part])
            beside[i, s, 8:24, :] += across[part]
        for copy in copies(i, True):
            copy.start()

    def each(act):
        for i in range(SLOTS):

            @pl.when(codes[i] >= 0)
            def _():
                act(i)

    @pl.when(lax.axis_index("lev") == 0)
    def _():
        each(lambda i: [copy.start() for copy in copies(i, False)])
        each(one_box)
        each(lambda i: [copy.wait() for copy in copies(i, True)])


def shifted(block, axis, distance):
    devices = range(lax.axis_size(axis))
    return lax.ppermute(block, axis, [(i - distance, i) for i in devices if i - distance in devices])


def per_device(
    box_states, cell_code, diffusivity, reaction, coarse_child, coarse_octant, fine_parent, fine_octant, fine_count
):
    row = lax.axis_index("lev")
    count = lax.axis_size("box")
    swap = [(i, i ^ 1) for i in range(count)]
    vmem = pltpu.CompilerParams(vmem_limit_bytes=62 * 1024 * 1024)
    small = pltpu.CompilerParams(vmem_limit_bytes=8 * 1024 * 1024)

    def whole(a):
        zeros = (0,) * a.ndim
        return pl.BlockSpec(a.shape, lambda i, *_: zeros)

    def each(shape):
        tail = (0,) * len(shape)
        return pl.BlockSpec((1,) + shape, lambda i, *_: (i,) + tail)

    smem = pl.BlockSpec(memory_space=pltpu.SMEM)
    hbm = pl.BlockSpec(memory_space=pl.ANY)
    in_vmem = pl.BlockSpec(memory_space=pltpu.VMEM)
    previous = lambda i: jnp.maximum(i - 1, 0)
    following = lambda i: jnp.minimum(i + 1, SLOTS - 1)
    shape = jax.ShapeDtypeStruct
    sel_x, sel_yz = table(SEL_X), table(SEL_YZ)
    by_octant = lambda i, octants, *_: (octants[i], 0, 0)

    message, halo = pl.pallas_call(
        message_kernel,
        in_specs=[smem] * 4 + [in_vmem] + [hbm] * 5,
        out_specs=[in_vmem, in_vmem],
        scratch_shapes=[
            pltpu.VMEM((2, 256, 256), BF16),
            pltpu.VMEM((SLOTS, 8, 32, 1024), F32),
            pltpu.VMEM((SLOTS, 32, 1024), jnp.int32),
            pltpu.VMEM((SLOTS, 1024, 256), BF16),
            pltpu.VMEM((SLOTS, 1024, 128), BF16),
            pltpu.VMEM((SLOTS, 256, 128), BF16),
            pltpu.SemaphoreType.DMA((SLOTS, 5)),
        ],
        out_shape=[shape((SLOTS, 160, 128), F32), shape((640, 128), F32)],
        compiler_params=vmem,
        name="shells",
    )(
        coarse_octant, coarse_child, diffusivity, reaction, reaction, box_states, cell_code, sel_x, table(WINDOW_Z),
        table(CENTER),
    )

    mean_x, couple = table(0.25 * UP_X.T), table(TWICE.T)
    layers, layers_t = table(LAYERS), table(LAYERS.transpose(0, 2, 1))

    def early(base, boxes, *carried):
        def at(dims):
            tail = (0,) * len(dims)
            return pl.BlockSpec((1,) + dims, lambda i, *_: (base + i,) + tail)

        def for_octant(dims):
            return pl.BlockSpec((1,) + dims, lambda i, octants, *_: (octants[base + i], 0, 0))

        blocks = [(8, 32, 1024), (64, 128), (544, 128), (32, 1024), (128, 256)]
        return pl.pallas_call(
            functools.partial(early_kernel, base, len(carried) > 0),
            grid_spec=pltpu.PrefetchScalarGridSpec(
                num_scalar_prefetch=3,
                grid=(boxes,),
                in_specs=[
                    smem,
                    smem,
                    at((8, 32, 1024)),
                    at((32, 1024)),
                    pl.BlockSpec((1, 8, 8, 1024), lambda i, *_: (previous(base + i), 0, 3, 0)),
                    pl.BlockSpec((1, 8, 1024), lambda i, *_: (previous(base + i), 3, 0)),
                    pl.BlockSpec((1, 8, 8, 1024), lambda i, *_: (following(base + i), 0, 0, 0)),
                    pl.BlockSpec((1, 8, 1024), lambda i, *_: (following(base + i), 0, 0)),
                    for_octant((1024, 256)),
                    for_octant((1024, 128)),
                    pl.BlockSpec((1, 1024, 128), lambda i, octants, fine, *_: (fine[base + i], 0, 0)),
                    whole(mean_x),
                    whole(couple),
                ]
                + [hbm] * len(carried),
                out_specs=[at(dims) for dims in blocks],
                scratch_shapes=[
                    pltpu.VMEM((8, 10, 48, 128), F32),
                    pltpu.VMEM((8, 10, 48, 128), F32),
                    pltpu.VMEM((9, 8, 32, 128), F32),
                    pltpu.VMEM((8, 2, 32, 128), F32),
                    pltpu.VMEM((8, 2, 32, 128), F32),
                    pltpu.VMEM((2, 256, 256), BF16),
                    pltpu.VMEM((4, 256, 128), F32),
                ],
            ),
            out_shape=[shape((SLOTS,) + dims, F32) for dims in blocks],
            input_output_aliases={16 + n: n for n in range(len(carried))},
            compiler_params=vmem,
            cost_estimate=pl.CostEstimate(flops=10**9, bytes_accessed=30 * 10**6, transcendentals=0),
            name=f"early_{base}",
        )(
            coarse_octant, fine_octant, fine_count, diffusivity, reaction, box_states, cell_code, box_states, cell_code,
            box_states, cell_code, sel_x, sel_yz, layers_t, mean_x, couple, *carried,
        )

    updated, *carried = early(0, 3)
    spread_out = [lax.ppermute(message, "lev", [(0, r)]) for r in (1, 3, 2)]
    *spread_out, updated = lax.optimization_barrier((*spread_out, updated))
    own = jnp.where(row == 0, halo.reshape(SLOTS, 160, 128), spread_out[0] + spread_out[1] + spread_out[2])
    own_low = shifted(own, "box", 2)
    own_high = shifted(own, "box", -2)
    updated, register, *carried = early(3, 1, updated, *carried)
    own_low, own_high, updated = lax.optimization_barrier((own_low, own_high, updated))
    other = lax.ppermute(own, "box", swap)
    other_low = lax.ppermute(own_low, "box", swap)
    other_high = lax.ppermute(own_high, "box", swap)

    up_x, up_layer, twice, mean_layer = table(UP_X), table(UP_LAYER), table(TWICE), table(0.25 * UP_LAYER.T)
    mean_layers = table(LAYERS @ (0.25 * UP_X.T))
    constants = [up_x, up_layer, twice, mean_x, mean_layer, couple]
    states, payload, codes = pl.pallas_call(
        interface_kernel,
        in_specs=[smem] * 5 + [in_vmem] + [hbm] * 20,
        out_specs=[hbm, in_vmem, smem],
        scratch_shapes=[
            pltpu.VMEM((2, 256, 256), BF16),
            pltpu.VMEM((SLOTS, 160, 128), F32),
            pltpu.VMEM((8, 32, 128), F32),
            pltpu.VMEM((8, 16, 256), F32),
            pltpu.VMEM((SLOTS, 8, 32, 1024), F32),
            pltpu.VMEM((SLOTS, 32, 1024), jnp.int32),
            pltpu.VMEM((SLOTS, 544, 128), F32),
            pltpu.VMEM((SLOTS, 32, 1024), F32),
            pltpu.VMEM((SLOTS, 128, 256), F32),
        ]
        + [pltpu.VMEM(a.shape, BF16) for a in constants]
        + [
            pltpu.VMEM((SLOTS, 128, 1024), BF16),
            pltpu.VMEM((SLOTS, 1024, 128), BF16),
            pltpu.VMEM((SLOTS, 128, 256), BF16),
            pltpu.VMEM((3, 2, 160, 128), F32),
            pltpu.SemaphoreType.DMA((SLOTS, 10)),
            pltpu.SemaphoreType.DMA((9,)),
        ],
        out_shape=[
            shape((SLOTS, 8, 32, 1024), F32), shape((4, SLOTS, 40, 256), F32), shape((3, 8, 128), F32)
        ],
        input_output_aliases={25: 0},
        compiler_params=vmem,
        name="interfaces",
    )(
        fine_parent, fine_octant, fine_count, diffusivity, reaction, reaction, cell_code, *carried, *constants, layers,
        layers_t, mean_layers, own, own_low, own_high, other, other_low, other_high, updated,
    )

    mine = lax.all_to_all(payload, "lev", 0, 0)
    others = lax.ppermute(mine, "box", swap)
    bundle = shape((SLOTS, 40, 256), F32)
    to_low, stay, to_high = pl.pallas_call(
        route_kernel,
        in_specs=[smem] + [in_vmem] * 2,
        out_specs=[in_vmem] * 3,
        out_shape=[bundle] * 3,
        compiler_params=small,
        name="route",
    )(codes, mine, others)
    from_high = shifted(to_low, "box", -2)
    from_low = shifted(to_high, "box", 2)
    quarter = pl.pallas_call(
        choose_kernel,
        in_specs=[smem] + [in_vmem] * 3,
        out_specs=in_vmem,
        out_shape=shape((4, SLOTS, 40, 256), F32),
        compiler_params=small,
        name="choose",
    )(coarse_child, from_low, stay, from_high)
    parts = lax.all_to_all(quarter, "lev", 0, 0)

    return pl.pallas_call(
        finish_kernel,
        in_specs=[smem] * 2 + [in_vmem] * 6 + [hbm],
        out_specs=hbm,
        scratch_shapes=[
            pltpu.VMEM((SLOTS, 8, 32, 512), F32),
            pltpu.VMEM((SLOTS, 8, 32, 128), F32),
            pltpu.SemaphoreType.DMA((SLOTS, 2)),
        ],
        out_shape=shape((SLOTS, 8, 32, 1024), F32),
        input_output_aliases={8: 0},
        compiler_params=pltpu.CompilerParams(vmem_limit_bytes=24 * 1024 * 1024),
        name="finish",
    )(coarse_octant, coarse_child, message, register, parts, table(FILL), table(Z_COLUMN), table(Y_ROW), states)


def solution(mesh):
    return jax.shard_map(
        per_device,
        mesh=mesh,
        in_specs=(
            P(("lev", "box"), None, None, None),
            P(("lev", "box"), None, None),
            P(),
            P(),
            P("box"),
            P("box"),
            P(("lev", "box")),
            P(("lev", "box")),
            P(("lev", "box")),
        ),
        out_specs=P(("lev", "box"), None, None, None),
        check_vma=False,
    )
```

```python
import functools

import jax
import jax.numpy as jnp
import numpy as np
from jax import lax
from jax.experimental import pallas as pl
from jax.experimental.pallas import tpu as pltpu
from jax.sharding import PartitionSpec as P

ADVECT = 0.4
COARSE_STEP = 0.5
FLOOR = 0.5
LEVELS = 15.0
SLOTS = 4
REACH = 2
OFFSETS = 2 * REACH + 1
F32 = jnp.float32
BF16 = jnp.bfloat16


def selection_tables():
    lane = np.arange(1024)
    y, z = lane // 32, lane % 32
    place = np.arange(256)
    a, b = place // 16, place % 16
    i = np.arange(16)
    sel_x = np.zeros((4, 1024, 256), np.float32)
    sel_yz = np.zeros((4, 1024, 128), np.float32)
    for octant in range(4):
        y_half, z_half = octant % 2, octant // 2
        sel_x[octant, (16 * y_half + a) * 32 + 16 * z_half + b, place] = 1
        for g in range(4):
            sel_yz[octant, (16 - y_half) * 32 + 16 * z_half + i, 32 * g + i] = 1
            sel_yz[octant, (16 * y_half + i) * 32 + 16 - z_half, 32 * g + 16 + i] = 1
    up_x = np.zeros((256, 1024), np.float32)
    up_x[(y // 2) * 16 + z // 2, lane] = 1
    twice = np.zeros((256, 128), np.float32)
    rows = np.arange(256)
    twice[rows, rows // 32 * 16 + rows % 32 // 2] = 1
    window_z = np.zeros((2, 1024, 128), np.float32)
    for z_half in range(2):
        for step in range(3):
            rows = np.arange(32)
            window_z[z_half, rows * 32 + 15 - z_half + step, step * 32 + rows] = 1
    center = np.zeros((4, 256, 128), np.float32)
    for octant in range(4):
        for g in range(4):
            center[octant, 32 + 16 * (octant // 2) + i, 32 * g + i] = 1
            center[octant, 160 + 16 * (octant % 2) + i, 32 * g + 16 + i] = 1
    layers = np.zeros((4, 128, 1024), np.float32)
    line = np.arange(32)
    for octant in range(4):
        y_face, y_next = (0, 1) if octant % 2 else (31, 30)
        z_face, z_next = (0, 1) if octant // 2 else (31, 30)
        layers[octant, line, y_face * 32 + line] = 1
        layers[octant, 32 + line, y_next * 32 + line] = 1
        layers[octant, 64 + line, line * 32 + z_face] = 1
        layers[octant, 96 + line, line * 32 + z_next] = 1
    up_layer = np.zeros((128, 128), np.float32)
    for g in range(4):
        up_layer[32 * g + line // 2, line] = 1
        up_layer[32 * g + 16 + line // 2, 64 + line] = 1
    fill = np.zeros((2, 256, 512), np.float32)
    z_column = np.zeros((2, 128, 512), np.float32)
    y_row = np.zeros((4, 128, 128), np.float32)
    for g in range(4):
        for z_half in range(2):
            fill[z_half, place, a * 32 + 16 * z_half + b] = 1
            z_column[z_half, 32 * g + 16 + i, i * 32 + 16 - z_half] = 1
        for octant in range(4):
            y_row[octant, 32 * g + i, 96 * (octant % 2) + 16 * (octant // 2) + i] = 1
    return sel_x, sel_yz, up_x, twice, window_z, center, layers, up_layer, fill, z_column, y_row


SEL_X, SEL_YZ, UP_X, TWICE, WINDOW_Z, CENTER, LAYERS, UP_LAYER, FILL, Z_COLUMN, Y_ROW = selection_tables()


def table(values):
    return jnp.asarray(values.astype(jnp.bfloat16))


def halves(a):
    high = a.astype(BF16)
    return high, (a - high.astype(F32)).astype(BF16)


def dot(a, b):
    return jnp.dot(a, b, preferred_element_type=F32)


def pick(a, w):
    high, low = halves(a)
    return dot(high, w) + dot(low, w)


def left_pick(w, a):
    high, low = halves(a)
    return dot(w, high) + dot(w, low)


def iota(shape, dim):
    return lax.broadcasted_iota(jnp.int32, shape, dim)


def pack_rows(rows):
    group = iota((32, 128), 1) // 32
    out = rows[0:32]
    for g in range(1, 4):
        out = jnp.where(group == g, rows[32 * g : 32 * g + 32], out)
    return out


def unpack_rows(packed):
    group = iota((32, 128), 1) // 32
    return jnp.concatenate([jnp.where(group == g, packed, 0.0) for g in range(4)], axis=0)


def species_column(values_ref, factor, width):
    row = iota((8, width), 0)
    out = jnp.zeros((8, width), F32)
    for s in range(8):
        out = jnp.where(row == s, values_ref[s] * factor, out)
    return out


def set_rates(rates, reaction_ref, step):
    column = iota((1, 256), 1)
    for s in range(8):
        line = jnp.zeros((1, 256), F32)
        for t in range(8):
            line = jnp.where(column // 32 == t, reaction_ref[s, t] * step, line)
        high, low = halves(jnp.where(iota((32, 256), 0) == iota((32, 256), 1) % 32, line, 0.0))
        rates[0, 32 * s : 32 * s + 32] = high
        rates[1, 32 * s : 32 * s + 32] = low


def load_cells(cells, amounts):
    for t in range(8):
        cells[:, t + 1, 8:40, :] = amounts[:, :, 128 * t : 128 * t + 128]


def prepare(f, f_low, f_high, coef, scale):
    lane = iota((32, 1024), 1)
    row = iota((32, 1024), 0)
    depth = lane % 32
    scaling = scale / jnp.maximum(f, FLOOR)
    x_low = scaling * jnp.minimum(f, jnp.where(row == 0, f_low, pltpu.roll(f, 1, 0)))
    x_high = scaling * jnp.minimum(f, jnp.where(row == 31, f_high, pltpu.roll(f, 31, 0)))
    y_low = scaling * jnp.where(lane < 32, 0.0, jnp.minimum(f, pltpu.roll(f, 32, 1)))
    y_high = scaling * jnp.where(lane >= 992, 0.0, jnp.minimum(f, pltpu.roll(f, 992, 1)))
    z_low = scaling * jnp.where(depth == 0, 0.0, jnp.minimum(f, pltpu.roll(f, 1, 1)))
    z_high = scaling * jnp.where(depth == 31, 0.0, jnp.minimum(f, pltpu.roll(f, 1023, 1)))
    everything = x_low + x_high + y_low + y_high + z_low + z_high
    kinds = [x_low, x_high, y_low, y_high, z_low, z_high, everything, 1.0 - ADVECT * x_high, ADVECT * x_low]
    for k, kind in enumerate(kinds):
        for t in range(8):
            coef[k, t] = kind[:, 128 * t : 128 * t + 128]


def advance(cells, coef, reacted, rates, spread, store, layers=None, parts=None):
    lane = iota((8, 128), 1)

    def react(n, to):
        block = jnp.concatenate([cells[:, 2 * n + 1 + h, 8:40, :].reshape(256, 128) for h in range(2)], axis=1)
        high, low = halves(block)
        out = dot(rates[0], high) + dot(rates[1], high) + dot(rates[0], low)
        for h in range(2):
            to[:, h] = out[:, 128 * h : 128 * h + 128].reshape(8, 32, 128)
        if layers is not None:
            rows = layers[0, pl.ds(pl.multiple_of(256 * n, 256), 256), :]
            parts[n] = dot(high, rows) + dot(low, rows)

    def add(t, term):
        for xt in range(4):
            kinds = [coef[k, t, 8 * xt : 8 * xt + 8, :] for k in range(9)]
            x_low, x_high, y_low, y_high, z_low, z_high, everything, own, upwind = kinds
            at = 8 + 8 * xt
            for s in range(8):
                c = cells[s, t + 1, at : at + 8, :]
                below = cells[s, t + 1, at - 1 : at + 7, :]
                above = cells[s, t + 1, at + 1 : at + 9, :]
                left = pltpu.roll(jnp.where(lane >= 96, cells[s, t, at : at + 8, :], c), 32, 1)
                right = pltpu.roll(jnp.where(lane < 32, cells[s, t + 2, at : at + 8, :], c), 96, 1)
                change = x_low * below + x_high * above + y_low * left + y_high * right
                change = change + z_low * pltpu.roll(c, 1, 1) + z_high * pltpu.roll(c, 127, 1)
                change = change - everything * c
                result = own * c + upwind * below + spread[s] * change
                store(s, t, xt, result + term[s, 8 * xt : 8 * xt + 8, :])

    now, later = reacted
    react(0, now)

    def pair(m, carry):
        react(2 * m + 1, later)
        for h in range(2):
            add(4 * m + h, now.at[:, h])
        react(jnp.minimum(2 * m + 2, 3), now)
        for h in range(2):
            add(4 * m + 2 + h, later.at[:, h])
        return carry

    lax.fori_loop(0, 2, pair, 0)


def clear_rim(cells):
    cells[:, 0] = jnp.zeros((8, 48, 128), F32)
    cells[:, 9] = jnp.zeros((8, 48, 128), F32)
    cells[:, :, 0:8, :] = jnp.zeros((8, 10, 8, 128), F32)
    cells[:, :, 40:48, :] = jnp.zeros((8, 10, 8, 128), F32)


def message_kernel(
    octants, codes, spread_ref, reaction_smem, reaction_ref, boxes, words, sel_x_all, window_z_all, center_all, messages,
    halo_out, rates, box_ref, code_ref, sel_x_ref, window_z_ref, center_ref, message, halo, sems,
):
    def copies(i):
        octant = octants[i]
        pairs = (
            (boxes.at[i], box_ref.at[i]), (words.at[i], code_ref.at[i]), (window_z_all.at[octant // 2], window_z_ref.at[i]),
            (sel_x_all.at[octant], sel_x_ref.at[i]), (center_all.at[octant], center_ref.at[i]),
        )
        return [pltpu.make_async_copy(source, target, sems.at[i, n]) for n, (source, target) in enumerate(pairs)]

    def one_message(i, listed):
        y_half = octants[i] % 2
        box = box_ref.at[pl.ds(i, 1)]
        f = code_ref[i].astype(F32) / LEVELS
        lane = iota((32, 128), 1)
        place = lane % 32
        turn = 32 * (1 + y_half)
        spread = [spread_ref[s] for s in range(8)]

        def window_y(a, b):
            return jnp.where(iota(a.shape, 1) < turn, pltpu.roll(a, turn, 1), pltpu.roll(b, turn, 1))

        around_y = window_y(
            box[0, :, :, 384:512].reshape(256, 128), box[0, :, :, 512:640].reshape(256, 128)
        )
        around_z = pick(box[0].reshape(256, 1024), window_z_ref[i])
        f_windows = (window_y(f[:, 384:512], f[:, 512:640]), pick(f, window_z_ref[i]))
        both = jnp.concatenate([around_y, around_z], axis=1)
        high, low = halves(both)
        reacted = dot(rates[0], high) + dot(rates[1], high) + dot(rates[0], low)
        old_rows, new_rows = [[], []], [[], []]
        for w, (around, fw) in enumerate(zip((around_y, around_z), f_windows)):
            inner = fw[8:24]
            scaling = COARSE_STEP / jnp.maximum(inner, FLOOR)
            x_low = scaling * jnp.minimum(inner, pltpu.roll(fw, 1, 0)[8:24])
            x_high = scaling * jnp.minimum(inner, pltpu.roll(fw, 31, 0)[8:24])
            low_side = scaling * jnp.minimum(inner, pltpu.roll(inner, 32, 1))
            high_side = scaling * jnp.minimum(inner, pltpu.roll(inner, 96, 1))
            before = scaling * jnp.where(place[8:24] == 0, 0.0, jnp.minimum(inner, pltpu.roll(inner, 1, 1)))
            after = scaling * jnp.where(place[8:24] == 31, 0.0, jnp.minimum(inner, pltpu.roll(inner, 127, 1)))
            everything = x_low + x_high + low_side + high_side + before + after
            own = 1.0 - ADVECT * x_high
            upwind = ADVECT * x_low
            for s in range(8):
                rows = around[32 * s : 32 * s + 32]
                c = rows[8:24]
                below = pltpu.roll(rows, 1, 0)[8:24]
                above = pltpu.roll(rows, 31, 0)[8:24]
                change = x_low * below + x_high * above
                change = change + low_side * pltpu.roll(c, 32, 1) + high_side * pltpu.roll(c, 96, 1)
                change = change + before * pltpu.roll(c, 1, 1) + after * pltpu.roll(c, 127, 1) - everything * c
                term = reacted[32 * s + 8 : 32 * s + 24, 128 * w : 128 * w + 128]
                old_rows[w].append(c)
                new_rows[w].append(own * c + upwind * below + spread[s] * change + term)
        fractions = jnp.concatenate([fw[8:24] for fw in f_windows], axis=1)
        sides = [
            jnp.concatenate([jnp.concatenate(part[0], axis=0), jnp.concatenate(part[1], axis=0)], axis=1)
            for part in (old_rows, new_rows)
        ]
        side_parts = pick(jnp.concatenate(sides + [fractions], axis=0), center_ref[i])

        wide = species_column(spread_ref, 1.0, 1024)
        long = iota((1, 1024), 1)
        planes = [box[0, :, x, :] for x in (7, 24)]
        mixed = jnp.dot(
            reaction_ref[...], jnp.concatenate(planes, axis=1), precision=lax.Precision.HIGHEST,
            preferred_element_type=F32,
        )
        new_planes = []
        for n, x in enumerate((7, 24)):
            fx = f[x : x + 1]
            scaling = COARSE_STEP / jnp.maximum(fx, FLOOR)
            x_low = scaling * jnp.minimum(fx, f[x - 1 : x])
            x_high = scaling * jnp.minimum(fx, f[x + 1 : x + 2])
            shifts = ((32, long < 32), (992, long >= 992), (1, long % 32 == 0), (1023, long % 32 == 31))
            c = planes[n]
            below = box[0, :, x - 1, :]
            change = x_low * below + x_high * box[0, :, x + 1, :]
            everything = x_low + x_high
            for amount, wall in shifts:
                factor = scaling * jnp.where(wall, 0.0, jnp.minimum(fx, pltpu.roll(fx, amount, 1)))
                change = change + factor * pltpu.roll(c, amount, 1)
                everything = everything + factor
            change = change - everything * c
            moved = (1.0 - ADVECT * x_high) * c + ADVECT * x_low * below + wide * change
            new_planes.append(moved + COARSE_STEP * mixed[:, 1024 * n : 1024 * n + 1024])
        sublane = iota((8, 1024), 0)
        faces = jnp.where(sublane == 0, f[7:8], jnp.where(sublane == 1, f[24:25], 0.0))
        blank = jnp.zeros((8, 1024), F32)
        x_parts = pick(jnp.concatenate(planes + [faces] + new_planes + [blank], axis=0), sel_x_ref[i])

        message[i, 0:16, :] = x_parts[0:16, 0:128]
        message[i, 16:24, :] = jnp.where(iota((8, 128), 0) == 7, listed, x_parts[16:24, 0:128])
        message[i, 24:48, :] = x_parts[0:24, 128:256]
        message[i, 48:80, :] = pack_rows(side_parts[0:128])
        message[i, 80:96, :] = side_parts[256:272]
        message[i, 96:112, :] = x_parts[24:40, 0:128]
        message[i, 112:128, :] = x_parts[24:40, 128:256]
        message[i, 128:160, :] = pack_rows(side_parts[128:256])

        def put_plane(p, x):
            plane = box[0, :, x, :]
            for t in range(8):
                base = 32 + (p * 8 + t) * 16
                halo[base : base + 8, :] = plane[:, 128 * t : 128 * t + 128]
                halo[base + 8 : base + 16, :] = jnp.broadcast_to(f[x : x + 1, 128 * t : 128 * t + 128], (8, 128))

        @pl.when(i == 0)
        def _():
            put_plane(0, 0)

        @pl.when(i == SLOTS - 1)
        def _():
            put_plane(1, 31)

    @pl.when(lax.axis_index("lev") == 0)
    def _():
        for copy in copies(0):
            copy.start()
        set_rates(rates, reaction_smem, COARSE_STEP)
        where = iota((8, 128), 1)
        listed = jnp.zeros((8, 128), F32)
        for j in range(SLOTS):
            listed = jnp.where(where == j, codes[j].astype(F32), listed)
        halo[...] = jnp.zeros((640, 128), F32)
        halo[16:24, :] = listed

        def result(i):
            return pltpu.make_async_copy(message.at[i], messages.at[i], sems.at[i, 5])

        def each(i, carry):
            @pl.when(i + 1 < SLOTS)
            def _():
                for copy in copies(i + 1):
                    copy.start()

            for copy in copies(i):
                copy.wait()
            one_message(i, listed)
            result(i).start()
            return carry

        lax.fori_loop(0, SLOTS, each, 0)
        last = pltpu.make_async_copy(halo, halo_out, sems.at[0, 0])
        last.start()
        for i in range(SLOTS):
            result(i).wait()
        last.wait()


def early_kernel(
    base, again, octants, fine_octants, counts, spread_ref, reaction_smem, box, code, before, code_before, after,
    code_after, sel_x, sel_yz, layers, mean_x, couple, *refs,
):
    states, register, edges, ends, average, cells, later, coef, now, then, rates, parts = refs[5 * again :]
    i = pl.program_id(0)
    at = base + i
    coarse = lax.axis_index("lev") == 0
    used = coarse | (at < counts[0])

    @pl.when(jnp.logical_not(used))
    def _():
        states[0] = box[0]

    @pl.when(used)
    def _():
        @pl.when(i == 0)
        def _():
            set_rates(rates, reaction_smem, jnp.where(coarse, COARSE_STEP, 0.5 * COARSE_STEP))
            clear_rim(cells)
            clear_rim(later)

        f = code[0].astype(F32) / LEVELS
        f_before = jnp.where(coarse & (at > 0), code_before[0, 7:8, :].astype(F32) / LEVELS, 0.0)
        f_after = jnp.where(coarse & (at < SLOTS - 1), code_after[0, 0:1, :].astype(F32) / LEVELS, 0.0)
        load_cells(cells, box[0])
        for t in range(8):
            cells[:, t + 1, 7, :] = before[0, :, 7, 128 * t : 128 * t + 128]
            cells[:, t + 1, 40, :] = after[0, :, 0, 128 * t : 128 * t + 128]
        prepare(f, f_before, f_after, coef, COARSE_STEP)

        def store(s, t, xt, value):
            states[0, s, 8 * xt : 8 * xt + 8, pl.ds(pl.multiple_of(128 * t, 128), 128)] = value

        def store_later(s, t, xt, value):
            later[s, t + 1, 8 + 8 * xt : 16 + 8 * xt, :] = value

        @pl.when(coarse)
        def _():
            spread = [spread_ref[s] for s in range(8)]
            advance(cells, coef, (now, then), rates, spread, store)
            octant = octants[at]
            y_half = octant % 2
            z_half = octant // 2
            wide = species_column(spread_ref, 1.0, 1024)
            c7, c8 = box[0, :, 7, :], box[0, :, 8, :]
            c23, c24 = box[0, :, 23, :], box[0, :, 24, :]
            low_flux = -jnp.minimum(f[7:8], f[8:9]) * (ADVECT * c7 - wide * (c8 - c7))
            high_flux = jnp.minimum(f[23:24], f[24:25]) * (ADVECT * c23 - wide * (c24 - c23))
            x_parts = pick(jnp.concatenate([low_flux, high_flux], axis=0), sel_x[0])

            lane = iota((1, 1024), 1)
            y_row = lane // 32 == 16 - y_half
            y_roll = jnp.where(y_half == 0, 32, 992)
            z_roll = jnp.where(z_half == 0, 1, 1023)
            middle = f[8:24]
            inner_f = jnp.where(y_row, pltpu.roll(middle, y_roll, 1), pltpu.roll(middle, z_roll, 1))
            weight = -jnp.minimum(middle, inner_f)
            fluxes = []
            for s in range(8):
                c = box[0, s, 8:24, :]
                inner = jnp.where(y_row, pltpu.roll(c, y_roll, 1), pltpu.roll(c, z_roll, 1))
                fluxes.append(spread[s] * weight * (c - inner))
            side_parts = pick(jnp.concatenate(fluxes, axis=0), sel_yz[0])
            register[0, 0:16, :] = x_parts[:, 0:128]
            register[0, 16:32, :] = x_parts[:, 128:256]
            register[0, 32:64, :] = pack_rows(side_parts)

        @pl.when(jnp.logical_not(coarse))
        def _():
            spread = [spread_ref[s] * 2.0 for s in range(8)]
            advance(cells, coef, (now, then), rates, spread, store_later, layers, parts)
            edges[0, 0:256] = parts[0] + parts[1] + parts[2] + parts[3]
            advance(later, coef, (now, then), rates, spread, store, layers, parts)
            edges[0, 256:512] = parts[0] + parts[1] + parts[2] + parts[3]
            edges[0, 512:544] = pick(f, layers[0])
            ends[0, 0:8] = box[0, :, 0, :]
            ends[0, 8:16] = box[0, :, 31, :]
            for t in range(8):
                ends[0, 16:24, 128 * t : 128 * t + 128] = later[:, t + 1, 8, :]
                ends[0, 24:32, 128 * t : 128 * t + 128] = later[:, t + 1, 39, :]
            average[0] = 0.5 * left_pick(couple[...], pick(states[0].reshape(256, 1024), mean_x[...]))


def interface_kernel(
    parents, octants, counts, spread_ref, reaction_smem, reaction_ref, words, edges_all, ends_all, average_all, up_x_all,
    up_layer_all, twice_all, mean_x_all, mean_layer_all, couple_all, layers_all, layers_t_all, mean_layers_all,
    own, near_a, near_b, other, other_a, other_b, started, states, payloads, codes, rates, messages, taken, coarse,
    first, code, edges, ends, average, up_x, up_layer, twice, mean_x, mean_layer, couple, layers, layers_t, mean_layers,
    rim, payload, sems, fixed_sems,
):
    column = lax.axis_index("box")
    lists = [
        pltpu.make_async_copy(source.at[0, 16:24], codes.at[n], fixed_sems.at[n])
        for n, source in enumerate((near_a, own, near_b))
    ]
    turn_step = 1 - 2 * ((column >> 1) & 1)
    fixed = [
        pltpu.make_async_copy(source, target, fixed_sems.at[3 + n])
        for n, (source, target) in enumerate((
            (up_x_all, up_x), (up_layer_all, up_layer), (twice_all, twice), (mean_x_all, mean_x),
            (mean_layer_all, mean_layer), (couple_all, couple),
        ))
    ]

    def copies(n, last):
        octant = octants[n]
        pairs = (
            (words, code, n), (edges_all, edges, n), (ends_all, ends, n), (average_all, average, n),
            (layers_all, layers, octant), (layers_t_all, layers_t, octant), (mean_layers_all, mean_layers, octant),
            (started, first, n),
        )
        return [
            pltpu.make_async_copy(source.at[index], target.at[n], sems.at[n, k])
            for k, (source, target, index) in enumerate(pairs)
            if last is None or last == (k == 7)
        ]

    def message_copy(source, box, n):
        return pltpu.make_async_copy(source.at[box], messages.at[n], sems.at[n, 8])

    def result_copies(n):
        return [
            pltpu.make_async_copy(first.at[n], states.at[n], sems.at[n, 9]),
            pltpu.make_async_copy(payload.at[:, n], payloads.at[:, n], sems.at[n, 10]),
        ]

    for copy in lists:
        copy.start()

    def row_ends():
        odd = (column & 1) == 1
        wide = species_column(spread_ref, 1.0, 128)
        ends_at = ((0, 0), (SLOTS - 1, 24))
        loads = [pltpu.make_async_copy(own.at[pl.ds(0, 2)], rim.at[0], sems.at[0, 0])]
        for p, (box, x) in enumerate(ends_at):
            loads.append(pltpu.make_async_copy(words.at[box, pl.ds(x, 8)], code.at[p, pl.ds(0, 8)], sems.at[1, p]))
            loads.append(pltpu.make_async_copy(states.at[box, :, pl.ds(x, 8)], first.at[p, :, pl.ds(0, 8)], sems.at[2, p]))
        for p, step in enumerate((-1, 1)):
            inside = odd if p == 0 else jnp.logical_not(odd)
            for source, there in (
                (other, inside), (other_a, jnp.logical_not(inside) & (turn_step == step)),
                (other_b, jnp.logical_not(inside) & (turn_step != step)),
            ):

                @pl.when(there)
                def _():
                    pltpu.make_async_copy(source.at[pl.ds(0, 2)], rim.at[1 + p], sems.at[3, p]).start()

        for copy in loads:
            copy.start()
        for copy in loads:
            copy.wait()
        saves = []
        for p, (box, x) in enumerate(ends_at):
            pltpu.make_async_copy(other.at[pl.ds(0, 2)], rim.at[1 + p], sems.at[3, p]).wait()
            at = 7 * p
            f = code[p, at : at + 1, :].astype(F32) / LEVELS
            scaling = COARSE_STEP / jnp.maximum(f, FLOOR)
            for t in range(8):
                part = slice(128 * t, 128 * t + 128)
                here = 32 + (p * 8 + t) * 16
                there = 32 + ((1 - p) * 8 + t) * 16
                c = rim[0, here // 160, here % 160 : here % 160 + 8, :]
                g = rim[1 + p, there // 160, there % 160 : there % 160 + 8, :]
                g_f = rim[1 + p, there // 160, there % 160 + 8 : there % 160 + 9, :]
                m = jnp.minimum(f[:, part], g_f)
                if p == 0:
                    gain = m * (ADVECT * g - wide * (c - g))
                else:
                    gain = -m * (ADVECT * c - wide * (g - c))
                first[p, :, at, part] += scaling[:, part] * gain
            saves.append(
                pltpu.make_async_copy(first.at[p, :, pl.ds(0, 8)], states.at[box, :, pl.ds(x, 8)], sems.at[2, p])
            )
            saves[-1].start()
        for copy in saves:
            copy.wait()

    pl.when(lax.axis_index("lev") == 0)(row_ends)

    def fetch(n):
        for copy in copies(n, None):
            copy.start()
        home = parents[n] // SLOTS
        away = (home >> 1) - (column >> 1)
        same = ((home - column) & 1) == 0
        for source, is_same, step in (
            (near_a, True, turn_step), (own, True, 0), (near_b, True, -turn_step),
            (other_a, False, turn_step), (other, False, 0), (other_b, False, -turn_step),
        ):

            @pl.when((same == is_same) & (away == step))
            def _():
                message_copy(source, parents[n] % SLOTS, n).start()

    def one_slot(i, carry):
        @pl.when(i + 1 < counts[0])
        def _():
            fetch(i + 1)

        for copy in copies(i, False):
            copy.wait()
        message_copy(own, 0, i).wait()
        chosen = messages.at[i]
        octant = octants[i]
        y_half = octant % 2
        z_half = octant // 2
        spread = [spread_ref[s] * 2.0 for s in range(8)]
        wide = species_column(spread_ref, 2.0, 1024)
        f = code[i].astype(F32) / LEVELS

        x_old = jnp.concatenate([chosen[0:24], chosen[24:48]], axis=1)
        x_new = jnp.concatenate([chosen[96:112], chosen[112:128]], axis=1)
        x_mid = 0.5 * (x_old[0:16] + x_new)
        ghosts = pick(jnp.concatenate([x_old, x_mid, jnp.zeros((8, 256), F32)], axis=0), up_x[...])
        side_old = chosen[48:80]
        side_mid = 0.5 * (side_old + chosen[128:160])

        def side_ghosts(side):
            high, low = halves(unpack_rows(side))
            high = dot(twice[...], high).astype(BF16)
            low = dot(twice[...], low).astype(BF16)
            return dot(high, up_layer[...]) + dot(low, up_layer[...])

        ghost_old = side_ghosts(side_old)
        ghost_mid = side_ghosts(side_mid)
        high, low = halves(jnp.where(iota((16, 128), 1) < 32, chosen[80:96], 0.0))
        high = dot(twice[0:32, 0:16], high).astype(BF16)
        low = dot(twice[0:32, 0:16], low).astype(BF16)
        f_ghost = dot(high, up_layer[...]) + dot(low, up_layer[...])

        lane = iota((32, 128), 1)
        row = iota((32, 128), 0)
        face = lane // 32 % 2 == 0
        place = lane % 32
        fl = edges[i, 512:544]
        scaling = COARSE_STEP / jnp.maximum(fl, FLOOR)
        at_face = jnp.where(face, scaling, 0.0)
        through = jnp.where(face, jnp.minimum(fl, f_ghost), 0.0)
        x_low = at_face * jnp.where(row == 0, 0.0, jnp.minimum(fl, pltpu.roll(fl, 1, 0)))
        x_high = at_face * jnp.where(row == 31, 0.0, jnp.minimum(fl, pltpu.roll(fl, 31, 0)))
        t_low = at_face * jnp.where(place == 0, 0.0, jnp.minimum(fl, pltpu.roll(fl, 1, 1)))
        t_high = at_face * jnp.where(place == 31, 0.0, jnp.minimum(fl, pltpu.roll(fl, 127, 1)))
        behind = at_face * jnp.minimum(fl, pltpu.roll(fl, 96, 1))
        ahead = jnp.where(face, 0.0, scaling * jnp.minimum(fl, pltpu.roll(fl, 32, 1)))
        everything = x_low + x_high + t_low + t_high + behind
        own_part = 1.0 - ADVECT * x_high
        upwind = ADVECT * x_low
        flux_one = []
        for s in range(8):
            part = slice(32 * s, 32 * s + 32)
            q = through * (ghost_old[part] - edges[i, part])
            flux_one.append(q)
            taken[s] = spread[s] * (scaling * q)

        long = iota((1, 1024), 1)
        f_low, f_high = ghosts[16:17], ghosts[17:18]
        m_low = jnp.minimum(f[0:1], f_low)
        m_high = jnp.minimum(f[31:32], f_high)
        scale_low = COARSE_STEP / jnp.maximum(f[0:1], FLOOR)
        scale_high = COARSE_STEP / jnp.maximum(f[31:32], FLOOR)

        def end_fluxes(low, high, c_low, c_high):
            low_flux = -m_low * (ADVECT * low - wide * (c_low - low))
            high_flux = m_high * (ADVECT * c_high - wide * (high - c_high))
            return low_flux, high_flux

        low_one, high_one = end_fluxes(ghosts[0:8], ghosts[8:16], ends[i, 0:8], ends[i, 8:16])
        end_low = -scale_low * low_one
        end_high = -scale_high * high_one

        crossed = pick(jnp.concatenate([taken[:, 0, :], taken[:, 31, :]], axis=0), layers[i])
        ends_there = pick(jnp.concatenate([end_low, end_high], axis=0), layers_t[i])
        corner_y = jnp.where(z_half == 1, 0, 31)
        corner_z = 64 + jnp.where(y_half == 1, 0, 31)
        turn = corner_y - corner_z + 128
        back = corner_z - corner_y
        flux_two = []
        for s in range(8):
            part = slice(32 * s, 32 * s + 32)
            v = taken[s]
            c = edges[i, 256 + 32 * s : 288 + 32 * s] + v
            c = c + jnp.where(lane == corner_y, pltpu.roll(v, turn, 1), 0.0)
            c = c + jnp.where(lane == corner_z, pltpu.roll(v, back, 1), 0.0)
            c = c + jnp.where(row == 0, ends_there[s : s + 1], jnp.where(row == 31, ends_there[8 + s : 9 + s], 0.0))
            flux_two.append(through * (ghost_mid[part] - c))
        low_two, high_two = end_fluxes(
            ghosts[24:32], ghosts[32:40], ends[i, 16:24] + end_low + crossed[0:8],
            ends[i, 24:32] + end_high + crossed[8:16],
        )

        high, low = halves(taken[...].reshape(256, 128))
        mixed = dot(rates[0], high) + dot(rates[1], high) + dot(rates[0], low)
        totals = []
        for s in range(8):
            v = taken[s]
            below = pltpu.roll(v, 1, 0)
            change = x_low * below + x_high * pltpu.roll(v, 31, 0)
            change = change + t_low * pltpu.roll(v, 1, 1) + t_high * pltpu.roll(v, 127, 1)
            change = change + ahead * pltpu.roll(v, 32, 1) - everything * v + scaling * flux_two[s]
            totals.append(own_part * v + upwind * below + spread[s] * change + mixed[32 * s : 32 * s + 32])
        total = jnp.concatenate(totals, axis=0)

        def tangential(c, fx, scale, inner):
            change = jnp.zeros_like(c)
            everything = inner
            for amount, wall in ((32, long < 32), (992, long >= 992), (1, long % 32 == 0), (1023, long % 32 == 31)):
                factor = scale * jnp.where(wall, 0.0, jnp.minimum(fx, pltpu.roll(fx, amount, 1)))
                change = change + factor * pltpu.roll(c, amount, 1)
                everything = everything + factor
            return change - everything * c

        end_mixed = 0.5 * COARSE_STEP * jnp.dot(
            reaction_ref[...], jnp.concatenate([end_low, end_high], axis=1), precision=lax.Precision.HIGHEST,
            preferred_element_type=F32,
        )
        inner_low = jnp.minimum(f[0:1], f[1:2])
        inner_high = jnp.minimum(f[30:31], f[31:32])
        row0 = (1.0 - ADVECT * (scale_low * inner_low)) * end_low - scale_low * low_two + end_mixed[:, 0:1024]
        row0 = row0 + wide * tangential(end_low, f[0:1], scale_low, scale_low * inner_low)
        row1 = (wide + ADVECT) * (COARSE_STEP / jnp.maximum(f[1:2], FLOOR) * inner_low) * end_low
        row30 = wide * (COARSE_STEP / jnp.maximum(f[30:31], FLOOR) * inner_high) * end_high
        row31 = end_high - scale_high * high_two + end_mixed[:, 1024:2048]
        row31 = row31 + wide * tangential(end_high, f[31:32], scale_high, scale_high * inner_high)

        @pl.when(i == 0)
        def _():
            for copy in fixed[3:]:
                copy.wait()

        x_parts = pick(
            jnp.concatenate([low_one + low_two, high_one + high_two, row0 + row1, row30 + row31], axis=0), mean_x[...]
        )
        coarse[...] = (average[i] + 0.5 * left_pick(couple[...], pick(total, mean_layers[i]))).reshape(8, 16, 256)
        coarse[:, 0, :] += 0.5 * x_parts[16:24]
        coarse[:, 15, :] += 0.5 * x_parts[24:32]
        for q in range(3):
            payload[q, i] = coarse[...].reshape(128, 256)[40 * q : 40 * q + 40]
        payload[3, i, 0:8] = coarse[...].reshape(128, 256)[120:128]
        payload[3, i, 8:24] = 0.5 * x_parts[0:16]
        fluxes = jnp.concatenate([flux_one[s] + flux_two[s] for s in range(8)], axis=0)
        sides = left_pick(couple[...], pick(fluxes, mean_layer[...])).reshape(8, 16, 128)
        sides = jnp.concatenate([(-0.5 * spread[s]) * sides[s] for s in range(8)], axis=0)
        sides = pack_rows(sides)
        payload[3, i, 24:40, 0:128] = sides[0:16]
        payload[3, i, 24:40, 128:256] = sides[16:32]

        copies(i, True)[0].wait()
        high, low = halves(total)
        for n in range(4):
            part = slice(256 * n, 256 * n + 256)
            added = dot(high, layers[i, :, part]) + dot(low, layers[i, :, part])
            first[i, :, :, part] += added.reshape(8, 32, 256)
        first[i, :, 0, :] += row0
        first[i, :, 1, :] += row1
        first[i, :, 30, :] += row30
        first[i, :, 31, :] += row31
        for copy in result_copies(i):
            copy.start()
        return carry

    @pl.when(counts[0] > 0)
    def _():
        fetch(0)
        for copy in fixed:
            copy.start()
        set_rates(rates, reaction_smem, 0.5 * COARSE_STEP)
        for copy in fixed[:3]:
            copy.wait()
        lax.fori_loop(0, counts[0], one_slot, 0)
        for n in range(SLOTS):

            @pl.when(n < counts[0])
            def _():
                for copy in result_copies(n):
                    copy.wait()

    for copy in lists:
        copy.wait()


def decode(code):
    safe = jnp.maximum(code, 0)
    return safe // (OFFSETS * SLOTS) + 1, safe // SLOTS % OFFSETS - REACH, safe % SLOTS


def route_kernel(codes, mine, others, to_a, stay, to_b):
    column = lax.axis_index("box")
    turn_step = 1 - 2 * ((column >> 1) & 1)
    for n, (step, target) in enumerate(((turn_step, to_a), (0, stay), (-turn_step, to_b))):
        for j in range(SLOTS):
            row, offset, slot = decode(codes[n, 7, j].astype(jnp.int32))
            child = column + 2 * step + offset
            target[j] = jnp.where(((child - column) & 1) == 0, mine[row, slot], others[row, slot])


def choose_kernel(codes, from_a, stay, from_b, chosen):
    column = lax.axis_index("box")
    turn_step = 1 - 2 * ((column >> 1) & 1)
    for j in range(SLOTS):
        _, offset, _ = decode(codes[j])
        away = ((column + offset) >> 1) - (column >> 1)
        chosen[0, j] = jnp.where(away == turn_step, from_a[j], jnp.where(away == 0, stay[j], from_b[j]))


def finish_kernel(
    octants, codes, message, register, parts, fill, z_column, y_row, updated, states, window, beside, sems
):
    def copies(i, out):
        y_half = octants[i] % 2
        pairs = (
            (pl.ds(pl.multiple_of(512 * y_half, 512), 512), window.at[i]),
            (pl.ds(pl.multiple_of(512 - 128 * y_half, 128), 128), beside.at[i]),
        )
        result = []
        for n, (lanes, here) in enumerate(pairs):
            there = states.at[i, :, :, lanes]
            source, target = (here, there) if out else (there, here)
            result.append(pltpu.make_async_copy(source, target, sems.at[i, n]))
        return result

    def one_box(i):
        octant = octants[i]
        z_half = octant // 2
        inside = iota((1, 512), 1) % 32 // 16 == z_half
        own_f = jnp.concatenate([message[i, 0:24, :], message[i, 24:48, :]], axis=1)
        x_f = jnp.where(iota((16, 256), 0) < 8, own_f[16:17], own_f[17:18])
        reg_x = jnp.concatenate([register[i, 0:16, :], register[i, 16:32, :]], axis=1)
        fix_x = COARSE_STEP / jnp.maximum(x_f, FLOOR) * (parts[3, i, 8:24, :] - reg_x)
        side_f = jnp.concatenate([message[i, 80:96, :]] * 2, axis=0)
        sides = jnp.concatenate([parts[3, i, 24:40, 0:128], parts[3, i, 24:40, 128:256]], axis=0)
        fix_sides = unpack_rows(COARSE_STEP / jnp.maximum(side_f, FLOOR) * (sides - register[i, 32:64, :]))
        average = jnp.concatenate([parts[q, i] for q in range(3)] + [parts[3, i, 0:8, :]], axis=0)
        planes = pick(fix_x, fill[z_half])
        filled = pick(average, fill[z_half])
        along = pick(fix_sides, z_column[z_half])
        across = pick(fix_sides, y_row[octant])
        for copy in copies(i, False):
            copy.wait()
        window[i, :, 7, :] += planes[0:8]
        window[i, :, 24, :] += planes[8:16]
        for s in range(8):
            part = slice(16 * s, 16 * s + 16)
            window[i, s, 8:24, :] = jnp.where(inside, filled[part], window[i, s, 8:24, :] + along[part])
            beside[i, s, 8:24, :] += across[part]
        for copy in copies(i, True):
            copy.start()

    def each(act):
        for i in range(SLOTS):

            @pl.when(codes[i] >= 0)
            def _():
                act(i)

    @pl.when(lax.axis_index("lev") == 0)
    def _():
        each(lambda i: [copy.start() for copy in copies(i, False)])
        each(one_box)
        each(lambda i: [copy.wait() for copy in copies(i, True)])


def per_device(
    box_states, cell_code, diffusivity, reaction, coarse_child, coarse_octant, fine_parent, fine_octant, fine_count
):
    row = lax.axis_index("lev")
    count = lax.axis_size("box")
    swap = [(i, i ^ 1) for i in range(count)]
    round_a = [(i, i ^ 2) for i in range(count)]
    round_b = [(i, ((i + 2) ^ 2) - 2) for i in range(2, count - 2)]
    vmem = pltpu.CompilerParams(vmem_limit_bytes=62 * 1024 * 1024)
    small = pltpu.CompilerParams(vmem_limit_bytes=8 * 1024 * 1024)

    def whole(a):
        zeros = (0,) * a.ndim
        return pl.BlockSpec(a.shape, lambda i, *_: zeros)

    def each(shape):
        tail = (0,) * len(shape)
        return pl.BlockSpec((1,) + shape, lambda i, *_: (i,) + tail)

    smem = pl.BlockSpec(memory_space=pltpu.SMEM)
    hbm = pl.BlockSpec(memory_space=pl.ANY)
    in_vmem = pl.BlockSpec(memory_space=pltpu.VMEM)
    previous = lambda i: jnp.maximum(i - 1, 0)
    following = lambda i: jnp.minimum(i + 1, SLOTS - 1)
    shape = jax.ShapeDtypeStruct
    sel_x, sel_yz = table(SEL_X), table(SEL_YZ)
    by_octant = lambda i, octants, *_: (octants[i], 0, 0)

    message, halo = pl.pallas_call(
        message_kernel,
        in_specs=[smem] * 4 + [in_vmem] + [hbm] * 5,
        out_specs=[hbm, hbm],
        scratch_shapes=[
            pltpu.VMEM((2, 256, 256), BF16),
            pltpu.VMEM((SLOTS, 8, 32, 1024), F32),
            pltpu.VMEM((SLOTS, 32, 1024), jnp.int32),
            pltpu.VMEM((SLOTS, 1024, 256), BF16),
            pltpu.VMEM((SLOTS, 1024, 128), BF16),
            pltpu.VMEM((SLOTS, 256, 128), BF16),
            pltpu.VMEM((SLOTS, 160, 128), F32),
            pltpu.VMEM((640, 128), F32),
            pltpu.SemaphoreType.DMA((SLOTS, 6)),
        ],
        out_shape=[shape((SLOTS, 160, 128), F32), shape((640, 128), F32)],
        compiler_params=vmem,
        name="shells",
    )(
        coarse_octant, coarse_child, diffusivity, reaction, reaction, box_states, cell_code, sel_x, table(WINDOW_Z),
        table(CENTER),
    )

    mean_x, couple = table(0.25 * UP_X.T), table(TWICE.T)
    layers, layers_t = table(LAYERS), table(LAYERS.transpose(0, 2, 1))

    def early(base, boxes, *carried):
        def at(dims):
            tail = (0,) * len(dims)
            return pl.BlockSpec((1,) + dims, lambda i, *_: (base + i,) + tail)

        def for_octant(dims):
            return pl.BlockSpec((1,) + dims, lambda i, octants, *_: (octants[base + i], 0, 0))

        blocks = [(8, 32, 1024), (64, 128), (544, 128), (32, 1024), (128, 256)]
        return pl.pallas_call(
            functools.partial(early_kernel, base, len(carried) > 0),
            grid_spec=pltpu.PrefetchScalarGridSpec(
                num_scalar_prefetch=3,
                grid=(boxes,),
                in_specs=[
                    smem,
                    smem,
                    at((8, 32, 1024)),
                    at((32, 1024)),
                    pl.BlockSpec((1, 8, 8, 1024), lambda i, *_: (previous(base + i), 0, 3, 0)),
                    pl.BlockSpec((1, 8, 1024), lambda i, *_: (previous(base + i), 3, 0)),
                    pl.BlockSpec((1, 8, 8, 1024), lambda i, *_: (following(base + i), 0, 0, 0)),
                    pl.BlockSpec((1, 8, 1024), lambda i, *_: (following(base + i), 0, 0)),
                    for_octant((1024, 256)),
                    for_octant((1024, 128)),
                    pl.BlockSpec((1, 1024, 128), lambda i, octants, fine, *_: (fine[base + i], 0, 0)),
                    whole(mean_x),
                    whole(couple),
                ]
                + [hbm] * len(carried),
                out_specs=[at(dims) for dims in blocks],
                scratch_shapes=[
                    pltpu.VMEM((8, 10, 48, 128), F32),
                    pltpu.VMEM((8, 10, 48, 128), F32),
                    pltpu.VMEM((9, 8, 32, 128), F32),
                    pltpu.VMEM((8, 2, 32, 128), F32),
                    pltpu.VMEM((8, 2, 32, 128), F32),
                    pltpu.VMEM((2, 256, 256), BF16),
                    pltpu.VMEM((4, 256, 128), F32),
                ],
            ),
            out_shape=[shape((SLOTS,) + dims, F32) for dims in blocks],
            input_output_aliases={16 + n: n for n in range(len(carried))},
            compiler_params=vmem,
            cost_estimate=pl.CostEstimate(flops=10**9, bytes_accessed=30 * 10**6, transcendentals=0),
            name=f"early_{base}",
        )(
            coarse_octant, fine_octant, fine_count, diffusivity, reaction, box_states, cell_code, box_states, cell_code,
            box_states, cell_code, sel_x, sel_yz, layers_t, mean_x, couple, *carried,
        )

    updated, *carried = early(0, 3)
    spread_out = [lax.ppermute(message, "lev", [(0, r)]) for r in (1, 3, 2)]
    *spread_out, updated = lax.optimization_barrier((*spread_out, updated))
    own = jnp.where(row == 0, halo.reshape(SLOTS, 160, 128), spread_out[0] + spread_out[1] + spread_out[2])
    near_a = lax.ppermute(own, "box", round_a)
    near_b = lax.ppermute(own, "box", round_b)
    updated, register, *carried = early(3, 1, updated, *carried)
    near_a, near_b, updated = lax.optimization_barrier((near_a, near_b, updated))
    other = lax.ppermute(own, "box", swap)
    other_a = lax.ppermute(near_a, "box", swap)
    other_b = lax.ppermute(near_b, "box", swap)

    up_x, up_layer, twice, mean_layer = table(UP_X), table(UP_LAYER), table(TWICE), table(0.25 * UP_LAYER.T)
    mean_layers = table(LAYERS @ (0.25 * UP_X.T))
    constants = [up_x, up_layer, twice, mean_x, mean_layer, couple]
    states, payload, codes = pl.pallas_call(
        interface_kernel,
        in_specs=[smem] * 5 + [in_vmem] + [hbm] * 20,
        out_specs=[hbm, hbm, smem],
        scratch_shapes=[
            pltpu.VMEM((2, 256, 256), BF16),
            pltpu.VMEM((SLOTS, 160, 128), F32),
            pltpu.VMEM((8, 32, 128), F32),
            pltpu.VMEM((8, 16, 256), F32),
            pltpu.VMEM((SLOTS, 8, 32, 1024), F32),
            pltpu.VMEM((SLOTS, 32, 1024), jnp.int32),
            pltpu.VMEM((SLOTS, 544, 128), F32),
            pltpu.VMEM((SLOTS, 32, 1024), F32),
            pltpu.VMEM((SLOTS, 128, 256), F32),
        ]
        + [pltpu.VMEM(a.shape, BF16) for a in constants]
        + [
            pltpu.VMEM((SLOTS, 128, 1024), BF16),
            pltpu.VMEM((SLOTS, 1024, 128), BF16),
            pltpu.VMEM((SLOTS, 128, 256), BF16),
            pltpu.VMEM((3, 2, 160, 128), F32),
            pltpu.VMEM((4, SLOTS, 40, 256), F32),
            pltpu.SemaphoreType.DMA((SLOTS, 11)),
            pltpu.SemaphoreType.DMA((9,)),
        ],
        out_shape=[
            shape((SLOTS, 8, 32, 1024), F32), shape((4, SLOTS, 40, 256), F32), shape((3, 8, 128), F32)
        ],
        input_output_aliases={25: 0},
        compiler_params=vmem,
        name="interfaces",
    )(
        fine_parent, fine_octant, fine_count, diffusivity, reaction, reaction, cell_code, *carried, *constants, layers,
        layers_t, mean_layers, own, near_a, near_b, other, other_a, other_b, updated,
    )

    mine = lax.all_to_all(payload, "lev", 0, 0)
    others = lax.ppermute(mine, "box", swap)
    bundle = shape((SLOTS, 40, 256), F32)
    to_a, stay, to_b = pl.pallas_call(
        route_kernel,
        in_specs=[smem] + [in_vmem] * 2,
        out_specs=[in_vmem] * 3,
        out_shape=[bundle] * 3,
        compiler_params=small,
        name="route",
    )(codes, mine, others)
    from_a = lax.ppermute(to_a, "box", round_a)
    from_b = lax.ppermute(to_b, "box", round_b)
    quarter = pl.pallas_call(
        choose_kernel,
        in_specs=[smem] + [in_vmem] * 3,
        out_specs=in_vmem,
        out_shape=shape((4, SLOTS, 40, 256), F32),
        compiler_params=small,
        name="choose",
    )(coarse_child, from_a, stay, from_b)
    parts = lax.all_to_all(quarter, "lev", 0, 0)

    return pl.pallas_call(
        finish_kernel,
        in_specs=[smem] * 2 + [in_vmem] * 6 + [hbm],
        out_specs=hbm,
        scratch_shapes=[
            pltpu.VMEM((SLOTS, 8, 32, 512), F32),
            pltpu.VMEM((SLOTS, 8, 32, 128), F32),
            pltpu.SemaphoreType.DMA((SLOTS, 2)),
        ],
        out_shape=shape((SLOTS, 8, 32, 1024), F32),
        input_output_aliases={8: 0},
        compiler_params=pltpu.CompilerParams(vmem_limit_bytes=24 * 1024 * 1024),
        name="finish",
    )(coarse_octant, coarse_child, message, register, parts, table(FILL), table(Z_COLUMN), table(Y_ROW), states)


def solution(mesh):
    return jax.shard_map(
        per_device,
        mesh=mesh,
        in_specs=(
            P(("lev", "box"), None, None, None),
            P(("lev", "box"), None, None),
            P(),
            P(),
            P("box"),
            P("box"),
            P(("lev", "box")),
            P(("lev", "box")),
            P(("lev", "box")),
        ),
        out_specs=P(("lev", "box"), None, None, None),
        check_vma=False,
    )
```

```python
import functools

import jax
import jax.numpy as jnp
import numpy as np
from jax import lax
from jax.experimental import pallas as pl
from jax.experimental.pallas import tpu as pltpu
from jax.sharding import PartitionSpec as P

ADVECT = 0.4
COARSE_STEP = 0.5
FLOOR = 0.5
LEVELS = 15.0
SLOTS = 4
REACH = 2
OFFSETS = 2 * REACH + 1
F32 = jnp.float32
BF16 = jnp.bfloat16


def selection_tables():
    lane = np.arange(1024)
    y, z = lane // 32, lane % 32
    place = np.arange(256)
    a, b = place // 16, place % 16
    i = np.arange(16)
    sel_x = np.zeros((4, 1024, 256), np.float32)
    sel_yz = np.zeros((4, 1024, 128), np.float32)
    for octant in range(4):
        y_half, z_half = octant % 2, octant // 2
        sel_x[octant, (16 * y_half + a) * 32 + 16 * z_half + b, place] = 1
        for g in range(4):
            sel_yz[octant, (16 - y_half) * 32 + 16 * z_half + i, 32 * g + i] = 1
            sel_yz[octant, (16 * y_half + i) * 32 + 16 - z_half, 32 * g + 16 + i] = 1
    up_x = np.zeros((256, 1024), np.float32)
    up_x[(y // 2) * 16 + z // 2, lane] = 1
    twice = np.zeros((256, 128), np.float32)
    rows = np.arange(256)
    twice[rows, rows // 32 * 16 + rows % 32 // 2] = 1
    window_z = np.zeros((2, 1024, 128), np.float32)
    for z_half in range(2):
        for step in range(3):
            rows = np.arange(32)
            window_z[z_half, rows * 32 + 15 - z_half + step, step * 32 + rows] = 1
    center = np.zeros((4, 256, 128), np.float32)
    for octant in range(4):
        for g in range(4):
            center[octant, 32 + 16 * (octant // 2) + i, 32 * g + i] = 1
            center[octant, 160 + 16 * (octant % 2) + i, 32 * g + 16 + i] = 1
    layers = np.zeros((4, 128, 1024), np.float32)
    line = np.arange(32)
    for octant in range(4):
        y_face, y_next = (0, 1) if octant % 2 else (31, 30)
        z_face, z_next = (0, 1) if octant // 2 else (31, 30)
        layers[octant, line, y_face * 32 + line] = 1
        layers[octant, 32 + line, y_next * 32 + line] = 1
        layers[octant, 64 + line, line * 32 + z_face] = 1
        layers[octant, 96 + line, line * 32 + z_next] = 1
    up_layer = np.zeros((128, 128), np.float32)
    for g in range(4):
        up_layer[32 * g + line // 2, line] = 1
        up_layer[32 * g + 16 + line // 2, 64 + line] = 1
    fill = np.zeros((2, 256, 512), np.float32)
    z_column = np.zeros((2, 128, 512), np.float32)
    y_row = np.zeros((4, 128, 128), np.float32)
    for g in range(4):
        for z_half in range(2):
            fill[z_half, place, a * 32 + 16 * z_half + b] = 1
            z_column[z_half, 32 * g + 16 + i, i * 32 + 16 - z_half] = 1
        for octant in range(4):
            y_row[octant, 32 * g + i, 96 * (octant % 2) + 16 * (octant // 2) + i] = 1
    return sel_x, sel_yz, up_x, twice, window_z, center, layers, up_layer, fill, z_column, y_row


SEL_X, SEL_YZ, UP_X, TWICE, WINDOW_Z, CENTER, LAYERS, UP_LAYER, FILL, Z_COLUMN, Y_ROW = selection_tables()


def table(values):
    return jnp.asarray(values.astype(jnp.bfloat16))


def halves(a):
    high = a.astype(BF16)
    return high, (a - high.astype(F32)).astype(BF16)


def dot(a, b):
    return jnp.dot(a, b, preferred_element_type=F32)


def pick(a, w):
    high, low = halves(a)
    return dot(high, w) + dot(low, w)


def left_pick(w, a):
    high, low = halves(a)
    return dot(w, high) + dot(w, low)


def iota(shape, dim):
    return lax.broadcasted_iota(jnp.int32, shape, dim)


def pack_rows(rows):
    group = iota((32, 128), 1) // 32
    out = rows[0:32]
    for g in range(1, 4):
        out = jnp.where(group == g, rows[32 * g : 32 * g + 32], out)
    return out


def unpack_rows(packed):
    group = iota((32, 128), 1) // 32
    return jnp.concatenate([jnp.where(group == g, packed, 0.0) for g in range(4)], axis=0)


def species_column(values_ref, factor, width):
    row = iota((8, width), 0)
    out = jnp.zeros((8, width), F32)
    for s in range(8):
        out = jnp.where(row == s, values_ref[s] * factor, out)
    return out


def set_rates(rates, reaction_ref, step):
    column = iota((1, 256), 1)
    for s in range(8):
        line = jnp.zeros((1, 256), F32)
        for t in range(8):
            line = jnp.where(column // 32 == t, reaction_ref[s, t] * step, line)
        high, low = halves(jnp.where(iota((32, 256), 0) == iota((32, 256), 1) % 32, line, 0.0))
        rates[0, 32 * s : 32 * s + 32] = high
        rates[1, 32 * s : 32 * s + 32] = low


def load_cells(cells, amounts):
    for t in range(8):
        cells[:, t + 1, 8:40, :] = amounts[:, :, 128 * t : 128 * t + 128]


def prepare(f, f_low, f_high, coef, scale):
    lane = iota((32, 1024), 1)
    row = iota((32, 1024), 0)
    depth = lane % 32
    scaling = scale / jnp.maximum(f, FLOOR)
    x_low = scaling * jnp.minimum(f, jnp.where(row == 0, f_low, pltpu.roll(f, 1, 0)))
    x_high = scaling * jnp.minimum(f, jnp.where(row == 31, f_high, pltpu.roll(f, 31, 0)))
    y_low = scaling * jnp.where(lane < 32, 0.0, jnp.minimum(f, pltpu.roll(f, 32, 1)))
    y_high = scaling * jnp.where(lane >= 992, 0.0, jnp.minimum(f, pltpu.roll(f, 992, 1)))
    z_low = scaling * jnp.where(depth == 0, 0.0, jnp.minimum(f, pltpu.roll(f, 1, 1)))
    z_high = scaling * jnp.where(depth == 31, 0.0, jnp.minimum(f, pltpu.roll(f, 1023, 1)))
    everything = x_low + x_high + y_low + y_high + z_low + z_high
    kinds = [x_low, x_high, y_low, y_high, z_low, z_high, everything, 1.0 - ADVECT * x_high, ADVECT * x_low]
    for k, kind in enumerate(kinds):
        for t in range(8):
            coef[k, t] = kind[:, 128 * t : 128 * t + 128]


def advance(cells, coef, reacted, rates, spread, store, layers=None, parts=None):
    lane = iota((8, 128), 1)

    def react(n, to):
        block = jnp.concatenate([cells[:, 2 * n + 1 + h, 8:40, :].reshape(256, 128) for h in range(2)], axis=1)
        high, low = halves(block)
        out = dot(rates[0], high) + dot(rates[1], high) + dot(rates[0], low)
        for h in range(2):
            to[:, h] = out[:, 128 * h : 128 * h + 128].reshape(8, 32, 128)
        if layers is not None:
            rows = layers[0, pl.ds(pl.multiple_of(256 * n, 256), 256), :]
            parts[n] = dot(high, rows) + dot(low, rows)

    def add(t, term):
        for xt in range(4):
            kinds = [coef[k, t, 8 * xt : 8 * xt + 8, :] for k in range(9)]
            x_low, x_high, y_low, y_high, z_low, z_high, everything, own, upwind = kinds
            at = 8 + 8 * xt
            for s in range(8):
                c = cells[s, t + 1, at : at + 8, :]
                below = cells[s, t + 1, at - 1 : at + 7, :]
                above = cells[s, t + 1, at + 1 : at + 9, :]
                left = pltpu.roll(jnp.where(lane >= 96, cells[s, t, at : at + 8, :], c), 32, 1)
                right = pltpu.roll(jnp.where(lane < 32, cells[s, t + 2, at : at + 8, :], c), 96, 1)
                change = x_low * below + x_high * above + y_low * left + y_high * right
                change = change + z_low * pltpu.roll(c, 1, 1) + z_high * pltpu.roll(c, 127, 1)
                change = change - everything * c
                result = own * c + upwind * below + spread[s] * change
                store(s, t, xt, result + term[s, 8 * xt : 8 * xt + 8, :])

    now, later = reacted
    react(0, now)

    def pair(m, carry):
        react(2 * m + 1, later)
        for h in range(2):
            add(4 * m + h, now.at[:, h])
        react(jnp.minimum(2 * m + 2, 3), now)
        for h in range(2):
            add(4 * m + 2 + h, later.at[:, h])
        return carry

    lax.fori_loop(0, 2, pair, 0)


def clear_rim(cells):
    cells[:, 0] = jnp.zeros((8, 48, 128), F32)
    cells[:, 9] = jnp.zeros((8, 48, 128), F32)
    cells[:, :, 0:8, :] = jnp.zeros((8, 10, 8, 128), F32)
    cells[:, :, 40:48, :] = jnp.zeros((8, 10, 8, 128), F32)


def message_kernel(
    octants, codes, spread_ref, reaction_smem, reaction_ref, boxes, words, sel_x_all, window_z_all, center_all, messages,
    halo_out, rates, box_ref, code_ref, sel_x_ref, window_z_ref, center_ref, message, halo, sems,
):
    def copies(i):
        octant = octants[i]
        pairs = (
            (boxes.at[i], box_ref.at[i]), (words.at[i], code_ref.at[i]), (window_z_all.at[octant // 2], window_z_ref.at[i]),
            (sel_x_all.at[octant], sel_x_ref.at[i]), (center_all.at[octant], center_ref.at[i]),
        )
        return [pltpu.make_async_copy(source, target, sems.at[i, n]) for n, (source, target) in enumerate(pairs)]

    def one_message(i, listed):
        y_half = octants[i] % 2
        box = box_ref.at[pl.ds(i, 1)]
        f = code_ref[i].astype(F32) / LEVELS
        lane = iota((32, 128), 1)
        place = lane % 32
        turn = 32 * (1 + y_half)
        spread = [spread_ref[s] for s in range(8)]

        def window_y(a, b):
            return jnp.where(iota(a.shape, 1) < turn, pltpu.roll(a, turn, 1), pltpu.roll(b, turn, 1))

        around_y = window_y(
            box[0, :, :, 384:512].reshape(256, 128), box[0, :, :, 512:640].reshape(256, 128)
        )
        around_z = pick(box[0].reshape(256, 1024), window_z_ref[i])
        f_windows = (window_y(f[:, 384:512], f[:, 512:640]), pick(f, window_z_ref[i]))
        both = jnp.concatenate([around_y, around_z], axis=1)
        high, low = halves(both)
        reacted = dot(rates[0], high) + dot(rates[1], high) + dot(rates[0], low)
        old_rows, new_rows = [[], []], [[], []]
        for w, (around, fw) in enumerate(zip((around_y, around_z), f_windows)):
            inner = fw[8:24]
            scaling = COARSE_STEP / jnp.maximum(inner, FLOOR)
            x_low = scaling * jnp.minimum(inner, pltpu.roll(fw, 1, 0)[8:24])
            x_high = scaling * jnp.minimum(inner, pltpu.roll(fw, 31, 0)[8:24])
            low_side = scaling * jnp.minimum(inner, pltpu.roll(inner, 32, 1))
            high_side = scaling * jnp.minimum(inner, pltpu.roll(inner, 96, 1))
            before = scaling * jnp.where(place[8:24] == 0, 0.0, jnp.minimum(inner, pltpu.roll(inner, 1, 1)))
            after = scaling * jnp.where(place[8:24] == 31, 0.0, jnp.minimum(inner, pltpu.roll(inner, 127, 1)))
            everything = x_low + x_high + low_side + high_side + before + after
            own = 1.0 - ADVECT * x_high
            upwind = ADVECT * x_low
            for s in range(8):
                rows = around[32 * s : 32 * s + 32]
                c = rows[8:24]
                below = pltpu.roll(rows, 1, 0)[8:24]
                above = pltpu.roll(rows, 31, 0)[8:24]
                change = x_low * below + x_high * above
                change = change + low_side * pltpu.roll(c, 32, 1) + high_side * pltpu.roll(c, 96, 1)
                change = change + before * pltpu.roll(c, 1, 1) + after * pltpu.roll(c, 127, 1) - everything * c
                term = reacted[32 * s + 8 : 32 * s + 24, 128 * w : 128 * w + 128]
                old_rows[w].append(c)
                new_rows[w].append(own * c + upwind * below + spread[s] * change + term)
        fractions = jnp.concatenate([fw[8:24] for fw in f_windows], axis=1)
        sides = [
            jnp.concatenate([jnp.concatenate(part[0], axis=0), jnp.concatenate(part[1], axis=0)], axis=1)
            for part in (old_rows, new_rows)
        ]
        side_parts = pick(jnp.concatenate(sides + [fractions], axis=0), center_ref[i])

        wide = species_column(spread_ref, 1.0, 1024)
        long = iota((1, 1024), 1)
        planes = [box[0, :, x, :] for x in (7, 24)]
        mixed = jnp.dot(
            reaction_ref[...], jnp.concatenate(planes, axis=1), precision=lax.Precision.HIGHEST,
            preferred_element_type=F32,
        )
        new_planes = []
        for n, x in enumerate((7, 24)):
            fx = f[x : x + 1]
            scaling = COARSE_STEP / jnp.maximum(fx, FLOOR)
            x_low = scaling * jnp.minimum(fx, f[x - 1 : x])
            x_high = scaling * jnp.minimum(fx, f[x + 1 : x + 2])
            shifts = ((32, long < 32), (992, long >= 992), (1, long % 32 == 0), (1023, long % 32 == 31))
            c = planes[n]
            below = box[0, :, x - 1, :]
            change = x_low * below + x_high * box[0, :, x + 1, :]
            everything = x_low + x_high
            for amount, wall in shifts:
                factor = scaling * jnp.where(wall, 0.0, jnp.minimum(fx, pltpu.roll(fx, amount, 1)))
                change = change + factor * pltpu.roll(c, amount, 1)
                everything = everything + factor
            change = change - everything * c
            moved = (1.0 - ADVECT * x_high) * c + ADVECT * x_low * below + wide * change
            new_planes.append(moved + COARSE_STEP * mixed[:, 1024 * n : 1024 * n + 1024])
        sublane = iota((8, 1024), 0)
        faces = jnp.where(sublane == 0, f[7:8], jnp.where(sublane == 1, f[24:25], 0.0))
        blank = jnp.zeros((8, 1024), F32)
        x_parts = pick(jnp.concatenate(planes + [faces] + new_planes + [blank], axis=0), sel_x_ref[i])

        sublane = iota((8, 128), 0)
        message[i, 0:16, :] = x_parts[0:16, 0:128]
        message[i, 16:32, :] = x_parts[0:16, 128:256]
        message[i, 32:64, :] = pack_rows(side_parts[0:128])
        face_f = jnp.where(sublane < 2, x_parts[16:24, 0:128], pltpu.roll(x_parts[16:24, 128:256], 2, 0))
        message[i, 64:72, :] = jnp.where(sublane < 4, face_f, jnp.where(sublane == 7, listed, 0.0))
        message[i, 72:80, :] = jnp.where(iota((8, 128), 1) < 64, side_parts[256:264], side_parts[264:272])
        message[i, 80:96, :] = x_parts[24:40, 0:128]
        message[i, 96:112, :] = x_parts[24:40, 128:256]
        message[i, 112:144, :] = pack_rows(side_parts[128:256])

        def put_plane(p, x):
            plane = box[0, :, x, :]
            for t in range(8):
                base = 144 + (p * 8 + t) * 16
                halo[base : base + 8, :] = plane[:, 128 * t : 128 * t + 128]
                halo[base + 8 : base + 16, :] = jnp.broadcast_to(f[x : x + 1, 128 * t : 128 * t + 128], (8, 128))

        @pl.when(i == 0)
        def _():
            put_plane(0, 0)

        @pl.when(i == SLOTS - 1)
        def _():
            put_plane(1, 31)

    @pl.when(lax.axis_index("lev") == 0)
    def _():
        for copy in copies(0):
            copy.start()
        set_rates(rates, reaction_smem, COARSE_STEP)
        where = iota((8, 128), 1)
        listed = jnp.zeros((8, 128), F32)
        for j in range(SLOTS):
            listed = jnp.where(where == j, codes[j].astype(F32), listed)
        halo[...] = jnp.zeros((576, 128), F32)
        halo[64:72, :] = listed

        def result(i):
            return pltpu.make_async_copy(message.at[i], messages.at[i], sems.at[i, 5])

        def each(i, carry):
            @pl.when(i + 1 < SLOTS)
            def _():
                for copy in copies(i + 1):
                    copy.start()

            for copy in copies(i):
                copy.wait()
            one_message(i, listed)
            result(i).start()
            return carry

        lax.fori_loop(0, SLOTS, each, 0)
        last = pltpu.make_async_copy(halo, halo_out, sems.at[0, 0])
        last.start()
        for i in range(SLOTS):
            result(i).wait()
        last.wait()


def early_kernel(
    base, again, octants, fine_octants, counts, spread_ref, reaction_smem, box, code, boxes, words,
    sel_x_all, sel_yz_all, layers, mean_x, couple, *refs,
):
    states, register, edges, ends, average, *refs = refs[5 * again :]
    cells, later, coef, now, then, rates, parts, before, code_before, after, code_after, sel_x, sel_yz, sems = refs
    i = pl.program_id(0)
    at = base + i
    coarse = lax.axis_index("lev") == 0
    used = coarse | (at < counts[0])

    def coarse_copies(first=0, last=6):
        octant = octants[at]
        previous, following = jnp.maximum(at - 1, 0), jnp.minimum(at + 1, SLOTS - 1)
        pairs = (
            (boxes.at[previous, :, pl.ds(24, 8)], before), (words.at[previous, pl.ds(24, 8)], code_before),
            (boxes.at[following, :, pl.ds(0, 8)], after), (words.at[following, pl.ds(0, 8)], code_after),
            (sel_x_all.at[octant], sel_x), (sel_yz_all.at[octant], sel_yz),
        )
        return [pltpu.make_async_copy(*pairs[n], sems.at[n]) for n in range(first, last)]

    @pl.when(coarse)
    def _():
        for copy in coarse_copies():
            copy.start()

    @pl.when(jnp.logical_not(used))
    def _():
        states[0] = box[0]

    @pl.when(used)
    def _():
        @pl.when(i == 0)
        def _():
            set_rates(rates, reaction_smem, jnp.where(coarse, COARSE_STEP, 0.5 * COARSE_STEP))
            clear_rim(cells)
            clear_rim(later)

        f = code[0].astype(F32) / LEVELS
        load_cells(cells, box[0])

        def store(s, t, xt, value):
            states[0, s, 8 * xt : 8 * xt + 8, pl.ds(pl.multiple_of(128 * t, 128), 128)] = value

        def store_later(s, t, xt, value):
            later[s, t + 1, 8 + 8 * xt : 16 + 8 * xt, :] = value

        @pl.when(coarse)
        def _():
            octant = octants[at]
            for copy in coarse_copies(0, 4):
                copy.wait()
            for t in range(8):
                cells[:, t + 1, 7, :] = before[:, 7, 128 * t : 128 * t + 128]
                cells[:, t + 1, 40, :] = after[:, 0, 128 * t : 128 * t + 128]
            f_before = jnp.where(at > 0, code_before[7:8, :].astype(F32) / LEVELS, 0.0)
            f_after = jnp.where(at < SLOTS - 1, code_after[0:1, :].astype(F32) / LEVELS, 0.0)
            prepare(f, f_before, f_after, coef, COARSE_STEP)
            spread = [spread_ref[s] for s in range(8)]
            advance(cells, coef, (now, then), rates, spread, store)
            y_half = octant % 2
            z_half = octant // 2
            wide = species_column(spread_ref, 1.0, 1024)
            c7, c8 = box[0, :, 7, :], box[0, :, 8, :]
            c23, c24 = box[0, :, 23, :], box[0, :, 24, :]
            low_flux = -jnp.minimum(f[7:8], f[8:9]) * (ADVECT * c7 - wide * (c8 - c7))
            high_flux = jnp.minimum(f[23:24], f[24:25]) * (ADVECT * c23 - wide * (c24 - c23))
            for copy in coarse_copies(4, 6):
                copy.wait()
            x_parts = pick(jnp.concatenate([low_flux, high_flux], axis=0), sel_x[...])

            lane = iota((1, 1024), 1)
            y_row = lane // 32 == 16 - y_half
            y_roll = jnp.where(y_half == 0, 32, 992)
            z_roll = jnp.where(z_half == 0, 1, 1023)
            middle = f[8:24]
            inner_f = jnp.where(y_row, pltpu.roll(middle, y_roll, 1), pltpu.roll(middle, z_roll, 1))
            weight = -jnp.minimum(middle, inner_f)
            fluxes = []
            for s in range(8):
                c = box[0, s, 8:24, :]
                inner = jnp.where(y_row, pltpu.roll(c, y_roll, 1), pltpu.roll(c, z_roll, 1))
                fluxes.append(spread[s] * weight * (c - inner))
            side_parts = pick(jnp.concatenate(fluxes, axis=0), sel_yz[...])
            register[0, 0:16, :] = x_parts[:, 0:128]
            register[0, 16:32, :] = x_parts[:, 128:256]
            register[0, 32:64, :] = pack_rows(side_parts)

        @pl.when(jnp.logical_not(coarse))
        def _():
            prepare(f, 0.0, 0.0, coef, COARSE_STEP)
            spread = [spread_ref[s] * 2.0 for s in range(8)]
            advance(cells, coef, (now, then), rates, spread, store_later, layers, parts)
            edges[0, 0:256] = parts[0] + parts[1] + parts[2] + parts[3]
            advance(later, coef, (now, then), rates, spread, store, layers, parts)
            edges[0, 256:512] = parts[0] + parts[1] + parts[2] + parts[3]
            edges[0, 512:544] = pick(f, layers[0])
            ends[0, 0:8] = box[0, :, 0, :]
            ends[0, 8:16] = box[0, :, 31, :]
            for t in range(8):
                ends[0, 16:24, 128 * t : 128 * t + 128] = later[:, t + 1, 8, :]
                ends[0, 24:32, 128 * t : 128 * t + 128] = later[:, t + 1, 39, :]
            average[0] = 0.5 * left_pick(couple[...], pick(states[0].reshape(256, 1024), mean_x[...]))


def interface_kernel(
    parents, octants, counts, spread_ref, reaction_smem, reaction_ref, words, edges_all, ends_all, average_all, up_x_all,
    up_layer_all, twice_all, mean_x_all, mean_layer_all, couple_all, layers_all, layers_t_all, mean_layers_all,
    own, near_a, near_b, other, other_a, other_b, started, states, payloads, rates, messages, taken, coarse,
    first, code, edges, ends, average, up_x, up_layer, twice, mean_x, mean_layer, couple, layers, layers_t, mean_layers,
    rim, payload, sems, fixed_sems,
):
    column = lax.axis_index("box")
    turn_step = 1 - 2 * ((column >> 1) & 1)
    fixed = [
        pltpu.make_async_copy(source, target, fixed_sems.at[n])
        for n, (source, target) in enumerate((
            (up_x_all, up_x), (up_layer_all, up_layer), (twice_all, twice), (mean_x_all, mean_x),
            (mean_layer_all, mean_layer), (couple_all, couple),
        ))
    ]

    def copies(n, last):
        octant = octants[n]
        pairs = (
            (words, code, n), (edges_all, edges, n), (ends_all, ends, n), (average_all, average, n),
            (layers_all, layers, octant), (layers_t_all, layers_t, octant), (mean_layers_all, mean_layers, octant),
            (started, first, n),
        )
        return [
            pltpu.make_async_copy(source.at[index], target.at[n], sems.at[n, k])
            for k, (source, target, index) in enumerate(pairs)
            if last is None or last == (k == 7)
        ]

    def message_copy(source, box, n):
        return pltpu.make_async_copy(source.at[box], messages.at[n], sems.at[n, 8])

    def result_copies(n):
        return [
            pltpu.make_async_copy(first.at[n], states.at[n], sems.at[n, 9]),
            pltpu.make_async_copy(payload.at[:, n], payloads.at[:, n], sems.at[n, 10]),
        ]

    def row_ends():
        odd = (column & 1) == 1
        wide = species_column(spread_ref, 1.0, 128)
        ends_at = ((0, 0), (SLOTS - 1, 24))
        loads = [pltpu.make_async_copy(own.at[pl.ds(1, 2)], rim.at[0], sems.at[0, 0])]
        for p, (box, x) in enumerate(ends_at):
            loads.append(pltpu.make_async_copy(words.at[box, pl.ds(x, 8)], code.at[p, pl.ds(0, 8)], sems.at[1, p]))
            loads.append(pltpu.make_async_copy(states.at[box, :, pl.ds(x, 8)], first.at[p, :, pl.ds(0, 8)], sems.at[2, p]))
        for p, step in enumerate((-1, 1)):
            inside = odd if p == 0 else jnp.logical_not(odd)
            for source, there in (
                (other, inside), (other_a, jnp.logical_not(inside) & (turn_step == step)),
                (other_b, jnp.logical_not(inside) & (turn_step != step)),
            ):

                @pl.when(there)
                def _():
                    pltpu.make_async_copy(source.at[pl.ds(1, 2)], rim.at[1 + p], sems.at[3, p]).start()

        for copy in loads:
            copy.start()
        for copy in loads:
            copy.wait()
        saves = []
        for p, (box, x) in enumerate(ends_at):
            pltpu.make_async_copy(other.at[pl.ds(1, 2)], rim.at[1 + p], sems.at[3, p]).wait()
            at = 7 * p
            f = code[p, at : at + 1, :].astype(F32) / LEVELS
            scaling = COARSE_STEP / jnp.maximum(f, FLOOR)
            for t in range(8):
                part = slice(128 * t, 128 * t + 128)
                here = (p * 8 + t) * 16
                there = ((1 - p) * 8 + t) * 16
                c = rim[0, here // 144, here % 144 : here % 144 + 8, :]
                g = rim[1 + p, there // 144, there % 144 : there % 144 + 8, :]
                g_f = rim[1 + p, there // 144, there % 144 + 8 : there % 144 + 9, :]
                m = jnp.minimum(f[:, part], g_f)
                if p == 0:
                    gain = m * (ADVECT * g - wide * (c - g))
                else:
                    gain = -m * (ADVECT * c - wide * (g - c))
                first[p, :, at, part] += scaling[:, part] * gain
            saves.append(
                pltpu.make_async_copy(first.at[p, :, pl.ds(0, 8)], states.at[box, :, pl.ds(x, 8)], sems.at[2, p])
            )
            saves[-1].start()
        for copy in saves:
            copy.wait()

    pl.when(lax.axis_index("lev") == 0)(row_ends)

    def fetch(n):
        for copy in copies(n, None):
            copy.start()
        home = parents[n] // SLOTS
        away = (home >> 1) - (column >> 1)
        same = ((home - column) & 1) == 0
        for source, is_same, step in (
            (near_a, True, turn_step), (own, True, 0), (near_b, True, -turn_step),
            (other_a, False, turn_step), (other, False, 0), (other_b, False, -turn_step),
        ):

            @pl.when((same == is_same) & (away == step))
            def _():
                message_copy(source, parents[n] % SLOTS, n).start()

    def one_slot(i, carry):
        @pl.when(i + 1 < counts[0])
        def _():
            fetch(i + 1)

        for copy in copies(i, False):
            copy.wait()
        message_copy(own, 0, i).wait()
        chosen = messages.at[i]
        octant = octants[i]
        y_half = octant % 2
        z_half = octant // 2
        spread = [spread_ref[s] * 2.0 for s in range(8)]
        wide = species_column(spread_ref, 2.0, 1024)
        f = code[i].astype(F32) / LEVELS

        x_old = jnp.concatenate([chosen[0:16], chosen[16:32]], axis=1)
        x_new = jnp.concatenate([chosen[80:96], chosen[96:112]], axis=1)
        face_f = jnp.concatenate([chosen[64:72], pltpu.roll(chosen[64:72], 6, 0)], axis=1)
        ghosts = pick(jnp.concatenate([x_old, 0.5 * (x_old + x_new), face_f], axis=0), up_x[...])
        side_old = chosen[32:64]
        side_mid = 0.5 * (side_old + chosen[112:144])

        def side_ghosts(side):
            high, low = halves(unpack_rows(side))
            high = dot(twice[...], high).astype(BF16)
            low = dot(twice[...], low).astype(BF16)
            return dot(high, up_layer[...]) + dot(low, up_layer[...])

        ghost_old = side_ghosts(side_old)
        ghost_mid = side_ghosts(side_mid)
        group = iota((8, 128), 1) // 32
        side_f = [jnp.where(group == g, chosen[72:80], 0.0) for g in (0, 2)]
        high, low = halves(jnp.concatenate(side_f, axis=0))
        high = dot(twice[0:32, 0:16], high).astype(BF16)
        low = dot(twice[0:32, 0:16], low).astype(BF16)
        f_ghost = dot(high, up_layer[...]) + dot(low, up_layer[...])

        lane = iota((32, 128), 1)
        row = iota((32, 128), 0)
        face = lane // 32 % 2 == 0
        place = lane % 32
        fl = edges[i, 512:544]
        scaling = COARSE_STEP / jnp.maximum(fl, FLOOR)
        at_face = jnp.where(face, scaling, 0.0)
        through = jnp.where(face, jnp.minimum(fl, f_ghost), 0.0)
        x_low = at_face * jnp.where(row == 0, 0.0, jnp.minimum(fl, pltpu.roll(fl, 1, 0)))
        x_high = at_face * jnp.where(row == 31, 0.0, jnp.minimum(fl, pltpu.roll(fl, 31, 0)))
        t_low = at_face * jnp.where(place == 0, 0.0, jnp.minimum(fl, pltpu.roll(fl, 1, 1)))
        t_high = at_face * jnp.where(place == 31, 0.0, jnp.minimum(fl, pltpu.roll(fl, 127, 1)))
        behind = at_face * jnp.minimum(fl, pltpu.roll(fl, 96, 1))
        ahead = jnp.where(face, 0.0, scaling * jnp.minimum(fl, pltpu.roll(fl, 32, 1)))
        everything = x_low + x_high + t_low + t_high + behind
        own_part = 1.0 - ADVECT * x_high
        upwind = ADVECT * x_low
        flux_one = []
        for s in range(8):
            part = slice(32 * s, 32 * s + 32)
            q = through * (ghost_old[part] - edges[i, part])
            flux_one.append(q)
            taken[s] = spread[s] * (scaling * q)

        long = iota((1, 1024), 1)
        f_low, f_high = ghosts[32:33], ghosts[33:34]
        m_low = jnp.minimum(f[0:1], f_low)
        m_high = jnp.minimum(f[31:32], f_high)
        scale_low = COARSE_STEP / jnp.maximum(f[0:1], FLOOR)
        scale_high = COARSE_STEP / jnp.maximum(f[31:32], FLOOR)

        def end_fluxes(low, high, c_low, c_high):
            low_flux = -m_low * (ADVECT * low - wide * (c_low - low))
            high_flux = m_high * (ADVECT * c_high - wide * (high - c_high))
            return low_flux, high_flux

        low_one, high_one = end_fluxes(ghosts[0:8], ghosts[8:16], ends[i, 0:8], ends[i, 8:16])
        end_low = -scale_low * low_one
        end_high = -scale_high * high_one

        crossed = pick(jnp.concatenate([taken[:, 0, :], taken[:, 31, :]], axis=0), layers[i])
        ends_there = pick(jnp.concatenate([end_low, end_high], axis=0), layers_t[i])
        corner_y = jnp.where(z_half == 1, 0, 31)
        corner_z = 64 + jnp.where(y_half == 1, 0, 31)
        turn = corner_y - corner_z + 128
        back = corner_z - corner_y
        flux_two = []
        for s in range(8):
            part = slice(32 * s, 32 * s + 32)
            v = taken[s]
            c = edges[i, 256 + 32 * s : 288 + 32 * s] + v
            c = c + jnp.where(lane == corner_y, pltpu.roll(v, turn, 1), 0.0)
            c = c + jnp.where(lane == corner_z, pltpu.roll(v, back, 1), 0.0)
            c = c + jnp.where(row == 0, ends_there[s : s + 1], jnp.where(row == 31, ends_there[8 + s : 9 + s], 0.0))
            flux_two.append(through * (ghost_mid[part] - c))
        low_two, high_two = end_fluxes(
            ghosts[16:24], ghosts[24:32], ends[i, 16:24] + end_low + crossed[0:8],
            ends[i, 24:32] + end_high + crossed[8:16],
        )

        high, low = halves(taken[...].reshape(256, 128))
        mixed = dot(rates[0], high) + dot(rates[1], high) + dot(rates[0], low)
        totals = []
        for s in range(8):
            v = taken[s]
            below = pltpu.roll(v, 1, 0)
            change = x_low * below + x_high * pltpu.roll(v, 31, 0)
            change = change + t_low * pltpu.roll(v, 1, 1) + t_high * pltpu.roll(v, 127, 1)
            change = change + ahead * pltpu.roll(v, 32, 1) - everything * v + scaling * flux_two[s]
            totals.append(own_part * v + upwind * below + spread[s] * change + mixed[32 * s : 32 * s + 32])
        total = jnp.concatenate(totals, axis=0)

        def tangential(c, fx, scale, inner):
            change = jnp.zeros_like(c)
            everything = inner
            for amount, wall in ((32, long < 32), (992, long >= 992), (1, long % 32 == 0), (1023, long % 32 == 31)):
                factor = scale * jnp.where(wall, 0.0, jnp.minimum(fx, pltpu.roll(fx, amount, 1)))
                change = change + factor * pltpu.roll(c, amount, 1)
                everything = everything + factor
            return change - everything * c

        end_mixed = 0.5 * COARSE_STEP * jnp.dot(
            reaction_ref[...], jnp.concatenate([end_low, end_high], axis=1), precision=lax.Precision.HIGHEST,
            preferred_element_type=F32,
        )
        inner_low = jnp.minimum(f[0:1], f[1:2])
        inner_high = jnp.minimum(f[30:31], f[31:32])
        row0 = (1.0 - ADVECT * (scale_low * inner_low)) * end_low - scale_low * low_two + end_mixed[:, 0:1024]
        row0 = row0 + wide * tangential(end_low, f[0:1], scale_low, scale_low * inner_low)
        row1 = (wide + ADVECT) * (COARSE_STEP / jnp.maximum(f[1:2], FLOOR) * inner_low) * end_low
        row30 = wide * (COARSE_STEP / jnp.maximum(f[30:31], FLOOR) * inner_high) * end_high
        row31 = end_high - scale_high * high_two + end_mixed[:, 1024:2048]
        row31 = row31 + wide * tangential(end_high, f[31:32], scale_high, scale_high * inner_high)

        @pl.when(i == 0)
        def _():
            for copy in fixed[3:]:
                copy.wait()

        x_parts = pick(
            jnp.concatenate([low_one + low_two, high_one + high_two, row0 + row1, row30 + row31], axis=0), mean_x[...]
        )
        coarse[...] = (average[i] + 0.5 * left_pick(couple[...], pick(total, mean_layers[i]))).reshape(8, 16, 256)
        coarse[:, 0, :] += 0.5 * x_parts[16:24]
        coarse[:, 15, :] += 0.5 * x_parts[24:32]
        for q in range(3):
            payload[q, i] = coarse[...].reshape(128, 256)[40 * q : 40 * q + 40]
        payload[3, i, 0:8] = coarse[...].reshape(128, 256)[120:128]
        payload[3, i, 8:24] = 0.5 * x_parts[0:16]
        fluxes = jnp.concatenate([flux_one[s] + flux_two[s] for s in range(8)], axis=0)
        sides = left_pick(couple[...], pick(fluxes, mean_layer[...])).reshape(8, 16, 128)
        sides = jnp.concatenate([(-0.5 * spread[s]) * sides[s] for s in range(8)], axis=0)
        sides = pack_rows(sides)
        payload[3, i, 24:40, 0:128] = sides[0:16]
        payload[3, i, 24:40, 128:256] = sides[16:32]

        copies(i, True)[0].wait()
        high, low = halves(total)
        for n in range(4):
            part = slice(256 * n, 256 * n + 256)
            added = dot(high, layers[i, :, part]) + dot(low, layers[i, :, part])
            first[i, :, :, part] += added.reshape(8, 32, 256)
        first[i, :, 0, :] += row0
        first[i, :, 1, :] += row1
        first[i, :, 30, :] += row30
        first[i, :, 31, :] += row31
        for copy in result_copies(i):
            copy.start()
        return carry

    @pl.when(counts[0] > 0)
    def _():
        fetch(0)
        for copy in fixed:
            copy.start()
        set_rates(rates, reaction_smem, 0.5 * COARSE_STEP)
        for copy in fixed[:3]:
            copy.wait()
        lax.fori_loop(0, counts[0], one_slot, 0)
        for n in range(SLOTS):

            @pl.when(n < counts[0])
            def _():
                for copy in result_copies(n):
                    copy.wait()


def decode(code):
    safe = jnp.maximum(code, 0)
    return safe // (OFFSETS * SLOTS) + 1, safe // SLOTS % OFFSETS - REACH, safe % SLOTS


def list_kernel(near_a, own, near_b, codes, sems):
    copies = [
        pltpu.make_async_copy(source.at[0, 64:72], codes.at[n], sems.at[n]) for n, source in enumerate((near_a, own, near_b))
    ]
    for copy in copies:
        copy.start()
    for copy in copies:
        copy.wait()


def route_kernel(codes, mine, others, to_a, stay, to_b):
    column = lax.axis_index("box")
    turn_step = 1 - 2 * ((column >> 1) & 1)
    for n, (step, target) in enumerate(((turn_step, to_a), (0, stay), (-turn_step, to_b))):
        for j in range(SLOTS):
            row, offset, slot = decode(codes[n, 7, j].astype(jnp.int32))
            child = column + 2 * step + offset
            target[j] = jnp.where(((child - column) & 1) == 0, mine[row, slot], others[row, slot])


def choose_kernel(codes, from_a, stay, from_b, chosen):
    column = lax.axis_index("box")
    turn_step = 1 - 2 * ((column >> 1) & 1)
    for j in range(SLOTS):
        _, offset, _ = decode(codes[j])
        away = ((column + offset) >> 1) - (column >> 1)
        chosen[0, j] = jnp.where(away == turn_step, from_a[j], jnp.where(away == 0, stay[j], from_b[j]))


def finish_kernel(
    octants, codes, message, register, parts, fill, z_column, y_row, updated, states, window, beside, sems
):
    def copies(i, out):
        y_half = octants[i] % 2
        pairs = (
            (pl.ds(pl.multiple_of(512 * y_half, 512), 512), window.at[i]),
            (pl.ds(pl.multiple_of(512 - 128 * y_half, 128), 128), beside.at[i]),
        )
        result = []
        for n, (lanes, here) in enumerate(pairs):
            there = states.at[i, :, :, lanes]
            source, target = (here, there) if out else (there, here)
            result.append(pltpu.make_async_copy(source, target, sems.at[i, n]))
        return result

    def one_box(i):
        octant = octants[i]
        z_half = octant // 2
        inside = iota((1, 512), 1) % 32 // 16 == z_half
        face_f = message[i, 64:72, :]
        low_f = jnp.concatenate([face_f[0:1], face_f[2:3]], axis=1)
        high_f = jnp.concatenate([face_f[1:2], face_f[3:4]], axis=1)
        x_f = jnp.where(iota((16, 256), 0) < 8, low_f, high_f)
        reg_x = jnp.concatenate([register[i, 0:16, :], register[i, 16:32, :]], axis=1)
        fix_x = COARSE_STEP / jnp.maximum(x_f, FLOOR) * (parts[3, i, 8:24, :] - reg_x)
        near_f = message[i, 72:80, :]
        far_f = pltpu.roll(near_f, 64, 1)
        left = iota((8, 128), 1) < 64
        side_f = jnp.concatenate([jnp.where(left, near_f, far_f), jnp.where(left, far_f, near_f)] * 2, axis=0)
        sides = jnp.concatenate([parts[3, i, 24:40, 0:128], parts[3, i, 24:40, 128:256]], axis=0)
        fix_sides = unpack_rows(COARSE_STEP / jnp.maximum(side_f, FLOOR) * (sides - register[i, 32:64, :]))
        average = jnp.concatenate([parts[q, i] for q in range(3)] + [parts[3, i, 0:8, :]], axis=0)
        planes = pick(fix_x, fill[z_half])
        filled = pick(average, fill[z_half])
        along = pick(fix_sides, z_column[z_half])
        across = pick(fix_sides, y_row[octant])
        for copy in copies(i, False):
            copy.wait()
        window[i, :, 7, :] += planes[0:8]
        window[i, :, 24, :] += planes[8:16]
        for s in range(8):
            part = slice(16 * s, 16 * s + 16)
            window[i, s, 8:24, :] = jnp.where(inside, filled[part], window[i, s, 8:24, :] + along[part])
            beside[i, s, 8:24, :] += across[part]
        for copy in copies(i, True):
            copy.start()

    def each(act):
        for i in range(SLOTS):

            @pl.when(codes[i] >= 0)
            def _():
                act(i)

    @pl.when(lax.axis_index("lev") == 0)
    def _():
        each(lambda i: [copy.start() for copy in copies(i, False)])
        each(one_box)
        each(lambda i: [copy.wait() for copy in copies(i, True)])


def per_device(
    box_states, cell_code, diffusivity, reaction, coarse_child, coarse_octant, fine_parent, fine_octant, fine_count
):
    row = lax.axis_index("lev")
    count = lax.axis_size("box")
    swap = [(i, i ^ 1) for i in range(count)]
    round_a = [(i, i ^ 2) for i in range(count)]
    round_b = [(i, ((i + 2) ^ 2) - 2) for i in range(2, count - 2)]
    vmem = pltpu.CompilerParams(vmem_limit_bytes=62 * 1024 * 1024)
    small = pltpu.CompilerParams(vmem_limit_bytes=8 * 1024 * 1024)

    def whole(a):
        zeros = (0,) * a.ndim
        return pl.BlockSpec(a.shape, lambda i, *_: zeros)

    def each(shape):
        tail = (0,) * len(shape)
        return pl.BlockSpec((1,) + shape, lambda i, *_: (i,) + tail)

    smem = pl.BlockSpec(memory_space=pltpu.SMEM)
    hbm = pl.BlockSpec(memory_space=pl.ANY)
    in_vmem = pl.BlockSpec(memory_space=pltpu.VMEM)
    previous = lambda i: jnp.maximum(i - 1, 0)
    following = lambda i: jnp.minimum(i + 1, SLOTS - 1)
    shape = jax.ShapeDtypeStruct
    sel_x, sel_yz = table(SEL_X), table(SEL_YZ)
    by_octant = lambda i, octants, *_: (octants[i], 0, 0)

    message, halo = pl.pallas_call(
        message_kernel,
        in_specs=[smem] * 4 + [in_vmem] + [hbm] * 5,
        out_specs=[hbm, hbm],
        scratch_shapes=[
            pltpu.VMEM((2, 256, 256), BF16),
            pltpu.VMEM((SLOTS, 8, 32, 1024), F32),
            pltpu.VMEM((SLOTS, 32, 1024), jnp.int32),
            pltpu.VMEM((SLOTS, 1024, 256), BF16),
            pltpu.VMEM((SLOTS, 1024, 128), BF16),
            pltpu.VMEM((SLOTS, 256, 128), BF16),
            pltpu.VMEM((SLOTS, 144, 128), F32),
            pltpu.VMEM((576, 128), F32),
            pltpu.SemaphoreType.DMA((SLOTS, 6)),
        ],
        out_shape=[shape((SLOTS, 144, 128), F32), shape((576, 128), F32)],
        compiler_params=vmem,
        name="shells",
    )(
        coarse_octant, coarse_child, diffusivity, reaction, reaction, box_states, cell_code, sel_x, table(WINDOW_Z),
        table(CENTER),
    )

    mean_x, couple = table(0.25 * UP_X.T), table(TWICE.T)
    layers, layers_t = table(LAYERS), table(LAYERS.transpose(0, 2, 1))

    def early(base, boxes, *carried):
        def at(dims):
            tail = (0,) * len(dims)
            return pl.BlockSpec((1,) + dims, lambda i, *_: (base + i,) + tail)

        def for_octant(dims):
            return pl.BlockSpec((1,) + dims, lambda i, octants, *_: (octants[base + i], 0, 0))

        blocks = [(8, 32, 1024), (64, 128), (544, 128), (32, 1024), (128, 256)]
        return pl.pallas_call(
            functools.partial(early_kernel, base, len(carried) > 0),
            grid_spec=pltpu.PrefetchScalarGridSpec(
                num_scalar_prefetch=3,
                grid=(boxes,),
                in_specs=[
                    smem,
                    smem,
                    at((8, 32, 1024)),
                    at((32, 1024)),
                    hbm,
                    hbm,
                    hbm,
                    hbm,
                    pl.BlockSpec((1, 1024, 128), lambda i, octants, fine, *_: (fine[base + i], 0, 0)),
                    whole(mean_x),
                    whole(couple),
                ]
                + [hbm] * len(carried),
                out_specs=[at(dims) for dims in blocks],
                scratch_shapes=[
                    pltpu.VMEM((8, 10, 48, 128), F32),
                    pltpu.VMEM((8, 10, 48, 128), F32),
                    pltpu.VMEM((9, 8, 32, 128), F32),
                    pltpu.VMEM((8, 2, 32, 128), F32),
                    pltpu.VMEM((8, 2, 32, 128), F32),
                    pltpu.VMEM((2, 256, 256), BF16),
                    pltpu.VMEM((4, 256, 128), F32),
                    pltpu.VMEM((8, 8, 1024), F32),
                    pltpu.VMEM((8, 1024), jnp.int32),
                    pltpu.VMEM((8, 8, 1024), F32),
                    pltpu.VMEM((8, 1024), jnp.int32),
                    pltpu.VMEM((1024, 256), BF16),
                    pltpu.VMEM((1024, 128), BF16),
                    pltpu.SemaphoreType.DMA((6,)),
                ],
            ),
            out_shape=[shape((SLOTS,) + dims, F32) for dims in blocks],
            input_output_aliases={14 + n: n for n in range(len(carried))},
            compiler_params=vmem,
            cost_estimate=pl.CostEstimate(flops=10**9, bytes_accessed=30 * 10**6, transcendentals=0),
            name=f"early_{base}",
        )(
            coarse_octant, fine_octant, fine_count, diffusivity, reaction, box_states, cell_code, box_states, cell_code,
            sel_x, sel_yz, layers_t, mean_x, couple, *carried,
        )

    updated, *carried = early(0, 3)
    spread_out = [lax.ppermute(message, "lev", [(0, r)]) for r in (1, 3, 2)]
    *spread_out, updated = lax.optimization_barrier((*spread_out, updated))
    own = jnp.where(row == 0, halo.reshape(SLOTS, 144, 128), spread_out[0] + spread_out[1] + spread_out[2])
    near_a = lax.ppermute(own, "box", round_a)
    near_b = lax.ppermute(own, "box", round_b)
    updated, register, *carried = early(3, 1, updated, *carried)
    near_a, near_b, updated = lax.optimization_barrier((near_a, near_b, updated))
    other = lax.ppermute(own, "box", swap)
    other_a = lax.ppermute(near_a, "box", swap)
    other_b = lax.ppermute(near_b, "box", swap)

    up_x, up_layer, twice, mean_layer = table(UP_X), table(UP_LAYER), table(TWICE), table(0.25 * UP_LAYER.T)
    mean_layers = table(LAYERS @ (0.25 * UP_X.T))
    constants = [up_x, up_layer, twice, mean_x, mean_layer, couple]
    states, payload = pl.pallas_call(
        interface_kernel,
        in_specs=[smem] * 5 + [in_vmem] + [hbm] * 20,
        out_specs=[hbm, hbm],
        scratch_shapes=[
            pltpu.VMEM((2, 256, 256), BF16),
            pltpu.VMEM((SLOTS, 144, 128), F32),
            pltpu.VMEM((8, 32, 128), F32),
            pltpu.VMEM((8, 16, 256), F32),
            pltpu.VMEM((SLOTS, 8, 32, 1024), F32),
            pltpu.VMEM((SLOTS, 32, 1024), jnp.int32),
            pltpu.VMEM((SLOTS, 544, 128), F32),
            pltpu.VMEM((SLOTS, 32, 1024), F32),
            pltpu.VMEM((SLOTS, 128, 256), F32),
        ]
        + [pltpu.VMEM(a.shape, BF16) for a in constants]
        + [
            pltpu.VMEM((SLOTS, 128, 1024), BF16),
            pltpu.VMEM((SLOTS, 1024, 128), BF16),
            pltpu.VMEM((SLOTS, 128, 256), BF16),
            pltpu.VMEM((3, 2, 144, 128), F32),
            pltpu.VMEM((4, SLOTS, 40, 256), F32),
            pltpu.SemaphoreType.DMA((SLOTS, 11)),
            pltpu.SemaphoreType.DMA((6,)),
        ],
        out_shape=[shape((SLOTS, 8, 32, 1024), F32), shape((4, SLOTS, 40, 256), F32)],
        input_output_aliases={25: 0},
        compiler_params=vmem,
        name="interfaces",
    )(
        fine_parent, fine_octant, fine_count, diffusivity, reaction, reaction, cell_code, *carried, *constants, layers,
        layers_t, mean_layers, own, near_a, near_b, other, other_a, other_b, updated,
    )

    mine = lax.all_to_all(payload, "lev", 0, 0)
    others = lax.ppermute(mine, "box", swap)
    mine, near_a, own, near_b = lax.optimization_barrier((mine, near_a, own, near_b))
    codes = pl.pallas_call(
        list_kernel,
        in_specs=[pl.BlockSpec(memory_space=pltpu.HBM)] * 3,
        out_specs=pl.BlockSpec(memory_space=pltpu.HBM),
        scratch_shapes=[pltpu.SemaphoreType.DMA((3,))],
        out_shape=shape((3, 8, 128), F32),
        compiler_params=small,
        name="lists",
    )(near_a, own, near_b)
    bundle = shape((SLOTS, 40, 256), F32)
    to_a, stay, to_b = pl.pallas_call(
        route_kernel,
        in_specs=[smem] + [in_vmem] * 2,
        out_specs=[in_vmem] * 3,
        out_shape=[bundle] * 3,
        compiler_params=small,
        name="route",
    )(codes, mine, others)
    from_a = lax.ppermute(to_a, "box", round_a)
    from_b = lax.ppermute(to_b, "box", round_b)
    quarter = pl.pallas_call(
        choose_kernel,
        in_specs=[smem] + [in_vmem] * 3,
        out_specs=in_vmem,
        out_shape=shape((4, SLOTS, 40, 256), F32),
        compiler_params=small,
        name="choose",
    )(coarse_child, from_a, stay, from_b)
    parts = lax.all_to_all(quarter, "lev", 0, 0)

    return pl.pallas_call(
        finish_kernel,
        in_specs=[smem] * 2 + [in_vmem] * 6 + [hbm],
        out_specs=hbm,
        scratch_shapes=[
            pltpu.VMEM((SLOTS, 8, 32, 512), F32),
            pltpu.VMEM((SLOTS, 8, 32, 128), F32),
            pltpu.SemaphoreType.DMA((SLOTS, 2)),
        ],
        out_shape=shape((SLOTS, 8, 32, 1024), F32),
        input_output_aliases={8: 0},
        compiler_params=pltpu.CompilerParams(vmem_limit_bytes=24 * 1024 * 1024),
        name="finish",
    )(coarse_octant, coarse_child, message, register, parts, table(FILL), table(Z_COLUMN), table(Y_ROW), states)


def solution(mesh):
    return jax.shard_map(
        per_device,
        mesh=mesh,
        in_specs=(
            P(("lev", "box"), None, None, None),
            P(("lev", "box"), None, None),
            P(),
            P(),
            P("box"),
            P("box"),
            P(("lev", "box")),
            P(("lev", "box")),
            P(("lev", "box")),
        ),
        out_specs=P(("lev", "box"), None, None, None),
        check_vma=False,
    )
```

```python
import functools

import jax
import jax.numpy as jnp
import numpy as np
from jax import lax
from jax.experimental import pallas as pl
from jax.experimental.pallas import tpu as pltpu
from jax.sharding import PartitionSpec as P

ADVECT = 0.4
COARSE_STEP = 0.5
FLOOR = 0.5
LEVELS = 15.0
SLOTS = 4
REACH = 2
OFFSETS = 2 * REACH + 1
F32 = jnp.float32
BF16 = jnp.bfloat16


def selection_tables():
    lane = np.arange(1024)
    y, z = lane // 32, lane % 32
    place = np.arange(256)
    a, b = place // 16, place % 16
    i = np.arange(16)
    sel_x = np.zeros((4, 1024, 256), np.float32)
    sel_yz = np.zeros((4, 1024, 128), np.float32)
    for octant in range(4):
        y_half, z_half = octant % 2, octant // 2
        sel_x[octant, (16 * y_half + a) * 32 + 16 * z_half + b, place] = 1
        for g in range(4):
            sel_yz[octant, (16 - y_half) * 32 + 16 * z_half + i, 32 * g + i] = 1
            sel_yz[octant, (16 * y_half + i) * 32 + 16 - z_half, 32 * g + 16 + i] = 1
    up_x = np.zeros((256, 1024), np.float32)
    up_x[(y // 2) * 16 + z // 2, lane] = 1
    twice = np.zeros((256, 128), np.float32)
    rows = np.arange(256)
    twice[rows, rows // 32 * 16 + rows % 32 // 2] = 1
    window_z = np.zeros((2, 1024, 128), np.float32)
    for z_half in range(2):
        for step in range(3):
            rows = np.arange(32)
            window_z[z_half, rows * 32 + 15 - z_half + step, step * 32 + rows] = 1
    center = np.zeros((4, 256, 128), np.float32)
    for octant in range(4):
        for g in range(4):
            center[octant, 32 + 16 * (octant // 2) + i, 32 * g + i] = 1
            center[octant, 160 + 16 * (octant % 2) + i, 32 * g + 16 + i] = 1
    layers = np.zeros((4, 128, 1024), np.float32)
    line = np.arange(32)
    for octant in range(4):
        y_face, y_next = (0, 1) if octant % 2 else (31, 30)
        z_face, z_next = (0, 1) if octant // 2 else (31, 30)
        layers[octant, line, y_face * 32 + line] = 1
        layers[octant, 32 + line, y_next * 32 + line] = 1
        layers[octant, 64 + line, line * 32 + z_face] = 1
        layers[octant, 96 + line, line * 32 + z_next] = 1
    up_layer = np.zeros((128, 128), np.float32)
    for g in range(4):
        up_layer[32 * g + line // 2, line] = 1
        up_layer[32 * g + 16 + line // 2, 64 + line] = 1
    fill = np.zeros((2, 256, 512), np.float32)
    z_column = np.zeros((2, 128, 512), np.float32)
    y_row = np.zeros((4, 128, 128), np.float32)
    for g in range(4):
        for z_half in range(2):
            fill[z_half, place, a * 32 + 16 * z_half + b] = 1
            z_column[z_half, 32 * g + 16 + i, i * 32 + 16 - z_half] = 1
        for octant in range(4):
            y_row[octant, 32 * g + i, 96 * (octant % 2) + 16 * (octant // 2) + i] = 1
    return sel_x, sel_yz, up_x, twice, window_z, center, layers, up_layer, fill, z_column, y_row


SEL_X, SEL_YZ, UP_X, TWICE, WINDOW_Z, CENTER, LAYERS, UP_LAYER, FILL, Z_COLUMN, Y_ROW = selection_tables()


def table(values):
    return jnp.asarray(values.astype(jnp.bfloat16))


def halves(a):
    high = a.astype(BF16)
    return high, (a - high.astype(F32)).astype(BF16)


def dot(a, b):
    return jnp.dot(a, b, preferred_element_type=F32)


def pick(a, w):
    high, low = halves(a)
    return dot(high, w) + dot(low, w)


def left_pick(w, a):
    high, low = halves(a)
    return dot(w, high) + dot(w, low)


def iota(shape, dim):
    return lax.broadcasted_iota(jnp.int32, shape, dim)


def pack_rows(rows):
    group = iota((32, 128), 1) // 32
    out = rows[0:32]
    for g in range(1, 4):
        out = jnp.where(group == g, rows[32 * g : 32 * g + 32], out)
    return out


def unpack_rows(packed):
    group = iota((32, 128), 1) // 32
    return jnp.concatenate([jnp.where(group == g, packed, 0.0) for g in range(4)], axis=0)


def species_column(values_ref, factor, width):
    row = iota((8, width), 0)
    out = jnp.zeros((8, width), F32)
    for s in range(8):
        out = jnp.where(row == s, values_ref[s] * factor, out)
    return out


def set_rates(rates, reaction_ref, step):
    column = iota((1, 256), 1)
    for s in range(8):
        line = jnp.zeros((1, 256), F32)
        for t in range(8):
            line = jnp.where(column // 32 == t, reaction_ref[s, t] * step, line)
        high, low = halves(jnp.where(iota((32, 256), 0) == iota((32, 256), 1) % 32, line, 0.0))
        rates[0, 32 * s : 32 * s + 32] = high
        rates[1, 32 * s : 32 * s + 32] = low


def load_cells(cells, amounts):
    for t in range(8):
        cells[:, t + 1, 8:40, :] = amounts[:, :, 128 * t : 128 * t + 128]


def prepare(f, f_low, f_high, coef, scale):
    lane = iota((32, 1024), 1)
    row = iota((32, 1024), 0)
    depth = lane % 32
    scaling = scale / jnp.maximum(f, FLOOR)
    x_low = scaling * jnp.minimum(f, jnp.where(row == 0, f_low, pltpu.roll(f, 1, 0)))
    x_high = scaling * jnp.minimum(f, jnp.where(row == 31, f_high, pltpu.roll(f, 31, 0)))
    y_low = scaling * jnp.where(lane < 32, 0.0, jnp.minimum(f, pltpu.roll(f, 32, 1)))
    y_high = scaling * jnp.where(lane >= 992, 0.0, jnp.minimum(f, pltpu.roll(f, 992, 1)))
    z_low = scaling * jnp.where(depth == 0, 0.0, jnp.minimum(f, pltpu.roll(f, 1, 1)))
    z_high = scaling * jnp.where(depth == 31, 0.0, jnp.minimum(f, pltpu.roll(f, 1023, 1)))
    everything = x_low + x_high + y_low + y_high + z_low + z_high
    kinds = [x_low, x_high, y_low, y_high, z_low, z_high, everything, 1.0 - ADVECT * x_high, ADVECT * x_low]
    for k, kind in enumerate(kinds):
        for t in range(8):
            coef[k, t] = kind[:, 128 * t : 128 * t + 128]


def advance(cells, coef, reacted, rates, spread, store, layers=None, parts=None):
    lane = iota((8, 128), 1)

    def react(n, to):
        block = jnp.concatenate([cells[:, 2 * n + 1 + h, 8:40, :].reshape(256, 128) for h in range(2)], axis=1)
        high, low = halves(block)
        out = dot(rates[0], high) + dot(rates[1], high) + dot(rates[0], low)
        for h in range(2):
            to[:, h] = out[:, 128 * h : 128 * h + 128].reshape(8, 32, 128)
        if layers is not None:
            rows = layers[0, pl.ds(pl.multiple_of(256 * n, 256), 256), :]
            parts[n] = dot(high, rows) + dot(low, rows)

    def add(t, term):
        for xt in range(4):
            kinds = [coef[k, t, 8 * xt : 8 * xt + 8, :] for k in range(9)]
            x_low, x_high, y_low, y_high, z_low, z_high, everything, own, upwind = kinds
            at = 8 + 8 * xt
            for s in range(8):
                c = cells[s, t + 1, at : at + 8, :]
                below = cells[s, t + 1, at - 1 : at + 7, :]
                above = cells[s, t + 1, at + 1 : at + 9, :]
                left = pltpu.roll(jnp.where(lane >= 96, cells[s, t, at : at + 8, :], c), 32, 1)
                right = pltpu.roll(jnp.where(lane < 32, cells[s, t + 2, at : at + 8, :], c), 96, 1)
                change = x_low * below + x_high * above + y_low * left + y_high * right
                change = change + z_low * pltpu.roll(c, 1, 1) + z_high * pltpu.roll(c, 127, 1)
                change = change - everything * c
                result = own * c + upwind * below + spread[s] * change
                store(s, t, xt, result + term[s, 8 * xt : 8 * xt + 8, :])

    now, later = reacted
    react(0, now)

    def pair(m, carry):
        react(2 * m + 1, later)
        for h in range(2):
            add(4 * m + h, now.at[:, h])
        react(jnp.minimum(2 * m + 2, 3), now)
        for h in range(2):
            add(4 * m + 2 + h, later.at[:, h])
        return carry

    lax.fori_loop(0, 2, pair, 0)


def clear_rim(cells):
    cells[:, 0] = jnp.zeros((8, 48, 128), F32)
    cells[:, 9] = jnp.zeros((8, 48, 128), F32)
    cells[:, :, 0:8, :] = jnp.zeros((8, 10, 8, 128), F32)
    cells[:, :, 40:48, :] = jnp.zeros((8, 10, 8, 128), F32)


def message_kernel(
    octants, codes, spread_ref, reaction_smem, reaction_ref, boxes, words, sel_x_all, window_z_all, center_all, messages,
    halo_out, rates, box_ref, code_ref, sel_x_ref, window_z_ref, center_ref, message, halo, sems,
):
    def copies(i):
        octant = octants[i]
        pairs = (
            (boxes.at[i], box_ref.at[i]), (words.at[i], code_ref.at[i]), (window_z_all.at[octant // 2], window_z_ref.at[i]),
            (sel_x_all.at[octant], sel_x_ref.at[i]), (center_all.at[octant], center_ref.at[i]),
        )
        return [pltpu.make_async_copy(source, target, sems.at[i, n]) for n, (source, target) in enumerate(pairs)]

    def one_message(i, listed):
        y_half = octants[i] % 2
        box = box_ref.at[pl.ds(i, 1)]
        f = code_ref[i].astype(F32) / LEVELS
        lane = iota((32, 128), 1)
        place = lane % 32
        turn = 32 * (1 + y_half)
        spread = [spread_ref[s] for s in range(8)]

        def window_y(a, b):
            return jnp.where(iota(a.shape, 1) < turn, pltpu.roll(a, turn, 1), pltpu.roll(b, turn, 1))

        around_y = window_y(
            box[0, :, :, 384:512].reshape(256, 128), box[0, :, :, 512:640].reshape(256, 128)
        )
        around_z = pick(box[0].reshape(256, 1024), window_z_ref[i])
        f_windows = (window_y(f[:, 384:512], f[:, 512:640]), pick(f, window_z_ref[i]))
        both = jnp.concatenate([around_y, around_z], axis=1)
        high, low = halves(both)
        reacted = dot(rates[0], high) + dot(rates[1], high) + dot(rates[0], low)
        old_rows, new_rows = [[], []], [[], []]
        for w, (around, fw) in enumerate(zip((around_y, around_z), f_windows)):
            inner = fw[8:24]
            scaling = COARSE_STEP / jnp.maximum(inner, FLOOR)
            x_low = scaling * jnp.minimum(inner, pltpu.roll(fw, 1, 0)[8:24])
            x_high = scaling * jnp.minimum(inner, pltpu.roll(fw, 31, 0)[8:24])
            low_side = scaling * jnp.minimum(inner, pltpu.roll(inner, 32, 1))
            high_side = scaling * jnp.minimum(inner, pltpu.roll(inner, 96, 1))
            before = scaling * jnp.where(place[8:24] == 0, 0.0, jnp.minimum(inner, pltpu.roll(inner, 1, 1)))
            after = scaling * jnp.where(place[8:24] == 31, 0.0, jnp.minimum(inner, pltpu.roll(inner, 127, 1)))
            everything = x_low + x_high + low_side + high_side + before + after
            own = 1.0 - ADVECT * x_high
            upwind = ADVECT * x_low
            for s in range(8):
                rows = around[32 * s : 32 * s + 32]
                c = rows[8:24]
                below = pltpu.roll(rows, 1, 0)[8:24]
                above = pltpu.roll(rows, 31, 0)[8:24]
                change = x_low * below + x_high * above
                change = change + low_side * pltpu.roll(c, 32, 1) + high_side * pltpu.roll(c, 96, 1)
                change = change + before * pltpu.roll(c, 1, 1) + after * pltpu.roll(c, 127, 1) - everything * c
                term = reacted[32 * s + 8 : 32 * s + 24, 128 * w : 128 * w + 128]
                old_rows[w].append(c)
                new_rows[w].append(own * c + upwind * below + spread[s] * change + term)
        fractions = jnp.concatenate([fw[8:24] for fw in f_windows], axis=1)
        sides = [
            jnp.concatenate([jnp.concatenate(part[0], axis=0), jnp.concatenate(part[1], axis=0)], axis=1)
            for part in (old_rows, new_rows)
        ]
        side_parts = pick(jnp.concatenate(sides + [fractions], axis=0), center_ref[i])

        wide = species_column(spread_ref, 1.0, 1024)
        long = iota((1, 1024), 1)
        planes = [box[0, :, x, :] for x in (7, 24)]
        mixed = jnp.dot(
            reaction_ref[...], jnp.concatenate(planes, axis=1), precision=lax.Precision.HIGHEST,
            preferred_element_type=F32,
        )
        new_planes = []
        for n, x in enumerate((7, 24)):
            fx = f[x : x + 1]
            scaling = COARSE_STEP / jnp.maximum(fx, FLOOR)
            x_low = scaling * jnp.minimum(fx, f[x - 1 : x])
            x_high = scaling * jnp.minimum(fx, f[x + 1 : x + 2])
            shifts = ((32, long < 32), (992, long >= 992), (1, long % 32 == 0), (1023, long % 32 == 31))
            c = planes[n]
            below = box[0, :, x - 1, :]
            change = x_low * below + x_high * box[0, :, x + 1, :]
            everything = x_low + x_high
            for amount, wall in shifts:
                factor = scaling * jnp.where(wall, 0.0, jnp.minimum(fx, pltpu.roll(fx, amount, 1)))
                change = change + factor * pltpu.roll(c, amount, 1)
                everything = everything + factor
            change = change - everything * c
            moved = (1.0 - ADVECT * x_high) * c + ADVECT * x_low * below + wide * change
            new_planes.append(moved + COARSE_STEP * mixed[:, 1024 * n : 1024 * n + 1024])
        sublane = iota((8, 1024), 0)
        faces = jnp.where(sublane == 0, f[7:8], jnp.where(sublane == 1, f[24:25], 0.0))
        blank = jnp.zeros((8, 1024), F32)
        x_parts = pick(jnp.concatenate(planes + [faces] + new_planes + [blank], axis=0), sel_x_ref[i])

        sublane = iota((8, 128), 0)
        message[i, 0:16, :] = x_parts[0:16, 0:128]
        message[i, 16:32, :] = x_parts[0:16, 128:256]
        message[i, 32:64, :] = pack_rows(side_parts[0:128])
        face_f = jnp.where(sublane < 2, x_parts[16:24, 0:128], pltpu.roll(x_parts[16:24, 128:256], 2, 0))
        message[i, 64:72, :] = jnp.where(sublane < 4, face_f, jnp.where(sublane == 7, listed, 0.0))
        message[i, 72:80, :] = jnp.where(iota((8, 128), 1) < 64, side_parts[256:264], side_parts[264:272])
        message[i, 80:96, :] = x_parts[24:40, 0:128]
        message[i, 96:112, :] = x_parts[24:40, 128:256]
        message[i, 112:144, :] = pack_rows(side_parts[128:256])

        def put_plane(p, x):
            plane = box[0, :, x, :]
            for t in range(8):
                base = 144 + (p * 8 + t) * 16
                halo[base : base + 8, :] = plane[:, 128 * t : 128 * t + 128]
                halo[base + 8 : base + 16, :] = jnp.broadcast_to(f[x : x + 1, 128 * t : 128 * t + 128], (8, 128))

        @pl.when(i == 0)
        def _():
            put_plane(0, 0)

        @pl.when(i == SLOTS - 1)
        def _():
            put_plane(1, 31)

    @pl.when(lax.axis_index("lev") == 0)
    def _():
        for copy in copies(0):
            copy.start()
        set_rates(rates, reaction_smem, COARSE_STEP)
        where = iota((8, 128), 1)
        listed = jnp.zeros((8, 128), F32)
        for j in range(SLOTS):
            listed = jnp.where(where == j, codes[j].astype(F32), listed)
        halo[...] = jnp.zeros((576, 128), F32)
        halo[64:72, :] = listed

        def result(i):
            return pltpu.make_async_copy(message.at[i], messages.at[i], sems.at[i, 5])

        def each(i, carry):
            @pl.when(i + 1 < SLOTS)
            def _():
                for copy in copies(i + 1):
                    copy.start()

            for copy in copies(i):
                copy.wait()
            one_message(i, listed)
            result(i).start()
            return carry

        lax.fori_loop(0, SLOTS, each, 0)
        last = pltpu.make_async_copy(halo, halo_out, sems.at[0, 0])
        last.start()
        for i in range(SLOTS):
            result(i).wait()
        last.wait()


def early_kernel(
    base, count, again, octants, fine_octants, counts, spread_ref, reaction_smem, box, code, boxes, words,
    sel_x_all, sel_yz_all, layers, mean_x, couple, *refs,
):
    states, register, edges, ends, average, *refs = refs[5 * again :]
    cells, later, coef, now, then, rates, parts, before, code_before, after, code_after, sel_x, sel_yz, sems = refs
    i = pl.program_id(0)
    at = base + i
    coarse = lax.axis_index("lev") == 0
    used = coarse | (at < counts[0])

    slot = i % 2

    def coarse_copies(at, to, first=0, last=6):
        octant = octants[at]
        previous, following = jnp.maximum(at - 1, 0), jnp.minimum(at + 1, SLOTS - 1)
        pairs = (
            (boxes.at[previous, :, pl.ds(24, 8)], before), (words.at[previous, pl.ds(24, 8)], code_before),
            (boxes.at[following, :, pl.ds(0, 8)], after), (words.at[following, pl.ds(0, 8)], code_after),
            (sel_x_all.at[octant], sel_x), (sel_yz_all.at[octant], sel_yz),
        )
        return [
            pltpu.make_async_copy(pairs[n][0], pairs[n][1].at[to], sems.at[to, n]) for n in range(first, last)
        ]

    @pl.when(coarse & (i == 0))
    def _():
        for copy in coarse_copies(at, slot):
            copy.start()

    @pl.when(coarse & (i + 1 < count))
    def _():
        for copy in coarse_copies(at + 1, 1 - slot):
            copy.start()

    @pl.when(jnp.logical_not(used))
    def _():
        states[0] = box[0]

    @pl.when(used)
    def _():
        @pl.when(i == 0)
        def _():
            set_rates(rates, reaction_smem, jnp.where(coarse, COARSE_STEP, 0.5 * COARSE_STEP))
            clear_rim(cells)
            clear_rim(later)

        f = code[0].astype(F32) / LEVELS
        load_cells(cells, box[0])

        def store(s, t, xt, value):
            states[0, s, 8 * xt : 8 * xt + 8, pl.ds(pl.multiple_of(128 * t, 128), 128)] = value

        def store_later(s, t, xt, value):
            later[s, t + 1, 8 + 8 * xt : 16 + 8 * xt, :] = value

        @pl.when(coarse)
        def _():
            octant = octants[at]
            for copy in coarse_copies(at, slot, 0, 4):
                copy.wait()
            for t in range(8):
                cells[:, t + 1, 7, :] = before[slot, :, 7, 128 * t : 128 * t + 128]
                cells[:, t + 1, 40, :] = after[slot, :, 0, 128 * t : 128 * t + 128]
            f_before = jnp.where(at > 0, code_before[slot, 7:8, :].astype(F32) / LEVELS, 0.0)
            f_after = jnp.where(at < SLOTS - 1, code_after[slot, 0:1, :].astype(F32) / LEVELS, 0.0)
            prepare(f, f_before, f_after, coef, COARSE_STEP)
            spread = [spread_ref[s] for s in range(8)]
            advance(cells, coef, (now, then), rates, spread, store)
            y_half = octant % 2
            z_half = octant // 2
            wide = species_column(spread_ref, 1.0, 1024)
            c7, c8 = box[0, :, 7, :], box[0, :, 8, :]
            c23, c24 = box[0, :, 23, :], box[0, :, 24, :]
            low_flux = -jnp.minimum(f[7:8], f[8:9]) * (ADVECT * c7 - wide * (c8 - c7))
            high_flux = jnp.minimum(f[23:24], f[24:25]) * (ADVECT * c23 - wide * (c24 - c23))
            for copy in coarse_copies(at, slot, 4, 6):
                copy.wait()
            x_parts = pick(jnp.concatenate([low_flux, high_flux], axis=0), sel_x[slot])

            lane = iota((1, 1024), 1)
            y_row = lane // 32 == 16 - y_half
            y_roll = jnp.where(y_half == 0, 32, 992)
            z_roll = jnp.where(z_half == 0, 1, 1023)
            middle = f[8:24]
            inner_f = jnp.where(y_row, pltpu.roll(middle, y_roll, 1), pltpu.roll(middle, z_roll, 1))
            weight = -jnp.minimum(middle, inner_f)
            fluxes = []
            for s in range(8):
                c = box[0, s, 8:24, :]
                inner = jnp.where(y_row, pltpu.roll(c, y_roll, 1), pltpu.roll(c, z_roll, 1))
                fluxes.append(spread[s] * weight * (c - inner))
            side_parts = pick(jnp.concatenate(fluxes, axis=0), sel_yz[slot])
            register[0, 0:16, :] = x_parts[:, 0:128]
            register[0, 16:32, :] = x_parts[:, 128:256]
            register[0, 32:64, :] = pack_rows(side_parts)

        @pl.when(jnp.logical_not(coarse))
        def _():
            prepare(f, 0.0, 0.0, coef, COARSE_STEP)
            spread = [spread_ref[s] * 2.0 for s in range(8)]
            advance(cells, coef, (now, then), rates, spread, store_later, layers, parts)
            edges[0, 0:256] = parts[0] + parts[1] + parts[2] + parts[3]
            advance(later, coef, (now, then), rates, spread, store, layers, parts)
            edges[0, 256:512] = parts[0] + parts[1] + parts[2] + parts[3]
            edges[0, 512:544] = pick(f, layers[0])
            ends[0, 0:8] = box[0, :, 0, :]
            ends[0, 8:16] = box[0, :, 31, :]
            for t in range(8):
                ends[0, 16:24, 128 * t : 128 * t + 128] = later[:, t + 1, 8, :]
                ends[0, 24:32, 128 * t : 128 * t + 128] = later[:, t + 1, 39, :]
            average[0] = 0.5 * left_pick(couple[...], pick(states[0].reshape(256, 1024), mean_x[...]))


def interface_kernel(
    parents, octants, counts, spread_ref, reaction_smem, reaction_ref, words, edges_all, ends_all, average_all, up_x_all,
    up_layer_all, twice_all, mean_x_all, mean_layer_all, couple_all, layers_all, layers_t_all, mean_layers_all,
    own, near_a, near_b, other, other_a, other_b, started, states, payloads, rates, messages, taken, coarse,
    first, code, edges, ends, average, up_x, up_layer, twice, mean_x, mean_layer, couple, layers, layers_t, mean_layers,
    rim, payload, sems, fixed_sems,
):
    column = lax.axis_index("box")
    turn_step = 1 - 2 * ((column >> 1) & 1)
    fixed = [
        pltpu.make_async_copy(source, target, fixed_sems.at[n])
        for n, (source, target) in enumerate((
            (up_x_all, up_x), (up_layer_all, up_layer), (twice_all, twice), (mean_x_all, mean_x),
            (mean_layer_all, mean_layer), (couple_all, couple),
        ))
    ]

    def copies(n, last):
        octant = octants[n]
        pairs = (
            (words, code, n), (edges_all, edges, n), (ends_all, ends, n), (average_all, average, n),
            (layers_all, layers, octant), (layers_t_all, layers_t, octant), (mean_layers_all, mean_layers, octant),
            (started, first, n),
        )
        return [
            pltpu.make_async_copy(source.at[index], target.at[n], sems.at[n, k])
            for k, (source, target, index) in enumerate(pairs)
            if last is None or last == (k == 7)
        ]

    def message_copy(source, box, n):
        return pltpu.make_async_copy(source.at[box], messages.at[n], sems.at[n, 8])

    def result_copies(n):
        return [
            pltpu.make_async_copy(first.at[n], states.at[n], sems.at[n, 9]),
            pltpu.make_async_copy(payload.at[:, n], payloads.at[:, n], sems.at[n, 10]),
        ]

    def row_ends():
        odd = (column & 1) == 1
        wide = species_column(spread_ref, 1.0, 128)
        ends_at = ((0, 0), (SLOTS - 1, 24))
        loads = [pltpu.make_async_copy(own.at[pl.ds(1, 2)], rim.at[0], sems.at[0, 0])]
        for p, (box, x) in enumerate(ends_at):
            loads.append(pltpu.make_async_copy(words.at[box, pl.ds(x, 8)], code.at[p, pl.ds(0, 8)], sems.at[1, p]))
            loads.append(pltpu.make_async_copy(states.at[box, :, pl.ds(x, 8)], first.at[p, :, pl.ds(0, 8)], sems.at[2, p]))
        for p, step in enumerate((-1, 1)):
            inside = odd if p == 0 else jnp.logical_not(odd)
            for source, there in (
                (other, inside), (other_a, jnp.logical_not(inside) & (turn_step == step)),
                (other_b, jnp.logical_not(inside) & (turn_step != step)),
            ):

                @pl.when(there)
                def _():
                    pltpu.make_async_copy(source.at[pl.ds(1, 2)], rim.at[1 + p], sems.at[3, p]).start()

        for copy in loads:
            copy.start()
        for copy in loads:
            copy.wait()
        saves = []
        for p, (box, x) in enumerate(ends_at):
            pltpu.make_async_copy(other.at[pl.ds(1, 2)], rim.at[1 + p], sems.at[3, p]).wait()
            at = 7 * p
            f = code[p, at : at + 1, :].astype(F32) / LEVELS
            scaling = COARSE_STEP / jnp.maximum(f, FLOOR)
            for t in range(8):
                part = slice(128 * t, 128 * t + 128)
                here = (p * 8 + t) * 16
                there = ((1 - p) * 8 + t) * 16
                c = rim[0, here // 144, here % 144 : here % 144 + 8, :]
                g = rim[1 + p, there // 144, there % 144 : there % 144 + 8, :]
                g_f = rim[1 + p, there // 144, there % 144 + 8 : there % 144 + 9, :]
                m = jnp.minimum(f[:, part], g_f)
                if p == 0:
                    gain = m * (ADVECT * g - wide * (c - g))
                else:
                    gain = -m * (ADVECT * c - wide * (g - c))
                first[p, :, at, part] += scaling[:, part] * gain
            saves.append(
                pltpu.make_async_copy(first.at[p, :, pl.ds(0, 8)], states.at[box, :, pl.ds(x, 8)], sems.at[2, p])
            )
            saves[-1].start()
        for copy in saves:
            copy.wait()

    pl.when(lax.axis_index("lev") == 0)(row_ends)

    def fetch(n):
        for copy in copies(n, None):
            copy.start()
        home = parents[n] // SLOTS
        away = (home >> 1) - (column >> 1)
        same = ((home - column) & 1) == 0
        for source, is_same, step in (
            (near_a, True, turn_step), (own, True, 0), (near_b, True, -turn_step),
            (other_a, False, turn_step), (other, False, 0), (other_b, False, -turn_step),
        ):

            @pl.when((same == is_same) & (away == step))
            def _():
                message_copy(source, parents[n] % SLOTS, n).start()

    def one_slot(i, carry):
        @pl.when(i + 1 < counts[0])
        def _():
            fetch(i + 1)

        for copy in copies(i, False):
            copy.wait()
        message_copy(own, 0, i).wait()
        chosen = messages.at[i]
        octant = octants[i]
        y_half = octant % 2
        z_half = octant // 2
        spread = [spread_ref[s] * 2.0 for s in range(8)]
        wide = species_column(spread_ref, 2.0, 1024)
        f = code[i].astype(F32) / LEVELS

        x_old = jnp.concatenate([chosen[0:16], chosen[16:32]], axis=1)
        x_new = jnp.concatenate([chosen[80:96], chosen[96:112]], axis=1)
        face_f = jnp.concatenate([chosen[64:72], pltpu.roll(chosen[64:72], 6, 0)], axis=1)
        ghosts = pick(jnp.concatenate([x_old, 0.5 * (x_old + x_new), face_f], axis=0), up_x[...])
        side_old = chosen[32:64]
        side_mid = 0.5 * (side_old + chosen[112:144])

        def side_ghosts(side):
            high, low = halves(unpack_rows(side))
            high = dot(twice[...], high).astype(BF16)
            low = dot(twice[...], low).astype(BF16)
            return dot(high, up_layer[...]) + dot(low, up_layer[...])

        ghost_old = side_ghosts(side_old)
        ghost_mid = side_ghosts(side_mid)
        group = iota((8, 128), 1) // 32
        side_f = [jnp.where(group == g, chosen[72:80], 0.0) for g in (0, 2)]
        high, low = halves(jnp.concatenate(side_f, axis=0))
        high = dot(twice[0:32, 0:16], high).astype(BF16)
        low = dot(twice[0:32, 0:16], low).astype(BF16)
        f_ghost = dot(high, up_layer[...]) + dot(low, up_layer[...])

        lane = iota((32, 128), 1)
        row = iota((32, 128), 0)
        face = lane // 32 % 2 == 0
        place = lane % 32
        fl = edges[i, 512:544]
        scaling = COARSE_STEP / jnp.maximum(fl, FLOOR)
        at_face = jnp.where(face, scaling, 0.0)
        through = jnp.where(face, jnp.minimum(fl, f_ghost), 0.0)
        x_low = at_face * jnp.where(row == 0, 0.0, jnp.minimum(fl, pltpu.roll(fl, 1, 0)))
        x_high = at_face * jnp.where(row == 31, 0.0, jnp.minimum(fl, pltpu.roll(fl, 31, 0)))
        t_low = at_face * jnp.where(place == 0, 0.0, jnp.minimum(fl, pltpu.roll(fl, 1, 1)))
        t_high = at_face * jnp.where(place == 31, 0.0, jnp.minimum(fl, pltpu.roll(fl, 127, 1)))
        behind = at_face * jnp.minimum(fl, pltpu.roll(fl, 96, 1))
        ahead = jnp.where(face, 0.0, scaling * jnp.minimum(fl, pltpu.roll(fl, 32, 1)))
        everything = x_low + x_high + t_low + t_high + behind
        own_part = 1.0 - ADVECT * x_high
        upwind = ADVECT * x_low
        flux_one = []
        for s in range(8):
            part = slice(32 * s, 32 * s + 32)
            q = through * (ghost_old[part] - edges[i, part])
            flux_one.append(q)
            taken[s] = spread[s] * (scaling * q)

        long = iota((1, 1024), 1)
        f_low, f_high = ghosts[32:33], ghosts[33:34]
        m_low = jnp.minimum(f[0:1], f_low)
        m_high = jnp.minimum(f[31:32], f_high)
        scale_low = COARSE_STEP / jnp.maximum(f[0:1], FLOOR)
        scale_high = COARSE_STEP / jnp.maximum(f[31:32], FLOOR)

        def end_fluxes(low, high, c_low, c_high):
            low_flux = -m_low * (ADVECT * low - wide * (c_low - low))
            high_flux = m_high * (ADVECT * c_high - wide * (high - c_high))
            return low_flux, high_flux

        low_one, high_one = end_fluxes(ghosts[0:8], ghosts[8:16], ends[i, 0:8], ends[i, 8:16])
        end_low = -scale_low * low_one
        end_high = -scale_high * high_one

        crossed = pick(jnp.concatenate([taken[:, 0, :], taken[:, 31, :]], axis=0), layers[i])
        ends_there = pick(jnp.concatenate([end_low, end_high], axis=0), layers_t[i])
        corner_y = jnp.where(z_half == 1, 0, 31)
        corner_z = 64 + jnp.where(y_half == 1, 0, 31)
        turn = corner_y - corner_z + 128
        back = corner_z - corner_y
        flux_two = []
        for s in range(8):
            part = slice(32 * s, 32 * s + 32)
            v = taken[s]
            c = edges[i, 256 + 32 * s : 288 + 32 * s] + v
            c = c + jnp.where(lane == corner_y, pltpu.roll(v, turn, 1), 0.0)
            c = c + jnp.where(lane == corner_z, pltpu.roll(v, back, 1), 0.0)
            c = c + jnp.where(row == 0, ends_there[s : s + 1], jnp.where(row == 31, ends_there[8 + s : 9 + s], 0.0))
            flux_two.append(through * (ghost_mid[part] - c))
        low_two, high_two = end_fluxes(
            ghosts[16:24], ghosts[24:32], ends[i, 16:24] + end_low + crossed[0:8],
            ends[i, 24:32] + end_high + crossed[8:16],
        )

        high, low = halves(taken[...].reshape(256, 128))
        mixed = dot(rates[0], high) + dot(rates[1], high) + dot(rates[0], low)
        totals = []
        for s in range(8):
            v = taken[s]
            below = pltpu.roll(v, 1, 0)
            change = x_low * below + x_high * pltpu.roll(v, 31, 0)
            change = change + t_low * pltpu.roll(v, 1, 1) + t_high * pltpu.roll(v, 127, 1)
            change = change + ahead * pltpu.roll(v, 32, 1) - everything * v + scaling * flux_two[s]
            totals.append(own_part * v + upwind * below + spread[s] * change + mixed[32 * s : 32 * s + 32])
        total = jnp.concatenate(totals, axis=0)

        def tangential(c, fx, scale, inner):
            change = jnp.zeros_like(c)
            everything = inner
            for amount, wall in ((32, long < 32), (992, long >= 992), (1, long % 32 == 0), (1023, long % 32 == 31)):
                factor = scale * jnp.where(wall, 0.0, jnp.minimum(fx, pltpu.roll(fx, amount, 1)))
                change = change + factor * pltpu.roll(c, amount, 1)
                everything = everything + factor
            return change - everything * c

        end_mixed = 0.5 * COARSE_STEP * jnp.dot(
            reaction_ref[...], jnp.concatenate([end_low, end_high], axis=1), precision=lax.Precision.HIGHEST,
            preferred_element_type=F32,
        )
        inner_low = jnp.minimum(f[0:1], f[1:2])
        inner_high = jnp.minimum(f[30:31], f[31:32])
        row0 = (1.0 - ADVECT * (scale_low * inner_low)) * end_low - scale_low * low_two + end_mixed[:, 0:1024]
        row0 = row0 + wide * tangential(end_low, f[0:1], scale_low, scale_low * inner_low)
        row1 = (wide + ADVECT) * (COARSE_STEP / jnp.maximum(f[1:2], FLOOR) * inner_low) * end_low
        row30 = wide * (COARSE_STEP / jnp.maximum(f[30:31], FLOOR) * inner_high) * end_high
        row31 = end_high - scale_high * high_two + end_mixed[:, 1024:2048]
        row31 = row31 + wide * tangential(end_high, f[31:32], scale_high, scale_high * inner_high)

        @pl.when(i == 0)
        def _():
            for copy in fixed[3:]:
                copy.wait()

        x_parts = pick(
            jnp.concatenate([low_one + low_two, high_one + high_two, row0 + row1, row30 + row31], axis=0), mean_x[...]
        )
        coarse[...] = (average[i] + 0.5 * left_pick(couple[...], pick(total, mean_layers[i]))).reshape(8, 16, 256)
        coarse[:, 0, :] += 0.5 * x_parts[16:24]
        coarse[:, 15, :] += 0.5 * x_parts[24:32]
        for q in range(3):
            payload[q, i] = coarse[...].reshape(128, 256)[40 * q : 40 * q + 40]
        payload[3, i, 0:8] = coarse[...].reshape(128, 256)[120:128]
        payload[3, i, 8:24] = 0.5 * x_parts[0:16]
        fluxes = jnp.concatenate([flux_one[s] + flux_two[s] for s in range(8)], axis=0)
        sides = left_pick(couple[...], pick(fluxes, mean_layer[...])).reshape(8, 16, 128)
        sides = jnp.concatenate([(-0.5 * spread[s]) * sides[s] for s in range(8)], axis=0)
        sides = pack_rows(sides)
        payload[3, i, 24:40, 0:128] = sides[0:16]
        payload[3, i, 24:40, 128:256] = sides[16:32]

        copies(i, True)[0].wait()
        high, low = halves(total)
        for n in range(4):
            part = slice(256 * n, 256 * n + 256)
            added = dot(high, layers[i, :, part]) + dot(low, layers[i, :, part])
            first[i, :, :, part] += added.reshape(8, 32, 256)
        first[i, :, 0, :] += row0
        first[i, :, 1, :] += row1
        first[i, :, 30, :] += row30
        first[i, :, 31, :] += row31
        for copy in result_copies(i):
            copy.start()
        return carry

    @pl.when(counts[0] > 0)
    def _():
        fetch(0)
        for copy in fixed:
            copy.start()
        set_rates(rates, reaction_smem, 0.5 * COARSE_STEP)
        for copy in fixed[:3]:
            copy.wait()
        lax.fori_loop(0, counts[0], one_slot, 0)
        for n in range(SLOTS):

            @pl.when(n < counts[0])
            def _():
                for copy in result_copies(n):
                    copy.wait()


def decode(code):
    safe = jnp.maximum(code, 0)
    return safe // (OFFSETS * SLOTS) + 1, safe // SLOTS % OFFSETS - REACH, safe % SLOTS


def list_kernel(near_a, own, near_b, codes, sems):
    copies = [
        pltpu.make_async_copy(source.at[0, 64:72], codes.at[n], sems.at[n]) for n, source in enumerate((near_a, own, near_b))
    ]
    for copy in copies:
        copy.start()
    for copy in copies:
        copy.wait()


def route_kernel(codes, mine, others, to_a, stay, to_b):
    column = lax.axis_index("box")
    turn_step = 1 - 2 * ((column >> 1) & 1)
    for n, (step, target) in enumerate(((turn_step, to_a), (0, stay), (-turn_step, to_b))):
        for j in range(SLOTS):
            row, offset, slot = decode(codes[n, 7, j].astype(jnp.int32))
            child = column + 2 * step + offset
            target[j] = jnp.where(((child - column) & 1) == 0, mine[row, slot], others[row, slot])


def choose_kernel(codes, from_a, stay, from_b, chosen):
    column = lax.axis_index("box")
    turn_step = 1 - 2 * ((column >> 1) & 1)
    for j in range(SLOTS):
        _, offset, _ = decode(codes[j])
        away = ((column + offset) >> 1) - (column >> 1)
        chosen[0, j] = jnp.where(away == turn_step, from_a[j], jnp.where(away == 0, stay[j], from_b[j]))


def finish_kernel(
    octants, codes, message, register, parts, fill, z_column, y_row, updated, states, window, beside, sems
):
    def copies(i, out):
        y_half = octants[i] % 2
        pairs = (
            (pl.ds(pl.multiple_of(512 * y_half, 512), 512), window.at[i]),
            (pl.ds(pl.multiple_of(512 - 128 * y_half, 128), 128), beside.at[i]),
        )
        result = []
        for n, (lanes, here) in enumerate(pairs):
            there = states.at[i, :, :, lanes]
            source, target = (here, there) if out else (there, here)
            result.append(pltpu.make_async_copy(source, target, sems.at[i, n]))
        return result

    def one_box(i):
        octant = octants[i]
        z_half = octant // 2
        inside = iota((1, 512), 1) % 32 // 16 == z_half
        face_f = message[i, 64:72, :]
        low_f = jnp.concatenate([face_f[0:1], face_f[2:3]], axis=1)
        high_f = jnp.concatenate([face_f[1:2], face_f[3:4]], axis=1)
        x_f = jnp.where(iota((16, 256), 0) < 8, low_f, high_f)
        reg_x = jnp.concatenate([register[i, 0:16, :], register[i, 16:32, :]], axis=1)
        fix_x = COARSE_STEP / jnp.maximum(x_f, FLOOR) * (parts[3, i, 8:24, :] - reg_x)
        near_f = message[i, 72:80, :]
        far_f = pltpu.roll(near_f, 64, 1)
        left = iota((8, 128), 1) < 64
        side_f = jnp.concatenate([jnp.where(left, near_f, far_f), jnp.where(left, far_f, near_f)] * 2, axis=0)
        sides = jnp.concatenate([parts[3, i, 24:40, 0:128], parts[3, i, 24:40, 128:256]], axis=0)
        fix_sides = unpack_rows(COARSE_STEP / jnp.maximum(side_f, FLOOR) * (sides - register[i, 32:64, :]))
        average = jnp.concatenate([parts[q, i] for q in range(3)] + [parts[3, i, 0:8, :]], axis=0)
        planes = pick(fix_x, fill[z_half])
        filled = pick(average, fill[z_half])
        along = pick(fix_sides, z_column[z_half])
        across = pick(fix_sides, y_row[octant])
        for copy in copies(i, False):
            copy.wait()
        window[i, :, 7, :] += planes[0:8]
        window[i, :, 24, :] += planes[8:16]
        for s in range(8):
            part = slice(16 * s, 16 * s + 16)
            window[i, s, 8:24, :] = jnp.where(inside, filled[part], window[i, s, 8:24, :] + along[part])
            beside[i, s, 8:24, :] += across[part]
        for copy in copies(i, True):
            copy.start()

    def each(act):
        for i in range(SLOTS):

            @pl.when(codes[i] >= 0)
            def _():
                act(i)

    @pl.when(lax.axis_index("lev") == 0)
    def _():
        each(lambda i: [copy.start() for copy in copies(i, False)])
        each(one_box)
        each(lambda i: [copy.wait() for copy in copies(i, True)])


def per_device(
    box_states, cell_code, diffusivity, reaction, coarse_child, coarse_octant, fine_parent, fine_octant, fine_count
):
    row = lax.axis_index("lev")
    count = lax.axis_size("box")
    swap = [(i, i ^ 1) for i in range(count)]
    round_a = [(i, i ^ 2) for i in range(count)]
    round_b = [(i, ((i + 2) ^ 2) - 2) for i in range(2, count - 2)]
    vmem = pltpu.CompilerParams(vmem_limit_bytes=62 * 1024 * 1024)
    small = pltpu.CompilerParams(vmem_limit_bytes=8 * 1024 * 1024)

    def whole(a):
        zeros = (0,) * a.ndim
        return pl.BlockSpec(a.shape, lambda i, *_: zeros)

    def each(shape):
        tail = (0,) * len(shape)
        return pl.BlockSpec((1,) + shape, lambda i, *_: (i,) + tail)

    smem = pl.BlockSpec(memory_space=pltpu.SMEM)
    hbm = pl.BlockSpec(memory_space=pl.ANY)
    in_vmem = pl.BlockSpec(memory_space=pltpu.VMEM)
    previous = lambda i: jnp.maximum(i - 1, 0)
    following = lambda i: jnp.minimum(i + 1, SLOTS - 1)
    shape = jax.ShapeDtypeStruct
    sel_x, sel_yz = table(SEL_X), table(SEL_YZ)
    by_octant = lambda i, octants, *_: (octants[i], 0, 0)

    message, halo = pl.pallas_call(
        message_kernel,
        in_specs=[smem] * 4 + [in_vmem] + [hbm] * 5,
        out_specs=[hbm, hbm],
        scratch_shapes=[
            pltpu.VMEM((2, 256, 256), BF16),
            pltpu.VMEM((SLOTS, 8, 32, 1024), F32),
            pltpu.VMEM((SLOTS, 32, 1024), jnp.int32),
            pltpu.VMEM((SLOTS, 1024, 256), BF16),
            pltpu.VMEM((SLOTS, 1024, 128), BF16),
            pltpu.VMEM((SLOTS, 256, 128), BF16),
            pltpu.VMEM((SLOTS, 144, 128), F32),
            pltpu.VMEM((576, 128), F32),
            pltpu.SemaphoreType.DMA((SLOTS, 6)),
        ],
        out_shape=[shape((SLOTS, 144, 128), F32), shape((576, 128), F32)],
        compiler_params=vmem,
        name="shells",
    )(
        coarse_octant, coarse_child, diffusivity, reaction, reaction, box_states, cell_code, sel_x, table(WINDOW_Z),
        table(CENTER),
    )

    mean_x, couple = table(0.25 * UP_X.T), table(TWICE.T)
    layers, layers_t = table(LAYERS), table(LAYERS.transpose(0, 2, 1))

    def early(base, boxes, *carried):
        def at(dims):
            tail = (0,) * len(dims)
            return pl.BlockSpec((1,) + dims, lambda i, *_: (base + i,) + tail)

        def for_octant(dims):
            return pl.BlockSpec((1,) + dims, lambda i, octants, *_: (octants[base + i], 0, 0))

        blocks = [(8, 32, 1024), (64, 128), (544, 128), (32, 1024), (128, 256)]
        return pl.pallas_call(
            functools.partial(early_kernel, base, boxes, len(carried) > 0),
            grid_spec=pltpu.PrefetchScalarGridSpec(
                num_scalar_prefetch=3,
                grid=(boxes,),
                in_specs=[
                    smem,
                    smem,
                    at((8, 32, 1024)),
                    at((32, 1024)),
                    hbm,
                    hbm,
                    hbm,
                    hbm,
                    pl.BlockSpec((1, 1024, 128), lambda i, octants, fine, *_: (fine[base + i], 0, 0)),
                    whole(mean_x),
                    whole(couple),
                ]
                + [hbm] * len(carried),
                out_specs=[at(dims) for dims in blocks],
                scratch_shapes=[
                    pltpu.VMEM((8, 10, 48, 128), F32),
                    pltpu.VMEM((8, 10, 48, 128), F32),
                    pltpu.VMEM((9, 8, 32, 128), F32),
                    pltpu.VMEM((8, 2, 32, 128), F32),
                    pltpu.VMEM((8, 2, 32, 128), F32),
                    pltpu.VMEM((2, 256, 256), BF16),
                    pltpu.VMEM((4, 256, 128), F32),
                    pltpu.VMEM((2, 8, 8, 1024), F32),
                    pltpu.VMEM((2, 8, 1024), jnp.int32),
                    pltpu.VMEM((2, 8, 8, 1024), F32),
                    pltpu.VMEM((2, 8, 1024), jnp.int32),
                    pltpu.VMEM((2, 1024, 256), BF16),
                    pltpu.VMEM((2, 1024, 128), BF16),
                    pltpu.SemaphoreType.DMA((2, 6)),
                ],
            ),
            out_shape=[shape((SLOTS,) + dims, F32) for dims in blocks],
            input_output_aliases={14 + n: n for n in range(len(carried))},
            compiler_params=vmem,
            cost_estimate=pl.CostEstimate(flops=10**9, bytes_accessed=30 * 10**6, transcendentals=0),
            name=f"early_{base}",
        )(
            coarse_octant, fine_octant, fine_count, diffusivity, reaction, box_states, cell_code, box_states, cell_code,
            sel_x, sel_yz, layers_t, mean_x, couple, *carried,
        )

    updated, *carried = early(0, 3)
    spread_out = [lax.ppermute(message, "lev", [(0, r)]) for r in (1, 3, 2)]
    *spread_out, updated = lax.optimization_barrier((*spread_out, updated))
    own = jnp.where(row == 0, halo.reshape(SLOTS, 144, 128), spread_out[0] + spread_out[1] + spread_out[2])
    near_a = lax.ppermute(own, "box", round_a)
    near_b = lax.ppermute(own, "box", round_b)
    updated, register, *carried = early(3, 1, updated, *carried)
    near_a, near_b, updated = lax.optimization_barrier((near_a, near_b, updated))
    other = lax.ppermute(own, "box", swap)
    other_a = lax.ppermute(near_a, "box", swap)
    other_b = lax.ppermute(near_b, "box", swap)

    up_x, up_layer, twice, mean_layer = table(UP_X), table(UP_LAYER), table(TWICE), table(0.25 * UP_LAYER.T)
    mean_layers = table(LAYERS @ (0.25 * UP_X.T))
    constants = [up_x, up_layer, twice, mean_x, mean_layer, couple]
    states, payload = pl.pallas_call(
        interface_kernel,
        in_specs=[smem] * 5 + [in_vmem] + [hbm] * 20,
        out_specs=[hbm, hbm],
        scratch_shapes=[
            pltpu.VMEM((2, 256, 256), BF16),
            pltpu.VMEM((SLOTS, 144, 128), F32),
            pltpu.VMEM((8, 32, 128), F32),
            pltpu.VMEM((8, 16, 256), F32),
            pltpu.VMEM((SLOTS, 8, 32, 1024), F32),
            pltpu.VMEM((SLOTS, 32, 1024), jnp.int32),
            pltpu.VMEM((SLOTS, 544, 128), F32),
            pltpu.VMEM((SLOTS, 32, 1024), F32),
            pltpu.VMEM((SLOTS, 128, 256), F32),
        ]
        + [pltpu.VMEM(a.shape, BF16) for a in constants]
        + [
            pltpu.VMEM((SLOTS, 128, 1024), BF16),
            pltpu.VMEM((SLOTS, 1024, 128), BF16),
            pltpu.VMEM((SLOTS, 128, 256), BF16),
            pltpu.VMEM((3, 2, 144, 128), F32),
            pltpu.VMEM((4, SLOTS, 40, 256), F32),
            pltpu.SemaphoreType.DMA((SLOTS, 11)),
            pltpu.SemaphoreType.DMA((6,)),
        ],
        out_shape=[shape((SLOTS, 8, 32, 1024), F32), shape((4, SLOTS, 40, 256), F32)],
        input_output_aliases={25: 0},
        compiler_params=vmem,
        name="interfaces",
    )(
        fine_parent, fine_octant, fine_count, diffusivity, reaction, reaction, cell_code, *carried, *constants, layers,
        layers_t, mean_layers, own, near_a, near_b, other, other_a, other_b, updated,
    )

    mine = lax.all_to_all(payload, "lev", 0, 0)
    others = lax.ppermute(mine, "box", swap)
    mine, near_a, own, near_b = lax.optimization_barrier((mine, near_a, own, near_b))
    codes = pl.pallas_call(
        list_kernel,
        in_specs=[pl.BlockSpec(memory_space=pltpu.HBM)] * 3,
        out_specs=pl.BlockSpec(memory_space=pltpu.HBM),
        scratch_shapes=[pltpu.SemaphoreType.DMA((3,))],
        out_shape=shape((3, 8, 128), F32),
        compiler_params=small,
        name="lists",
    )(near_a, own, near_b)
    bundle = shape((SLOTS, 40, 256), F32)
    to_a, stay, to_b = pl.pallas_call(
        route_kernel,
        in_specs=[smem] + [in_vmem] * 2,
        out_specs=[in_vmem] * 3,
        out_shape=[bundle] * 3,
        compiler_params=small,
        name="route",
    )(codes, mine, others)
    from_a = lax.ppermute(to_a, "box", round_a)
    from_b = lax.ppermute(to_b, "box", round_b)
    quarter = pl.pallas_call(
        choose_kernel,
        in_specs=[smem] + [in_vmem] * 3,
        out_specs=in_vmem,
        out_shape=shape((4, SLOTS, 40, 256), F32),
        compiler_params=small,
        name="choose",
    )(coarse_child, from_a, stay, from_b)
    parts = lax.all_to_all(quarter, "lev", 0, 0)

    return pl.pallas_call(
        finish_kernel,
        in_specs=[smem] * 2 + [in_vmem] * 6 + [hbm],
        out_specs=hbm,
        scratch_shapes=[
            pltpu.VMEM((SLOTS, 8, 32, 512), F32),
            pltpu.VMEM((SLOTS, 8, 32, 128), F32),
            pltpu.SemaphoreType.DMA((SLOTS, 2)),
        ],
        out_shape=shape((SLOTS, 8, 32, 1024), F32),
        input_output_aliases={8: 0},
        compiler_params=pltpu.CompilerParams(vmem_limit_bytes=24 * 1024 * 1024),
        name="finish",
    )(coarse_octant, coarse_child, message, register, parts, table(FILL), table(Z_COLUMN), table(Y_ROW), states)


def solution(mesh):
    return jax.shard_map(
        per_device,
        mesh=mesh,
        in_specs=(
            P(("lev", "box"), None, None, None),
            P(("lev", "box"), None, None),
            P(),
            P(),
            P("box"),
            P("box"),
            P(("lev", "box")),
            P(("lev", "box")),
            P(("lev", "box")),
        ),
        out_specs=P(("lev", "box"), None, None, None),
        check_vma=False,
    )
```
